32 devices in a mesh: ctx: 4 (over y, x), fsdp: 8 (over z, core).
Axes of the slice: x: 2, y: 2, z: 4, core: 2. Of those that a mesh axis runs over, the one named last changes fastest.
Arguments:
- tokens: bfloat16 [8, 1024, 2048], P('fsdp', 'ctx'), may hold values from -6 to 6
- segments: int32 [8, 1024], P('fsdp', 'ctx'), may hold values from 0 to 510, as said below
- positions: int32 [8, 1024], P('fsdp', 'ctx'), may hold values from 0 to 1023, as said below
- ln1_gain: bfloat16 [2048], P('fsdp'), may hold values from 0.5 to 1.5
- ln1_bias: bfloat16 [2048], P('fsdp'), may hold values from -2 to 2
- ln2_gain: bfloat16 [2048], P('fsdp'), may hold values from 0.5 to 1.5
- ln2_bias: bfloat16 [2048], P('fsdp'), may hold values from -2 to 2
- qkv_weight: bfloat16 [2048, 6144], P('fsdp'), may hold values from -0.125 to 0.125
- qkv_bias: bfloat16 [6144], P('fsdp'), may hold values from -2 to 2
- dense_weight: bfloat16 [2048, 2048], P('fsdp'), may hold values from -0.5 to 0.5
- dense_bias: bfloat16 [2048], P('fsdp'), may hold values from -2 to 2
- fc_in_weight: bfloat16 [2048, 8192], P('fsdp'), may hold values from -0.125 to 0.125
- fc_in_bias: bfloat16 [8192], P('fsdp'), may hold values from -2 to 2
- fc_out_weight: bfloat16 [8192, 2048], P('fsdp'), may hold values from -0.0625 to 0.0625
- fc_out_bias: bfloat16 [2048], P('fsdp'), may hold values from -2 to 2
- cotangent: bfloat16 [8, 1024, 2048], P('fsdp', 'ctx'), may hold values from -6 to 6
Outputs:
- output: bfloat16 [8, 1024, 2048], P('fsdp', 'ctx')
- input_grad: float32 [8, 1024, 2048], P('fsdp', 'ctx')
- ln1_gain_grad: float32 [2048], P('fsdp')
- ln1_bias_grad: float32 [2048], P('fsdp')
- ln2_gain_grad: float32 [2048], P('fsdp')
- ln2_bias_grad: float32 [2048], P('fsdp')
- qkv_weight_grad: float32 [2048, 6144], P('fsdp')
- qkv_bias_grad: float32 [6144], P('fsdp')
- dense_weight_grad: float32 [2048, 2048], P('fsdp')
- dense_bias_grad: float32 [2048], P('fsdp')
- fc_in_weight_grad: float32 [2048, 8192], P('fsdp')
- fc_in_bias_grad: float32 [8192], P('fsdp')
- fc_out_weight_grad: float32 [8192, 2048], P('fsdp')
- fc_out_bias_grad: float32 [2048], P('fsdp')
The draws below stay inside these ranges and needn't reach their ends.
Inputs may be any that keep to these rules, and one draw needn't show every extreme that they name: `segments`: within each sequence the document numbers start at 0, never fall and rise by at most one from a token to the next; one document of each sequence starts within its first 256 tokens and ends within its last 256 tokens. `positions`: 0 at the first token of each document, else one more than at the token before.
All inputs are finite; a program needn't handle non-finite values.
Results may differ from the reference program's by a relative error of at most 0.015.
Values may be sent and summed in bfloat16 or wider, within the bound.
No kernel may reach another device: no remote copies, remote signals or barrier semaphores. Data moves between devices by JAX's collectives and lax.ppermute only.
A program may use at most 576 MiB of HBM per device.

```python
import jax
import jax.numpy as jnp
from jax import lax

D = 2048
HEADS = 8
FF = 8192
BLOCK = 256
LENGTH = 1024
SEQS = 8


def document_layout(key):
    starts_key, ends_key, cuts_key, choose_key = jax.random.split(key, 4)
    token_index = jnp.arange(LENGTH, dtype=jnp.int32)[None, :]
    order = jax.random.permutation(choose_key, SEQS)
    row_index = jnp.arange(SEQS, dtype=jnp.int32)[:, None]
    whole_row = row_index == order[0]
    busy_row = row_index == order[1]
    doc_begin = jax.random.randint(starts_key, (SEQS, 1), 1, BLOCK)
    finish = jax.random.randint(ends_key, (SEQS, 1), LENGTH - BLOCK + 1, LENGTH)
    doc_begin = jnp.where(whole_row, 0, jnp.where(busy_row, BLOCK - 1, doc_begin))
    finish = jnp.where(whole_row, LENGTH, jnp.where(busy_row, LENGTH - BLOCK + 1, finish))
    cut_flags = (jax.random.randint(cuts_key, (SEQS, LENGTH), 0, 8) == 0) | busy_row
    inside = (token_index >= doc_begin) & (token_index < finish)
    boundary = jnp.where(inside, False, cut_flags)
    boundary = boundary | (token_index == doc_begin) | (token_index == finish)
    boundary = boundary & (token_index > 0)
    segment = jnp.cumsum(boundary.astype(jnp.int32), axis=1).astype(jnp.int32)
    doc_start = lax.cummax(jnp.where(boundary, token_index, 0), axis=1)
    return (segment, (token_index - doc_start).astype(jnp.int32))


def draw_segments(key, part):
    segment, position = document_layout(key)
    return segment


def draw_positions(key, part):
    segment, position = document_layout(key)
    return position


def with_spikes(drawn, key, source, target, shards_of, factor):
    owner, partner = [(jnp.arange(drawn.shape[dim]) // (drawn.shape[dim] // shards_of)).reshape([-1 if axis == dim else 1 for axis in range(drawn.ndim)]) for dim in (source, target)]
    chosen = jax.random.permutation(key, shards_of)[partner]
    strong = (owner == chosen) | (owner == (partner + shards_of // 2) % shards_of)
    return jnp.where(strong, factor * drawn, drawn)


def level_of(stream_key, dims, cuts, least, top_value):
    def one(dim, blocks):
        steps = jax.random.uniform(jax.random.fold_in(jax.random.fold_in(stream_key, 6), dim), (blocks,), jnp.float32, least / len(cuts), top_value / len(cuts))
        return jnp.repeat(jnp.exp(steps), dims[dim] // blocks).reshape((-1,) + (1,) * (len(dims) - dim - 1))

    gain = one(*cuts[0])
    for cut in cuts[1:]:
        gain = gain * one(*cut)
    return gain


def scatter_about(rng, extent, scale, limit, shards=(), kind=jnp.bfloat16):
    drawn = scale * jax.random.normal(rng, extent, jnp.float32)
    if shards:
        drawn = drawn * level_of(rng, extent, shards, -0.22, 0.18)
    return jnp.clip(drawn, -limit, limit).astype(kind)


def heavy_noise(rng, shape, width, limit, cuts, heavy, kind=jnp.bfloat16):
    array = width * jax.random.normal(rng, shape, jnp.float32)
    if cuts:
        array = array * level_of(rng, shape, cuts, -0.22, 0.18)
    return jnp.clip(with_spikes(array, jax.random.fold_in(rng, 3), *heavy), -limit, limit).astype(kind)


def setup_inputs(seed: int = 0) -> dict:
    keys = jax.random.split(jax.random.key(seed), 17)
    tokens = heavy_noise(keys[0], (SEQS, LENGTH, D), 1.0, 6.0, ((0, 8), (1, 4)), (0, 2, 8, 2.0))
    segments = draw_segments(jax.random.fold_in(keys[16], 71), 0)
    positions = draw_positions(jax.random.fold_in(keys[16], 71), 0)
    ln1_gain = jnp.clip(1.0 + 0.1 * jax.random.normal(keys[3], (D,), jnp.float32), 0.5, 1.5).astype(jnp.bfloat16)
    ln1_bias = scatter_about(keys[4], (D,), 0.3, 2.0, ((0, 8),))
    ln2_gain = jnp.clip(1.0 + 0.1 * jax.random.normal(keys[5], (D,), jnp.float32), 0.5, 1.5).astype(jnp.bfloat16)
    ln2_bias = scatter_about(keys[6], (D,), 0.3, 2.0, ((0, 8),))
    qkv_weight = scatter_about(keys[7], (D, 3 * D), D ** -0.5, 0.125, ((0, 8),))
    qkv_bias = scatter_about(keys[8], (3 * D,), 0.3, 2.0, ((0, 8),))
    dense_weight = scatter_about(keys[9], (D, D), (D // 16) ** -0.5, 0.5, ((0, 8),))
    dense_bias = scatter_about(keys[10], (D,), 0.3, 2.0, ((0, 8),))
    fc_in_weight = scatter_about(keys[11], (D, FF), D ** -0.5, 0.125, ((0, 8),))
    fc_in_bias = scatter_about(keys[12], (FF,), 0.3, 2.0, ((0, 8),))
    fc_out_weight = scatter_about(keys[13], (FF, D), FF ** -0.5, 0.0625, ((0, 8),))
    fc_out_bias = scatter_about(keys[14], (D,), 0.3, 2.0, ((0, 8),))
    cotangent = scatter_about(keys[15], (SEQS, LENGTH, D), 1.0, 6.0, ((0, 8), (1, 4)))
    return {"tokens": tokens, "segments": segments, "positions": positions, "ln1_gain": ln1_gain, "ln1_bias": ln1_bias, "ln2_gain": ln2_gain, "ln2_bias": ln2_bias, "qkv_weight": qkv_weight, "qkv_bias": qkv_bias, "dense_weight": dense_weight, "dense_bias": dense_bias, "fc_in_weight": fc_in_weight, "fc_in_bias": fc_in_bias, "fc_out_weight": fc_out_weight, "fc_out_bias": fc_out_bias, "cotangent": cotangent}


@jax.custom_vjp
def low(v):
    return lax.optimization_barrier(v.astype(jnp.bfloat16)).astype(jnp.float32)

@jax.custom_vjp
def low_back(v):
    return v

def low_keep(v):
    return (low(v), None)

def low_pass(kept, grad):
    return (grad,)

def back_keep(v):
    return (v, None)

def back_low(kept, grad):
    return (low(grad),)
low.defvjp(low_keep, low_pass)
low_back.defvjp(back_keep, back_low)
precise = lax.Precision.HIGHEST
eps_norm = 1e-05

def matmul(left_side, right_side):
    return jnp.dot(left_side, right_side, precision=precise)

def layer_norm(values, gain_vec, shift_vec):
    row_mean = lax.optimization_barrier(jnp.mean(values, axis=-1, keepdims=True))
    centred = values - row_mean
    spread = lax.optimization_barrier(jnp.mean(centred * centred, axis=-1, keepdims=True))
    return centred * lax.rsqrt(spread + eps_norm) * gain_vec + shift_vec

def rotary_tables(position, rotary):
    frequency = 10000.0 ** (-jnp.arange(0, rotary, 2, dtype=jnp.float32) / rotary)
    angles = position.astype(jnp.float32)[:, None] * frequency[None, :]
    angles = jnp.concatenate([angles, angles], axis=-1)
    return (jnp.cos(angles), jnp.sin(angles))

def rotate(values, cosine, sine_table):
    rotary = cosine.shape[-1]
    half_rot = rotary // 2
    turned = jnp.concatenate([-values[..., half_rot:rotary], values[..., :half_rot]], axis=-1)
    rotated_head = values[..., :rotary] * cosine[:, None, :] + turned * sine_table[:, None, :]
    return jnp.concatenate([rotated_head, values[..., rotary:]], axis=-1)

def forward(params, values, segment, position):
    gain_one, shift_one, gain_two, shift_two, w_qkv, b_qkv, w_dense, b_dense, w_expand, b_expand, w_reduce, b_reduce = params
    row_count = values.shape[0]
    head_dim = D // HEADS
    score_scale = head_dim ** (-0.5)
    normed_one = low(layer_norm(values, gain_one, shift_one))
    normed_two = low(layer_norm(values, gain_two, shift_two))
    packed = low_back(matmul(normed_one, w_qkv) + b_qkv).reshape(row_count, 3, HEADS, head_dim)
    cosine, sine_table = rotary_tables(position, head_dim // 4)
    queries = low(rotate(packed[:, 0], cosine, sine_table))
    key_heads = low(rotate(packed[:, 1], cosine, sine_table))
    value_heads = low(packed[:, 2])
    scores = low_back(jnp.einsum('qhd,khd->hqk', queries, key_heads, precision=precise)) * score_scale
    token_index = jnp.arange(row_count)
    allowed = (segment[:, None] == segment[None, :]) & (token_index[None, :] <= token_index[:, None])
    scores = jnp.where(allowed[None], scores, -1e+30)
    probs = low(jax.nn.softmax(scores, axis=-1))
    mixed_heads = jnp.einsum('hqk,khd->qhd', probs, value_heads, precision=precise).reshape(row_count, D)
    mixed_heads = low_back(low(mixed_heads))
    attn_out = matmul(mixed_heads, w_dense) + b_dense
    hidden = low_back(matmul(normed_two, w_expand) + b_expand)
    active = low(jax.nn.gelu(hidden, approximate=False))
    mlp_out = matmul(active, w_reduce) + b_reduce
    return values + attn_out + mlp_out

def reference(tokens, segments, positions, ln1_gain, ln1_bias, ln2_gain, ln2_bias, qkv_weight, qkv_bias, dense_weight, dense_bias, fc_in_weight, fc_in_bias, fc_out_weight, fc_out_bias, cotangent):
    params = (ln1_gain.astype(jnp.float32), ln1_bias.astype(jnp.float32), ln2_gain.astype(jnp.float32), ln2_bias.astype(jnp.float32), qkv_weight.astype(jnp.float32), qkv_bias.astype(jnp.float32), dense_weight.astype(jnp.float32), dense_bias.astype(jnp.float32), fc_in_weight.astype(jnp.float32), fc_in_bias.astype(jnp.float32), fc_out_weight.astype(jnp.float32), fc_out_bias.astype(jnp.float32))

    def one_sequence(totals, item):
        values, segment, position, grad_out = item

        def run_layer(weights, inputs):
            return forward(weights, inputs, segment, position)
        result, pullback = jax.vjp(run_layer, params, values)
        weight_grads, value_grads = pullback(grad_out)
        totals = jax.tree.map(jnp.add, totals, weight_grads)
        return (totals, (result.astype(jnp.bfloat16), value_grads))
    zeros = jax.tree.map(jnp.zeros_like, params)
    totals, (output, input_grad) = lax.scan(one_sequence, zeros, (tokens.astype(jnp.float32), segments, positions, cotangent.astype(jnp.float32)))
    return (output, input_grad, totals[0], totals[1], totals[2], totals[3], totals[4], totals[5], totals[6], totals[7], totals[8], totals[9], totals[10], totals[11])
```

```python
import jax
import jax.numpy as jnp
from jax import lax
from jax.sharding import PartitionSpec as P

HEADS = 8


eps_norm = 1e-05


def layer_norm(values, gain_vec, shift_vec):
    row_mean = jnp.mean(values, axis=-1, keepdims=True)
    centred = values - row_mean
    spread = jnp.mean(centred * centred, axis=-1, keepdims=True)
    return centred * lax.rsqrt(spread + eps_norm) * gain_vec + shift_vec


def rotary_tables(position, rotary):
    frequency = 10000.0 ** (-jnp.arange(0, rotary, 2, dtype=jnp.float32) / rotary)
    angles = position.astype(jnp.float32)[:, None] * frequency[None, :]
    angles = jnp.concatenate([angles, angles], axis=-1)
    return (jnp.cos(angles), jnp.sin(angles))


def rotate(values, cosine, sine_table):
    rotary = cosine.shape[-1]
    half_rot = rotary // 2
    turned = jnp.concatenate([-values[..., half_rot:rotary], values[..., :half_rot]], axis=-1)
    rotated_head = values[..., :rotary] * cosine[:, None, :] + turned * sine_table[:, None, :]
    return jnp.concatenate([rotated_head, values[..., rotary:]], axis=-1)


def gelu_exact(tensor):
    return jax.nn.gelu(tensor, approximate=False)


def dot_right(left_side, right_side):
    return lax.dot_general(
        left_side, right_side, (((1,), (1,)), ((), ())), preferred_element_type=jnp.float32
    )


def dot_left(left_side, right_side):
    return lax.dot_general(
        left_side, right_side, (((0,), (0,)), ((), ())), preferred_element_type=jnp.float32
    )


def reduce_grads(weight_one, bias_one, weight_two, bias_two, gain_grad, shift_grad):
    shared = (
        lax.psum_scatter(
            weight_one.astype(jnp.bfloat16), "fsdp", scatter_dimension=0, tiled=True
        ).astype(jnp.float32),
        lax.psum_scatter(
            bias_one.astype(jnp.bfloat16), "fsdp", scatter_dimension=0, tiled=True
        ).astype(jnp.float32),
        lax.psum_scatter(
            weight_two.astype(jnp.bfloat16), "fsdp", scatter_dimension=0, tiled=True
        ).astype(jnp.float32),
        lax.psum_scatter(
            bias_two.astype(jnp.bfloat16), "fsdp", scatter_dimension=0, tiled=True
        ).astype(jnp.float32),
        lax.psum_scatter(
            gain_grad.astype(jnp.bfloat16), "fsdp", scatter_dimension=0, tiled=True
        ).astype(jnp.float32),
        lax.psum_scatter(
            shift_grad.astype(jnp.bfloat16), "fsdp", scatter_dimension=0, tiled=True
        ).astype(jnp.float32),
    )
    return (
        lax.psum(shared[0].astype(jnp.bfloat16), "ctx").astype(jnp.float32),
        lax.psum(shared[1].astype(jnp.bfloat16), "ctx").astype(jnp.float32),
        lax.psum(shared[2].astype(jnp.bfloat16), "ctx").astype(jnp.float32),
        lax.psum(shared[3].astype(jnp.bfloat16), "ctx").astype(jnp.float32),
        lax.psum(shared[4].astype(jnp.bfloat16), "ctx").astype(jnp.float32),
        lax.psum(shared[5].astype(jnp.bfloat16), "ctx").astype(jnp.float32),
    )


def local(
    tokens,
    segments,
    positions,
    ln1_gain,
    ln1_bias,
    ln2_gain,
    ln2_bias,
    qkv_weight,
    qkv_bias,
    dense_weight,
    dense_bias,
    fc_in_weight,
    fc_in_bias,
    fc_out_weight,
    fc_out_bias,
    cotangent,
):
    model_width = tokens.shape[-1]
    values = tokens.reshape(-1, model_width).astype(jnp.float32)
    row_count = values.shape[0]
    head_dim = model_width // HEADS
    score_scale = head_dim ** (-0.5)
    everyone = lax.all_gather(segments, "ctx", axis=1, tiled=True).reshape(-1)
    seq_length = everyone.shape[0]
    own_segment = segments.reshape(-1)
    query_index = lax.axis_index("ctx") * row_count + jnp.arange(row_count, dtype=jnp.int32)
    key_index = jnp.arange(seq_length, dtype=jnp.int32)
    allowed = (own_segment[:, None] == everyone[None, :]) & (
        key_index[None, :] <= query_index[:, None]
    )
    cosine, sine_table = rotary_tables(positions.reshape(-1), head_dim // 4)
    gathered = (
        lax.all_gather(ln1_gain, "fsdp", axis=0, tiled=True),
        lax.all_gather(ln1_bias, "fsdp", axis=0, tiled=True),
        lax.all_gather(ln2_gain, "fsdp", axis=0, tiled=True),
        lax.all_gather(ln2_bias, "fsdp", axis=0, tiled=True),
        lax.all_gather(qkv_weight, "fsdp", axis=0, tiled=True),
        lax.all_gather(qkv_bias, "fsdp", axis=0, tiled=True),
        lax.all_gather(dense_weight, "fsdp", axis=0, tiled=True),
        lax.all_gather(dense_bias, "fsdp", axis=0, tiled=True),
        lax.all_gather(fc_in_weight, "fsdp", axis=0, tiled=True),
        lax.all_gather(fc_in_bias, "fsdp", axis=0, tiled=True),
        lax.all_gather(fc_out_weight, "fsdp", axis=0, tiled=True),
        lax.all_gather(fc_out_bias, "fsdp", axis=0, tiled=True),
    )
    gain_one = gathered[0].astype(jnp.float32)
    shift_one = gathered[1].astype(jnp.float32)
    gain_two = gathered[2].astype(jnp.float32)
    shift_two = gathered[3].astype(jnp.float32)
    normed_one = layer_norm(values, gain_one, shift_one).astype(jnp.bfloat16)
    normed_two = layer_norm(values, gain_two, shift_two).astype(jnp.bfloat16)
    packed = jnp.dot(normed_one, gathered[4], preferred_element_type=jnp.float32) + gathered[
        5
    ].astype(jnp.float32)
    shaped = packed.reshape(row_count, 3, HEADS, head_dim)
    query_low = rotate(shaped[:, 0], cosine, sine_table).astype(jnp.bfloat16)
    key_low = (
        rotate(shaped[:, 1], cosine, sine_table)
        .astype(jnp.bfloat16)
        .reshape(row_count, model_width)
    )
    value_low = shaped[:, 2].astype(jnp.bfloat16).reshape(row_count, model_width)
    keys_all, values_all = (
        lax.all_gather(key_low, "ctx", axis=0, tiled=True),
        lax.all_gather(value_low, "ctx", axis=0, tiled=True),
    )

    def score_block(key_rows):
        raw_scores = jnp.einsum(
            "qhd,khd->hqk",
            query_low,
            key_rows.reshape(seq_length, HEADS, head_dim),
            preferred_element_type=jnp.float32,
        )
        return jnp.where(allowed[None], raw_scores * score_scale, -1e30)

    scores = score_block(keys_all)
    row_max = jnp.max(scores, axis=-1, keepdims=True)
    exp_scores = jnp.exp(scores - row_max)
    row_total = jnp.sum(exp_scores, axis=-1, keepdims=True)
    probs_low = (exp_scores / row_total).astype(jnp.bfloat16)
    log_total = row_max + jnp.log(row_total)
    mixed_heads = jnp.einsum(
        "hqk,khd->qhd",
        probs_low,
        values_all.reshape(seq_length, HEADS, head_dim),
        preferred_element_type=jnp.float32,
    )
    mixed_low = mixed_heads.reshape(row_count, model_width).astype(jnp.bfloat16)
    attn_out = jnp.dot(mixed_low, gathered[6], preferred_element_type=jnp.float32) + gathered[
        7
    ].astype(jnp.float32)
    hidden = jnp.dot(normed_two, gathered[8], preferred_element_type=jnp.float32) + gathered[
        9
    ].astype(jnp.float32)
    active_low = gelu_exact(hidden).astype(jnp.bfloat16)
    mlp_out = jnp.dot(active_low, gathered[10], preferred_element_type=jnp.float32) + gathered[
        11
    ].astype(jnp.float32)
    output = (values + attn_out + mlp_out).astype(jnp.bfloat16).reshape(tokens.shape)
    regathered = (
        lax.all_gather(ln1_gain, "fsdp", axis=0, tiled=True),
        lax.all_gather(ln1_bias, "fsdp", axis=0, tiled=True),
        lax.all_gather(ln2_gain, "fsdp", axis=0, tiled=True),
        lax.all_gather(ln2_bias, "fsdp", axis=0, tiled=True),
        lax.all_gather(qkv_weight, "fsdp", axis=0, tiled=True),
        lax.all_gather(qkv_bias, "fsdp", axis=0, tiled=True),
        lax.all_gather(dense_weight, "fsdp", axis=0, tiled=True),
        lax.all_gather(dense_bias, "fsdp", axis=0, tiled=True),
        lax.all_gather(fc_in_weight, "fsdp", axis=0, tiled=True),
        lax.all_gather(fc_in_bias, "fsdp", axis=0, tiled=True),
        lax.all_gather(fc_out_weight, "fsdp", axis=0, tiled=True),
        lax.all_gather(fc_out_bias, "fsdp", axis=0, tiled=True),
    )
    keys_back, values_back = (
        lax.all_gather(key_low, "ctx", axis=0, tiled=True),
        lax.all_gather(value_low, "ctx", axis=0, tiled=True),
    )
    grad_out = cotangent.reshape(row_count, model_width)
    grad_wide = grad_out.astype(jnp.float32)
    d_active = dot_right(grad_out, regathered[10])
    d_hidden_low = jax.vjp(gelu_exact, hidden)[1](d_active)[0].astype(jnp.bfloat16)
    d_second = dot_right(d_hidden_low, regathered[8])
    d_mixed_low = (
        dot_right(grad_out, regathered[6]).astype(jnp.bfloat16).reshape(row_count, HEADS, head_dim)
    )
    probs_again = jnp.exp(score_block(keys_back) - log_total)
    probs_again_low = probs_again.astype(jnp.bfloat16)
    grad_probs = jnp.einsum(
        "qhd,khd->hqk",
        d_mixed_low,
        values_back.reshape(seq_length, HEADS, head_dim),
        preferred_element_type=jnp.float32,
    )
    row_delta = jnp.sum(probs_again * grad_probs, axis=-1, keepdims=True)
    grad_scores = (probs_again * (grad_probs - row_delta) * score_scale).astype(jnp.bfloat16)
    d_query = jnp.einsum(
        "hqk,khd->qhd",
        grad_scores,
        keys_back.reshape(seq_length, HEADS, head_dim),
        preferred_element_type=jnp.float32,
    )
    d_key = jnp.einsum(
        "hqk,qhd->khd", grad_scores, query_low, preferred_element_type=jnp.float32
    ).reshape(row_count * lax.axis_size("ctx"), model_width)
    d_value = jnp.einsum(
        "hqk,qhd->khd", probs_again_low, d_mixed_low, preferred_element_type=jnp.float32
    ).reshape(row_count * lax.axis_size("ctx"), model_width)
    kv_grad = lax.psum_scatter(
        jnp.concatenate([d_key, d_value], axis=1).astype(jnp.bfloat16),
        "ctx",
        scatter_dimension=0,
        tiled=True,
    ).astype(jnp.float32)
    d_key_own = kv_grad[:, :model_width].reshape(row_count, HEADS, head_dim)
    d_packed = jnp.concatenate(
        [
            rotate(d_query, cosine, -sine_table).reshape(row_count, model_width),
            rotate(d_key_own, cosine, -sine_table).reshape(row_count, model_width),
            kv_grad[:, model_width:],
        ],
        axis=1,
    )
    d_packed_low = d_packed.astype(jnp.bfloat16)
    d_first = dot_right(d_packed_low, regathered[4])
    norm_back_one = jax.vjp(layer_norm, values, gain_one, shift_one)[1]
    d_values_one, d_gain_one, d_shift_one = norm_back_one(d_first)
    norm_back_two = jax.vjp(layer_norm, values, gain_two, shift_two)[1]
    d_values_two, d_gain_two, d_shift_two = norm_back_two(d_second)
    input_grad = (grad_wide + d_values_one + d_values_two).reshape(tokens.shape)
    grad_sum = jnp.sum(grad_wide, axis=0)
    mlp_grads = reduce_grads(
        dot_left(normed_two, d_hidden_low),
        jnp.sum(d_hidden_low.astype(jnp.float32), axis=0),
        dot_left(active_low, grad_out),
        grad_sum,
        d_gain_two,
        d_shift_two,
    )
    attn_grads = reduce_grads(
        dot_left(normed_one, d_packed_low),
        jnp.sum(d_packed_low.astype(jnp.float32), axis=0),
        dot_left(mixed_low, grad_out),
        grad_sum,
        d_gain_one,
        d_shift_one,
    )
    return (
        output,
        input_grad,
        attn_grads[4],
        attn_grads[5],
        mlp_grads[4],
        mlp_grads[5],
        attn_grads[0],
        attn_grads[1],
        attn_grads[2],
        attn_grads[3],
        mlp_grads[0],
        mlp_grads[1],
        mlp_grads[2],
        mlp_grads[3],
    )


def gather_vectors(vectors):
    sizes = [v.shape[0] for v in vectors]
    everything = lax.all_gather(jnp.concatenate(vectors), "fsdp", axis=0, tiled=False)
    whole, start = [], 0
    for size in sizes:
        whole.append(everything[:, start : start + size].reshape(-1).astype(jnp.float32))
        start += size
    return whole


def local_by_head(
    tokens,
    segments,
    positions,
    ln1_gain,
    ln1_bias,
    ln2_gain,
    ln2_bias,
    qkv_weight,
    qkv_bias,
    dense_weight,
    dense_bias,
    fc_in_weight,
    fc_in_bias,
    fc_out_weight,
    fc_out_bias,
    cotangent,
):
    width = tokens.shape[-1]
    block = tokens.shape[1]
    nf = lax.axis_size("fsdp")
    nc = lax.axis_size("ctx")
    me_c = lax.axis_index("ctx")
    me_f = lax.axis_index("fsdp")
    hd = width // HEADS
    units = fc_in_weight.shape[1] // nf
    group = nf * block
    length = nc * block
    mine = nf // nc
    rows = width // nf
    part = rows // nc
    scale = hd ** (-0.5)
    x_own = tokens.reshape(block, width)
    g_own = cotangent.reshape(block, width)

    gain_one, shift_one, gain_two, shift_two, qkv_b, dense_b, fc_out_b = gather_vectors(
        [ln1_gain, ln1_bias, ln2_gain, ln2_bias, qkv_bias, dense_bias, fc_out_bias]
    )
    ints = lax.all_gather(
        jnp.concatenate([segments, positions], axis=0), "fsdp", axis=0, tiled=False
    )
    position_all = ints[:, 1].reshape(group)
    segment_all = lax.all_gather(ints[:, 0], "ctx", axis=1, tiled=True)
    segment_mine = lax.dynamic_slice_in_dim(segment_all, me_c * mine, mine, 0)

    joined = jnp.concatenate(
        [
            lax.dynamic_slice_in_dim(qkv_weight, me_c * part, part, 0)
            .reshape(part, 3, nf, hd)
            .transpose(2, 0, 1, 3)
            .reshape(nf, part, 3 * hd),
            lax.dynamic_slice_in_dim(fc_in_weight, me_c * part, part, 0)
            .reshape(part, nf, units)
            .transpose(1, 0, 2),
        ],
        axis=2,
    )
    quarter = lax.all_to_all(joined, "fsdp", 0, 0, tiled=True)
    columns = lax.all_gather(quarter, "ctx", axis=1, tiled=True).reshape(width, 3 * hd + units)
    w_qkv = columns[:, : 3 * hd]
    w_in = columns[:, 3 * hd :]

    x_all = lax.all_gather(x_own, "fsdp", axis=0, tiled=True)
    g_all = lax.all_gather(g_own, "fsdp", axis=0, tiled=True)
    values = x_all.astype(jnp.float32)
    row_mean = jnp.mean(values, axis=-1, keepdims=True)
    centred = values - row_mean
    spread = jnp.mean(centred * centred, axis=-1, keepdims=True)
    normal = centred * lax.rsqrt(spread + eps_norm)
    first = (normal * gain_one + shift_one).astype(jnp.bfloat16)
    second = (normal * gain_two + shift_two).astype(jnp.bfloat16)

    head_bias = lax.dynamic_index_in_dim(qkv_b.reshape(3, nf, hd), me_f, 1, keepdims=False)
    packed = jnp.dot(first, w_qkv, preferred_element_type=jnp.float32) + head_bias.reshape(-1)
    cosine, sine_table = rotary_tables(position_all, hd // 4)
    shaped = packed.reshape(group, 3, hd)
    turned = rotate(shaped[:, :2], cosine, sine_table)
    mixed = jnp.concatenate([turned, shaped[:, 2:]], axis=1).astype(jnp.bfloat16)
    mixed = mixed.reshape(nf, block, 3 * hd)
    mixed = lax.all_to_all(mixed, "ctx", 0, 1, tiled=True)
    q, k, v = (mixed[..., i * hd : (i + 1) * hd] for i in range(3))

    index = jnp.arange(length, dtype=jnp.int32)
    allowed = (segment_mine[:, :, None] == segment_mine[:, None, :]) & (
        index[None, None, :] <= index[None, :, None]
    )
    scores = jnp.einsum("sqd,skd->sqk", q, k, preferred_element_type=jnp.float32) * scale
    scores = jnp.where(allowed, scores, -1e30)
    row_max = jnp.max(scores, axis=-1, keepdims=True)
    probs = jnp.exp(scores - row_max)
    probs = probs / jnp.sum(probs, axis=-1, keepdims=True)
    probs_low = probs.astype(jnp.bfloat16)
    o = jnp.einsum("sqk,skd->sqd", probs_low, v, preferred_element_type=jnp.float32).astype(
        jnp.bfloat16
    )
    o_back = lax.all_to_all(o, "ctx", 1, 0, tiled=True).reshape(group, hd)

    hidden = jnp.dot(second, w_in, preferred_element_type=jnp.float32) + fc_in_bias.astype(
        jnp.float32
    )
    active = gelu_exact(hidden).astype(jnp.bfloat16)
    partial = jnp.dot(o_back, dense_weight, preferred_element_type=jnp.float32) + jnp.dot(
        active, fc_out_weight, preferred_element_type=jnp.float32
    )
    summed = lax.psum_scatter(
        partial.astype(jnp.bfloat16), "fsdp", scatter_dimension=0, tiled=True
    ).astype(jnp.float32)
    x_wide = x_own.astype(jnp.float32)
    output = (x_wide + summed + dense_b + fc_out_b).astype(jnp.bfloat16).reshape(tokens.shape)

    d_o = dot_right(g_all, dense_weight).astype(jnp.bfloat16).reshape(nf, block, hd)
    d_o = lax.all_to_all(d_o, "ctx", 0, 1, tiled=True)
    d_active = dot_right(g_all, fc_out_weight)
    d_hidden = jax.vjp(gelu_exact, hidden)[1](d_active)[0].astype(jnp.bfloat16)
    grad_fc_out = dot_left(active, g_all).astype(jnp.bfloat16)
    grad_fc_in = dot_left(second, d_hidden).astype(jnp.bfloat16)
    grad_dense = dot_left(o_back, g_all).astype(jnp.bfloat16)

    d_probs = jnp.einsum("sqd,skd->sqk", d_o, v, preferred_element_type=jnp.float32)
    delta = jnp.sum(probs * d_probs, axis=-1, keepdims=True)
    d_scores = (probs * (d_probs - delta) * scale).astype(jnp.bfloat16)
    d_q = jnp.einsum("sqk,skd->sqd", d_scores, k, preferred_element_type=jnp.float32)
    d_k = jnp.einsum("sqk,sqd->skd", d_scores, q, preferred_element_type=jnp.float32)
    d_v = jnp.einsum("sqk,sqd->skd", probs_low, d_o, preferred_element_type=jnp.float32)
    d_mixed = jnp.concatenate([d_q, d_k, d_v], axis=-1).astype(jnp.bfloat16)
    d_mixed = lax.all_to_all(d_mixed, "ctx", 1, 0, tiled=True).reshape(group, 3, hd)
    d_mixed = d_mixed.astype(jnp.float32)
    d_packed = jnp.concatenate(
        [rotate(d_mixed[:, :2], cosine, -sine_table), d_mixed[:, 2:]], axis=1
    ).reshape(group, 3 * hd)
    d_packed = d_packed.astype(jnp.bfloat16)
    grad_qkv = dot_left(first, d_packed).astype(jnp.bfloat16)

    d_first = dot_right(d_packed, w_qkv)
    d_second = dot_right(d_hidden, w_in)
    d_normal = lax.psum_scatter(
        (d_first * gain_one + d_second * gain_two).astype(jnp.bfloat16),
        "fsdp",
        scatter_dimension=0,
        tiled=True,
    ).astype(jnp.float32)
    own_mean = jnp.mean(x_wide, axis=-1, keepdims=True)
    own_centred = x_wide - own_mean
    own_rstd = lax.rsqrt(jnp.mean(own_centred * own_centred, axis=-1, keepdims=True) + eps_norm)
    own_normal = own_centred * own_rstd
    d_x = own_rstd * (
        d_normal
        - jnp.mean(d_normal, axis=-1, keepdims=True)
        - own_normal * jnp.mean(d_normal * own_normal, axis=-1, keepdims=True)
    )
    input_grad = (g_own.astype(jnp.float32) + d_x).reshape(tokens.shape)

    def spread_out(values, parts):
        whole = jnp.zeros((parts, nf, values.shape[0] // parts), jnp.float32)
        return lax.dynamic_update_slice_in_dim(
            whole, values.reshape(parts, 1, -1), me_f, 1
        ).reshape(nf, -1)

    small = jnp.concatenate(
        [
            jnp.sum(d_first * normal, axis=0).reshape(nf, -1),
            jnp.sum(d_first, axis=0).reshape(nf, -1),
            jnp.sum(d_second * normal, axis=0).reshape(nf, -1),
            jnp.sum(d_second, axis=0).reshape(nf, -1),
            spread_out(jnp.sum(d_packed.astype(jnp.float32), axis=0), 3),
            spread_out(jnp.sum(d_hidden.astype(jnp.float32), axis=0), 1),
        ],
        axis=1,
    )
    small = lax.psum_scatter(small, "fsdp", scatter_dimension=0, tiled=True)
    g_sum = lax.dynamic_slice_in_dim(jnp.sum(g_all.astype(jnp.float32), axis=0), me_f * rows, rows)
    small = lax.psum(jnp.concatenate([small.reshape(-1), g_sum]), "ctx")
    qkv_cols = 3 * width // nf
    cuts, start = [], 0
    for size in (rows, rows, rows, rows, qkv_cols, units, rows):
        cuts.append(small[start : start + size])
        start += size

    def by_rows(grad):
        cols = grad.shape[1]
        mine_rows = lax.psum_scatter(
            grad.reshape(nf, nc, part, cols), "ctx", scatter_dimension=1, tiled=True
        ).reshape(nf, part, cols)
        mine_rows = lax.all_to_all(mine_rows, "fsdp", 0, 0, tiled=True)
        return lax.all_gather(mine_rows, "ctx", axis=1, tiled=True).astype(jnp.float32)

    grad_fc_in = by_rows(grad_fc_in).transpose(1, 0, 2).reshape(fc_in_weight.shape)
    grad_qkv = (
        by_rows(grad_qkv)
        .reshape(nf, rows, 3, hd)
        .transpose(1, 2, 0, 3)
        .reshape(qkv_weight.shape)
    )
    grad_fc_out = lax.psum(grad_fc_out, "ctx").astype(jnp.float32)
    grad_dense = lax.psum(grad_dense, "ctx").astype(jnp.float32)
    return (
        output,
        input_grad,
        cuts[0],
        cuts[1],
        cuts[2],
        cuts[3],
        grad_qkv,
        cuts[4],
        grad_dense,
        cuts[6],
        grad_fc_in,
        cuts[5],
        grad_fc_out,
        cuts[6],
    )


def solution(mesh):
    placed = (
        P("fsdp", "ctx", None),
        P("fsdp", "ctx"),
        P("fsdp", "ctx"),
        P("fsdp"),
        P("fsdp"),
        P("fsdp"),
        P("fsdp"),
        P("fsdp", None),
        P("fsdp"),
        P("fsdp", None),
        P("fsdp"),
        P("fsdp", None),
        P("fsdp"),
        P("fsdp", None),
        P("fsdp"),
        P("fsdp", "ctx", None),
    )
    by_head = mesh.shape["fsdp"] == HEADS and HEADS % mesh.shape["ctx"] == 0
    return jax.shard_map(
        local_by_head if by_head else local,
        mesh=mesh,
        in_specs=placed,
        out_specs=(
            P("fsdp", "ctx", None),
            P("fsdp", "ctx", None),
            P("fsdp"),
            P("fsdp"),
            P("fsdp"),
            P("fsdp"),
            P("fsdp", None),
            P("fsdp"),
            P("fsdp", None),
            P("fsdp"),
            P("fsdp", None),
            P("fsdp"),
            P("fsdp", None),
            P("fsdp"),
        ),
        check_vma=False,
    )
```

```python
import jax
import jax.numpy as jnp
from jax import lax
from jax.experimental import pallas as pl
from jax.experimental.pallas import tpu as pltpu
from jax.sharding import PartitionSpec as P

HEADS = 8


eps_norm = 1e-05


def layer_norm(values, gain_vec, shift_vec):
    row_mean = jnp.mean(values, axis=-1, keepdims=True)
    centred = values - row_mean
    spread = jnp.mean(centred * centred, axis=-1, keepdims=True)
    return centred * lax.rsqrt(spread + eps_norm) * gain_vec + shift_vec


def rotary_tables(position, rotary):
    frequency = 10000.0 ** (-jnp.arange(0, rotary, 2, dtype=jnp.float32) / rotary)
    angles = position.astype(jnp.float32)[:, None] * frequency[None, :]
    angles = jnp.concatenate([angles, angles], axis=-1)
    return (jnp.cos(angles), jnp.sin(angles))


def rotate(values, cosine, sine_table):
    rotary = cosine.shape[-1]
    half_rot = rotary // 2
    turned = jnp.concatenate([-values[..., half_rot:rotary], values[..., :half_rot]], axis=-1)
    rotated_head = values[..., :rotary] * cosine[:, None, :] + turned * sine_table[:, None, :]
    return jnp.concatenate([rotated_head, values[..., rotary:]], axis=-1)


def gelu_exact(tensor):
    return jax.nn.gelu(tensor, approximate=False)


def dot_right(left_side, right_side):
    return lax.dot_general(
        left_side, right_side, (((1,), (1,)), ((), ())), preferred_element_type=jnp.float32
    )


def dot_left(left_side, right_side):
    return lax.dot_general(
        left_side, right_side, (((0,), (0,)), ((), ())), preferred_element_type=jnp.float32
    )


def reduce_grads(weight_one, bias_one, weight_two, bias_two, gain_grad, shift_grad):
    shared = (
        lax.psum_scatter(
            weight_one.astype(jnp.bfloat16), "fsdp", scatter_dimension=0, tiled=True
        ).astype(jnp.float32),
        lax.psum_scatter(
            bias_one.astype(jnp.bfloat16), "fsdp", scatter_dimension=0, tiled=True
        ).astype(jnp.float32),
        lax.psum_scatter(
            weight_two.astype(jnp.bfloat16), "fsdp", scatter_dimension=0, tiled=True
        ).astype(jnp.float32),
        lax.psum_scatter(
            bias_two.astype(jnp.bfloat16), "fsdp", scatter_dimension=0, tiled=True
        ).astype(jnp.float32),
        lax.psum_scatter(
            gain_grad.astype(jnp.bfloat16), "fsdp", scatter_dimension=0, tiled=True
        ).astype(jnp.float32),
        lax.psum_scatter(
            shift_grad.astype(jnp.bfloat16), "fsdp", scatter_dimension=0, tiled=True
        ).astype(jnp.float32),
    )
    return (
        lax.psum(shared[0].astype(jnp.bfloat16), "ctx").astype(jnp.float32),
        lax.psum(shared[1].astype(jnp.bfloat16), "ctx").astype(jnp.float32),
        lax.psum(shared[2].astype(jnp.bfloat16), "ctx").astype(jnp.float32),
        lax.psum(shared[3].astype(jnp.bfloat16), "ctx").astype(jnp.float32),
        lax.psum(shared[4].astype(jnp.bfloat16), "ctx").astype(jnp.float32),
        lax.psum(shared[5].astype(jnp.bfloat16), "ctx").astype(jnp.float32),
    )


def local(
    tokens,
    segments,
    positions,
    ln1_gain,
    ln1_bias,
    ln2_gain,
    ln2_bias,
    qkv_weight,
    qkv_bias,
    dense_weight,
    dense_bias,
    fc_in_weight,
    fc_in_bias,
    fc_out_weight,
    fc_out_bias,
    cotangent,
):
    model_width = tokens.shape[-1]
    values = tokens.reshape(-1, model_width).astype(jnp.float32)
    row_count = values.shape[0]
    head_dim = model_width // HEADS
    score_scale = head_dim ** (-0.5)
    everyone = lax.all_gather(segments, "ctx", axis=1, tiled=True).reshape(-1)
    seq_length = everyone.shape[0]
    own_segment = segments.reshape(-1)
    query_index = lax.axis_index("ctx") * row_count + jnp.arange(row_count, dtype=jnp.int32)
    key_index = jnp.arange(seq_length, dtype=jnp.int32)
    allowed = (own_segment[:, None] == everyone[None, :]) & (
        key_index[None, :] <= query_index[:, None]
    )
    cosine, sine_table = rotary_tables(positions.reshape(-1), head_dim // 4)
    gathered = (
        lax.all_gather(ln1_gain, "fsdp", axis=0, tiled=True),
        lax.all_gather(ln1_bias, "fsdp", axis=0, tiled=True),
        lax.all_gather(ln2_gain, "fsdp", axis=0, tiled=True),
        lax.all_gather(ln2_bias, "fsdp", axis=0, tiled=True),
        lax.all_gather(qkv_weight, "fsdp", axis=0, tiled=True),
        lax.all_gather(qkv_bias, "fsdp", axis=0, tiled=True),
        lax.all_gather(dense_weight, "fsdp", axis=0, tiled=True),
        lax.all_gather(dense_bias, "fsdp", axis=0, tiled=True),
        lax.all_gather(fc_in_weight, "fsdp", axis=0, tiled=True),
        lax.all_gather(fc_in_bias, "fsdp", axis=0, tiled=True),
        lax.all_gather(fc_out_weight, "fsdp", axis=0, tiled=True),
        lax.all_gather(fc_out_bias, "fsdp", axis=0, tiled=True),
    )
    gain_one = gathered[0].astype(jnp.float32)
    shift_one = gathered[1].astype(jnp.float32)
    gain_two = gathered[2].astype(jnp.float32)
    shift_two = gathered[3].astype(jnp.float32)
    normed_one = layer_norm(values, gain_one, shift_one).astype(jnp.bfloat16)
    normed_two = layer_norm(values, gain_two, shift_two).astype(jnp.bfloat16)
    packed = jnp.dot(normed_one, gathered[4], preferred_element_type=jnp.float32) + gathered[
        5
    ].astype(jnp.float32)
    shaped = packed.reshape(row_count, 3, HEADS, head_dim)
    query_low = rotate(shaped[:, 0], cosine, sine_table).astype(jnp.bfloat16)
    key_low = (
        rotate(shaped[:, 1], cosine, sine_table)
        .astype(jnp.bfloat16)
        .reshape(row_count, model_width)
    )
    value_low = shaped[:, 2].astype(jnp.bfloat16).reshape(row_count, model_width)
    keys_all, values_all = (
        lax.all_gather(key_low, "ctx", axis=0, tiled=True),
        lax.all_gather(value_low, "ctx", axis=0, tiled=True),
    )

    def score_block(key_rows):
        raw_scores = jnp.einsum(
            "qhd,khd->hqk",
            query_low,
            key_rows.reshape(seq_length, HEADS, head_dim),
            preferred_element_type=jnp.float32,
        )
        return jnp.where(allowed[None], raw_scores * score_scale, -1e30)

    scores = score_block(keys_all)
    row_max = jnp.max(scores, axis=-1, keepdims=True)
    exp_scores = jnp.exp(scores - row_max)
    row_total = jnp.sum(exp_scores, axis=-1, keepdims=True)
    probs_low = (exp_scores / row_total).astype(jnp.bfloat16)
    log_total = row_max + jnp.log(row_total)
    mixed_heads = jnp.einsum(
        "hqk,khd->qhd",
        probs_low,
        values_all.reshape(seq_length, HEADS, head_dim),
        preferred_element_type=jnp.float32,
    )
    mixed_low = mixed_heads.reshape(row_count, model_width).astype(jnp.bfloat16)
    attn_out = jnp.dot(mixed_low, gathered[6], preferred_element_type=jnp.float32) + gathered[
        7
    ].astype(jnp.float32)
    hidden = jnp.dot(normed_two, gathered[8], preferred_element_type=jnp.float32) + gathered[
        9
    ].astype(jnp.float32)
    active_low = gelu_exact(hidden).astype(jnp.bfloat16)
    mlp_out = jnp.dot(active_low, gathered[10], preferred_element_type=jnp.float32) + gathered[
        11
    ].astype(jnp.float32)
    output = (values + attn_out + mlp_out).astype(jnp.bfloat16).reshape(tokens.shape)
    regathered = (
        lax.all_gather(ln1_gain, "fsdp", axis=0, tiled=True),
        lax.all_gather(ln1_bias, "fsdp", axis=0, tiled=True),
        lax.all_gather(ln2_gain, "fsdp", axis=0, tiled=True),
        lax.all_gather(ln2_bias, "fsdp", axis=0, tiled=True),
        lax.all_gather(qkv_weight, "fsdp", axis=0, tiled=True),
        lax.all_gather(qkv_bias, "fsdp", axis=0, tiled=True),
        lax.all_gather(dense_weight, "fsdp", axis=0, tiled=True),
        lax.all_gather(dense_bias, "fsdp", axis=0, tiled=True),
        lax.all_gather(fc_in_weight, "fsdp", axis=0, tiled=True),
        lax.all_gather(fc_in_bias, "fsdp", axis=0, tiled=True),
        lax.all_gather(fc_out_weight, "fsdp", axis=0, tiled=True),
        lax.all_gather(fc_out_bias, "fsdp", axis=0, tiled=True),
    )
    keys_back, values_back = (
        lax.all_gather(key_low, "ctx", axis=0, tiled=True),
        lax.all_gather(value_low, "ctx", axis=0, tiled=True),
    )
    grad_out = cotangent.reshape(row_count, model_width)
    grad_wide = grad_out.astype(jnp.float32)
    d_active = dot_right(grad_out, regathered[10])
    d_hidden_low = jax.vjp(gelu_exact, hidden)[1](d_active)[0].astype(jnp.bfloat16)
    d_second = dot_right(d_hidden_low, regathered[8])
    d_mixed_low = (
        dot_right(grad_out, regathered[6]).astype(jnp.bfloat16).reshape(row_count, HEADS, head_dim)
    )
    probs_again = jnp.exp(score_block(keys_back) - log_total)
    probs_again_low = probs_again.astype(jnp.bfloat16)
    grad_probs = jnp.einsum(
        "qhd,khd->hqk",
        d_mixed_low,
        values_back.reshape(seq_length, HEADS, head_dim),
        preferred_element_type=jnp.float32,
    )
    row_delta = jnp.sum(probs_again * grad_probs, axis=-1, keepdims=True)
    grad_scores = (probs_again * (grad_probs - row_delta) * score_scale).astype(jnp.bfloat16)
    d_query = jnp.einsum(
        "hqk,khd->qhd",
        grad_scores,
        keys_back.reshape(seq_length, HEADS, head_dim),
        preferred_element_type=jnp.float32,
    )
    d_key = jnp.einsum(
        "hqk,qhd->khd", grad_scores, query_low, preferred_element_type=jnp.float32
    ).reshape(row_count * lax.axis_size("ctx"), model_width)
    d_value = jnp.einsum(
        "hqk,qhd->khd", probs_again_low, d_mixed_low, preferred_element_type=jnp.float32
    ).reshape(row_count * lax.axis_size("ctx"), model_width)
    kv_grad = lax.psum_scatter(
        jnp.concatenate([d_key, d_value], axis=1).astype(jnp.bfloat16),
        "ctx",
        scatter_dimension=0,
        tiled=True,
    ).astype(jnp.float32)
    d_key_own = kv_grad[:, :model_width].reshape(row_count, HEADS, head_dim)
    d_packed = jnp.concatenate(
        [
            rotate(d_query, cosine, -sine_table).reshape(row_count, model_width),
            rotate(d_key_own, cosine, -sine_table).reshape(row_count, model_width),
            kv_grad[:, model_width:],
        ],
        axis=1,
    )
    d_packed_low = d_packed.astype(jnp.bfloat16)
    d_first = dot_right(d_packed_low, regathered[4])
    norm_back_one = jax.vjp(layer_norm, values, gain_one, shift_one)[1]
    d_values_one, d_gain_one, d_shift_one = norm_back_one(d_first)
    norm_back_two = jax.vjp(layer_norm, values, gain_two, shift_two)[1]
    d_values_two, d_gain_two, d_shift_two = norm_back_two(d_second)
    input_grad = (grad_wide + d_values_one + d_values_two).reshape(tokens.shape)
    grad_sum = jnp.sum(grad_wide, axis=0)
    mlp_grads = reduce_grads(
        dot_left(normed_two, d_hidden_low),
        jnp.sum(d_hidden_low.astype(jnp.float32), axis=0),
        dot_left(active_low, grad_out),
        grad_sum,
        d_gain_two,
        d_shift_two,
    )
    attn_grads = reduce_grads(
        dot_left(normed_one, d_packed_low),
        jnp.sum(d_packed_low.astype(jnp.float32), axis=0),
        dot_left(mixed_low, grad_out),
        grad_sum,
        d_gain_one,
        d_shift_one,
    )
    return (
        output,
        input_grad,
        attn_grads[4],
        attn_grads[5],
        mlp_grads[4],
        mlp_grads[5],
        attn_grads[0],
        attn_grads[1],
        attn_grads[2],
        attn_grads[3],
        mlp_grads[0],
        mlp_grads[1],
        mlp_grads[2],
        mlp_grads[3],
    )


LANES = 128
FAST = pltpu.CompilerParams(vmem_limit_bytes=56 * 1024 * 1024)
SMALL = pl.CostEstimate(flops=1, bytes_accessed=1, transcendentals=0)
ANY = pl.BlockSpec(memory_space=pl.ANY)
SCALARS = pl.BlockSpec(memory_space=pltpu.SMEM)
WHOLE = pl.BlockSpec(memory_space=pltpu.VMEM)
low = jnp.bfloat16
wide = jnp.float32


def dot(a, b, left=1, right=0):
    return lax.dot_general(a, b, (((left,), (right,)), ((), ())), preferred_element_type=wide)


def swap(values, axis, mask):
    return lax.ppermute(values, axis, [(i, i ^ mask) for i in range(lax.axis_size(axis))])


def at(values, index, axis=0):
    return lax.dynamic_index_in_dim(values, index, axis, keepdims=False)


def added(*values):
    total = values[0].astype(wide)
    for v in values[1:]:
        total = total + v.astype(wide)
    return total.astype(low)


def then(value, *events):
    return lax.optimization_barrier((value,) + events)[0]


def gather_plane(first, second):
    first_x, second_y = swap(first, "ctx", 1), swap(second, "ctx", 2)
    first_y, second_x = swap(first, "ctx", 2), swap(second, "ctx", 1)
    first_xy = swap(first_y, "ctx", 1)
    second_xy = swap(second_x, "ctx", 2)
    return [first, first_x, first_y, first_xy], [second, second_x, second_y, second_xy]


def place(pieces, places, count):
    sizes = [p.shape[0] for p in pieces]

    total = sum(sizes)

    def body(places_ref, *refs):
        out, buf, sems_in, sems_out = refs[-4:]
        copies = []
        for ref, size in zip(refs, sizes):
            for i in range(size):
                n = len(copies)
                copies.append(pltpu.make_async_copy(ref.at[i], buf.at[n], sems_in.at[n]))
                copies[n].start()
        leaving = []
        for n in range(total):
            copies[n].wait()
            copy = pltpu.make_async_copy(buf.at[n], out.at[places_ref[n]], sems_out.at[n])
            copy.start()
            leaving.append(copy)
        for copy in leaving:
            copy.wait()

    return pl.pallas_call(
        body,
        out_shape=jax.ShapeDtypeStruct((count,) + pieces[0].shape[1:], pieces[0].dtype),
        in_specs=[SCALARS] + [ANY] * len(pieces),
        out_specs=ANY,
        scratch_shapes=[
            pltpu.VMEM((total,) + pieces[0].shape[1:], pieces[0].dtype),
            pltpu.SemaphoreType.DMA((total,)),
            pltpu.SemaphoreType.DMA((total,)),
        ],
        compiler_params=FAST,
        cost_estimate=SMALL,
    )(places, *pieces)


def cut_weights(qkv_weight, fc_in_weight, extra, places, hd, units, part):
    span = qkv_weight.shape[1] // 3
    cols = 3 * hd + units

    def body(places_ref, qkv_ref, in_ref, extra_ref, *refs):
        outs, buf, sems_in, sems_out = refs[:4], refs[4], refs[5], refs[6]
        row = pl.ds(pl.multiple_of(places_ref[8] * part, part), part)
        copies = []
        for n in range(8):
            f = places_ref[n]
            for t in range(3):
                copies.append(
                    pltpu.make_async_copy(
                        qkv_ref.at[row, pl.ds(pl.multiple_of(t * span + f * hd, LANES), hd)],
                        buf.at[n, :, pl.ds(t * hd, hd)],
                        sems_in.at[len(copies)],
                    )
                )
                copies[-1].start()
            copies.append(
                pltpu.make_async_copy(
                    in_ref.at[row, pl.ds(pl.multiple_of(f * units, LANES), units)],
                    buf.at[n, :, pl.ds(3 * hd, units)],
                    sems_in.at[len(copies)],
                )
            )
            copies[-1].start()
            copies.append(
                pltpu.make_async_copy(
                    extra_ref, buf.at[n, :, pl.ds(cols, LANES)], sems_in.at[len(copies)]
                )
            )
            copies[-1].start()
        leaving = []
        for n in range(8):
            for copy in copies[5 * n : 5 * n + 5]:
                copy.wait()
            copy = pltpu.make_async_copy(buf.at[n], outs[n % 4].at[n // 4], sems_out.at[n])
            copy.start()
            leaving.append(copy)
        for copy in leaving:
            copy.wait()

    return pl.pallas_call(
        body,
        out_shape=[jax.ShapeDtypeStruct((2, part, cols + LANES), low)] * 4,
        in_specs=[SCALARS, ANY, ANY, ANY],
        out_specs=[ANY] * 4,
        scratch_shapes=[
            pltpu.VMEM((8, part, cols + LANES), low),
            pltpu.SemaphoreType.DMA((40,)),
            pltpu.SemaphoreType.DMA((8,)),
        ],
        compiler_params=FAST,
        cost_estimate=SMALL,
    )(places, qkv_weight, fc_in_weight, extra)


def finish(pieces, rows_at, cols_at, shape, thirds=1):
    sizes = [p.shape[0] for p in pieces]
    total = sum(sizes)
    rows, cols = pieces[0].shape[1:]
    span = cols // thirds

    def body(rows_ref, cols_ref, *refs):
        out, narrow, full, sems_in, sems_out = refs[-5:]
        copies = []
        for ref, size in zip(refs, sizes):
            for i in range(size):
                n = len(copies)
                copies.append(pltpu.make_async_copy(ref.at[i], narrow.at[n], sems_in.at[n]))
                copies[n].start()
        leaving = []
        for n in range(total):
            copies[n].wait()
            full[n] = narrow[n].astype(wide)
            row = pl.ds(pl.multiple_of(rows_ref[n] * rows, rows), rows)
            for t in range(thirds):
                start = t * (shape[1] // thirds) + cols_ref[n] * span
                copy = pltpu.make_async_copy(
                    full.at[n, :, pl.ds(t * span, span)],
                    out.at[row, pl.ds(pl.multiple_of(start, LANES), span)],
                    sems_out.at[n * thirds + t],
                )
                copy.start()
                leaving.append(copy)
        for copy in leaving:
            copy.wait()

    return pl.pallas_call(
        body,
        out_shape=jax.ShapeDtypeStruct(shape, wide),
        in_specs=[SCALARS, SCALARS] + [ANY] * len(pieces),
        out_specs=ANY,
        scratch_shapes=[
            pltpu.VMEM((total, rows, cols), low),
            pltpu.VMEM((total, rows, cols), wide),
            pltpu.SemaphoreType.DMA((total,)),
            pltpu.SemaphoreType.DMA((total * thirds,)),
        ],
        compiler_params=FAST,
        cost_estimate=SMALL,
    )(rows_at, cols_at, *pieces)


def normalised(values):
    centred = values - jnp.mean(values, axis=-1, keepdims=True)
    spread = jnp.mean(centred * centred, axis=-1, keepdims=True)
    rstd = lax.rsqrt(spread + eps_norm)
    return centred * rstd, rstd


def turn_tables(position, rotary):
    cosine, sine = rotary_tables(position, rotary)
    half = rotary // 2
    zero = jnp.zeros((position.shape[0], LANES - rotary), wide)
    none = jnp.zeros_like(sine[:, :half])
    return (
        jnp.concatenate([cosine, zero + 1.0], axis=1),
        jnp.concatenate([-sine[:, :half], none, zero], axis=1),
        jnp.concatenate([none, sine[:, half:], zero], axis=1),
    )


def turn(values, here, above, below, half):
    return (
        values * here
        + pltpu.roll(values, LANES - half, 1) * above
        + pltpu.roll(values, half, 1) * below
    )


def project(x_all, weight, bias, norms, tables, block, hd):
    group, width = x_all.shape
    cols = weight.shape[1]
    half = hd // 8

    def body(x_ref, w_ref, b_ref, n_ref, t0, t1, t2, first_ref, second_ref, out_ref):
        normal, _ = normalised(x_ref[...].astype(wide))
        first = (normal * n_ref[0:1] + n_ref[1:2]).astype(low)
        second_ref[...] = (normal * n_ref[2:3] + n_ref[3:4]).astype(low)
        first_ref[...] = first
        packed = dot(first, w_ref[...]) + b_ref[...]
        for i in range(3):
            lead = packed[:, i * hd : i * hd + LANES]
            if i < 2:
                lead = turn(lead, t0[...], t1[...], t2[...], half)
            out_ref[:, i * hd : i * hd + LANES] = lead.astype(low)
            out_ref[:, i * hd + LANES : (i + 1) * hd] = packed[
                :, i * hd + LANES : (i + 1) * hd
            ].astype(low)

    row = lambda n: pl.BlockSpec((block, n), lambda i: (i, 0))
    return pl.pallas_call(
        body,
        grid=(group // block,),
        in_specs=[row(width), WHOLE, WHOLE, WHOLE, row(LANES), row(LANES), row(LANES)],
        out_specs=[row(width), row(width), row(cols)],
        out_shape=[
            jax.ShapeDtypeStruct((group, width), low),
            jax.ShapeDtypeStruct((group, width), low),
            jax.ShapeDtypeStruct((group, cols), low),
        ],
        compiler_params=FAST,
        cost_estimate=SMALL,
    )(x_all, weight, bias, norms, *tables)


def expand(second, weight, bias, block):
    group, width = second.shape
    cols = weight.shape[1]

    def body(s_ref, w_ref, b_ref, active_ref, slope_ref):
        hidden = dot(s_ref[...], w_ref[...]) + b_ref[...]
        upper = 0.5 * (1.0 + lax.erf(hidden * (0.5**0.5)))
        active_ref[...] = (hidden * upper).astype(low)
        bell = jnp.exp(-0.5 * hidden * hidden) * ((2.0 * jnp.pi) ** -0.5)
        slope_ref[...] = (upper + hidden * bell).astype(low)

    row = lambda n: pl.BlockSpec((block, n), lambda i: (i, 0))
    return pl.pallas_call(
        body,
        grid=(group // block,),
        in_specs=[row(width), WHOLE, WHOLE],
        out_specs=[row(cols), row(cols)],
        out_shape=[jax.ShapeDtypeStruct((group, cols), low)] * 2,
        compiler_params=FAST,
        cost_estimate=SMALL,
    )(second, weight, bias)


def contract(o_back, active, dense_weight, fc_out_weight, block):
    group = active.shape[0]
    width = fc_out_weight.shape[1]

    def body(o_ref, a_ref, w1_ref, w2_ref, out_ref):
        out_ref[...] = (dot(o_ref[...], w1_ref[...]) + dot(a_ref[...], w2_ref[...])).astype(low)

    row = lambda n: pl.BlockSpec((block, n), lambda i: (i, 0))
    return pl.pallas_call(
        body,
        grid=(group // block,),
        in_specs=[row(o_back.shape[1]), row(active.shape[1]), WHOLE, WHOLE],
        out_specs=row(width),
        out_shape=jax.ShapeDtypeStruct((group, width), low),
        compiler_params=FAST,
        cost_estimate=SMALL,
    )(o_back, active, dense_weight, fc_out_weight)


def hidden_back(g_all, fc_out_weight, slope, block):
    group, width = g_all.shape
    units = fc_out_weight.shape[0]

    def body(g_ref, w_ref, s_ref, out_ref, sum_ref):
        @pl.when(pl.program_id(0) == 0)
        def _():
            sum_ref[...] = jnp.zeros_like(sum_ref)

        d_hidden = (dot(g_ref[...], w_ref[...], 1, 1) * s_ref[...].astype(wide)).astype(low)
        out_ref[...] = d_hidden
        sum_ref[...] += jnp.sum(d_hidden.astype(wide), axis=0, keepdims=True)

    row = lambda n: pl.BlockSpec((block, n), lambda i: (i, 0))
    return pl.pallas_call(
        body,
        grid=(group // block,),
        in_specs=[row(width), WHOLE, row(units)],
        out_specs=[row(units), pl.BlockSpec((1, units), lambda i: (0, 0))],
        out_shape=[
            jax.ShapeDtypeStruct((group, units), low),
            jax.ShapeDtypeStruct((1, units), wide),
        ],
        compiler_params=FAST,
        cost_estimate=SMALL,
    )(g_all, fc_out_weight, slope)


def grad_pair(left, right, keep, send, parts):
    tokens = left.shape[0]
    cols = right.shape[1]
    n = len(keep)
    size = LANES // parts

    def body(keep_ref, send_ref, a_ref, b_ref, right_ref, keep_out, send_out):
        both = jnp.concatenate([a_ref[...], b_ref[...]], axis=1)
        result = dot(both, right_ref[...], 0, 0).astype(low)
        keep_out[...] = result[:LANES].reshape(1, parts, size, cols)
        send_out[...] = result[LANES:].reshape(1, parts, size, cols)

    shape = jax.ShapeDtypeStruct((n, parts, size, cols), low)
    out = pl.BlockSpec((1, parts, size, cols), lambda i, k, s: (i, 0, 0, 0))
    return pl.pallas_call(
        body,
        grid_spec=pltpu.PrefetchScalarGridSpec(
            num_scalar_prefetch=2,
            grid=(n,),
            in_specs=[
                pl.BlockSpec((tokens, LANES), lambda i, k, s: (0, k[i])),
                pl.BlockSpec((tokens, LANES), lambda i, k, s: (0, s[i])),
                pl.BlockSpec((tokens, cols), lambda i, k, s: (0, 0)),
            ],
            out_specs=[out, out],
        ),
        out_shape=[shape, shape],
        compiler_params=FAST,
        cost_estimate=SMALL,
    )(jnp.stack(keep).astype(jnp.int32), jnp.stack(send).astype(jnp.int32), left, left, right)


def add_split(kept, got, bit):
    n, _, rows, cols = kept.shape

    def body(bit_ref, a_ref, b_ref, keep_out, send_out):
        for out, half in ((keep_out, bit_ref[0]), (send_out, 1 - bit_ref[0])):
            out[...] = (a_ref[:, half].astype(wide) + b_ref[:, half].astype(wide)).astype(low)

    shape = jax.ShapeDtypeStruct((n, rows, cols), low)
    both = pl.BlockSpec((n // 2 if n > 1 else 1, 2, rows, cols), lambda i: (i, 0, 0, 0))
    out = pl.BlockSpec((n // 2 if n > 1 else 1, rows, cols), lambda i: (i, 0, 0))
    return pl.pallas_call(
        body,
        grid=(2 if n > 1 else 1,),
        in_specs=[SCALARS, both, both],
        out_specs=[out, out],
        out_shape=[shape, shape],
        compiler_params=FAST,
        cost_estimate=SMALL,
    )(bit[None].astype(jnp.int32), kept, got)


def fetch(places_ref, sources, target, sems, block, sequences):
    copies = []
    for m, source in enumerate(sources):
        for s in range(sequences):
            n = len(copies)
            start = pl.multiple_of(places_ref[m] * block, block)
            copies.append(
                pltpu.make_async_copy(source.at[s], target.at[s, pl.ds(start, block)], sems.at[n])
            )
            copies[n].start()
    return copies


def send(places_ref, source, targets, sems):
    copies = [
        pltpu.make_async_copy(source.at[places_ref[m]], target, sems.at[m])
        for m, target in enumerate(targets)
    ]
    for copy in copies:
        copy.start()
    for copy in copies:
        copy.wait()


def block_scores(buf, row_ref, col_ref, s, i, block, hd, scale):
    count = (i + 1) * block
    query = buf[s, i * block : count, 0:hd]
    key = buf[s, 0:count, hd : 2 * hd]
    scores = dot(query, key, 1, 1) * scale
    q_index = lax.broadcasted_iota(jnp.int32, (block, count), 0) + i * block
    k_index = lax.broadcasted_iota(jnp.int32, (block, count), 1)
    allowed = (col_ref[s, i * block : count, :] == row_ref[s, :, 0:count]) & (k_index <= q_index)
    scores = jnp.where(allowed, scores, -1e30)
    probs = jnp.exp(scores - jnp.max(scores, axis=-1, keepdims=True))
    return query, key, probs / jnp.sum(probs, axis=-1, keepdims=True)


def attend(parts, places, seg_row, seg_col, hd):
    count = len(parts)
    sequences, block, cols = parts[0].shape
    scale = hd ** (-0.5)

    def body(places_ref, row_ref, col_ref, *refs):
        outs, (buf, mixed, sems_in, sems_out) = refs[-4 - count : -4], refs[-4:]
        for copy in fetch(places_ref, refs[:count], buf, sems_in, block, sequences):
            copy.wait()
        for s in range(sequences):
            for i in range(count):
                _, _, probs = block_scores(buf, row_ref, col_ref, s, i, block, hd, scale)
                value = buf[s, 0 : (i + 1) * block, 2 * hd : 3 * hd]
                mixed[i, s] = dot(probs.astype(low), value).astype(low)
        send(places_ref, mixed, outs, sems_out)

    return pl.pallas_call(
        body,
        out_shape=[jax.ShapeDtypeStruct((sequences, block, hd), low)] * count,
        in_specs=[SCALARS, WHOLE, WHOLE] + [ANY] * count,
        out_specs=[ANY] * count,
        scratch_shapes=[
            pltpu.VMEM((sequences, count * block, cols), low),
            pltpu.VMEM((count, sequences, block, hd), low),
            pltpu.SemaphoreType.DMA((count * sequences,)),
            pltpu.SemaphoreType.DMA((count,)),
        ],
        compiler_params=FAST,
        cost_estimate=SMALL,
    )(places, seg_row, seg_col, *parts)


def attend_back(parts, d_parts, places, seg_row, seg_col, tables, hd):
    count = len(parts)
    sequences, block, cols = parts[0].shape
    length = count * block
    scale = hd ** (-0.5)
    half = hd // 8

    def body(places_ref, row_ref, col_ref, t0, t1, t2, *refs):
        outs = refs[2 * count : 3 * count]
        buf, d_buf, key_sum, value_sum, done, sems_in, sems_d, sems_out = refs[3 * count :]
        waits = fetch(places_ref, refs[:count], buf, sems_in, block, sequences)
        waits += fetch(places_ref, refs[count : 2 * count], d_buf, sems_d, block, sequences)
        for copy in waits:
            copy.wait()

        def put(values, s, i, which):
            lead = values[:, 0:LANES]
            if which < 2:
                rows = slice(i * block, (i + 1) * block)
                lead = turn(lead, t0[s, rows], -t1[s, rows], -t2[s, rows], half)
            done[i, s, :, which * hd : which * hd + LANES] = lead.astype(low)
            done[i, s, :, which * hd + LANES : (which + 1) * hd] = values[:, LANES:].astype(low)

        for s in range(sequences):
            for i in reversed(range(count)):
                n = (i + 1) * block
                query, key, probs = block_scores(buf, row_ref, col_ref, s, i, block, hd, scale)
                value = buf[s, 0:n, 2 * hd : 3 * hd]
                d_out = d_buf[s, i * block : n]
                d_probs = dot(d_out, value, 1, 1)
                delta = jnp.sum(probs * d_probs, axis=-1, keepdims=True)
                d_scores = (probs * (d_probs - delta) * scale).astype(low)
                put(dot(d_scores, key), s, i, 0)
                key_part = dot(d_scores, query, 0, 0)
                value_part = dot(probs.astype(low), d_out, 0, 0)
                if i == count - 1:
                    key_sum[...] = key_part
                    value_sum[...] = value_part
                else:
                    key_sum[0:n] += key_part
                    value_sum[0:n] += value_part
                put(key_sum[i * block : n], s, i, 1)
                put(value_sum[i * block : n], s, i, 2)
        send(places_ref, done, outs, sems_out)

    return pl.pallas_call(
        body,
        out_shape=[jax.ShapeDtypeStruct((sequences, block, cols), low)] * count,
        in_specs=[SCALARS] + [WHOLE] * 5 + [ANY] * (2 * count),
        out_specs=[ANY] * count,
        scratch_shapes=[
            pltpu.VMEM((sequences, length, cols), low),
            pltpu.VMEM((sequences, length, hd), low),
            pltpu.VMEM((length, hd), wide),
            pltpu.VMEM((length, hd), wide),
            pltpu.VMEM((count, sequences, block, cols), low),
            pltpu.SemaphoreType.DMA((count * sequences,)),
            pltpu.SemaphoreType.DMA((count * sequences,)),
            pltpu.SemaphoreType.DMA((count,)),
        ],
        compiler_params=FAST,
        cost_estimate=SMALL,
    )(places, seg_row, seg_col, *tables, *parts, *d_parts)


def norm_back(x_all, d_packed, d_hidden, w_qkv, w_in, gains, block):
    group, width = x_all.shape

    def body(x_ref, p_ref, h_ref, w1_ref, w2_ref, g_ref, out_ref, sums_ref):
        @pl.when(pl.program_id(0) == 0)
        def _():
            sums_ref[...] = jnp.zeros_like(sums_ref)

        normal, _ = normalised(x_ref[...].astype(wide))
        one = dot(p_ref[...], w1_ref[...], 1, 1)
        two = dot(h_ref[...], w2_ref[...], 1, 1)
        out_ref[...] = (one * g_ref[0:1] + two * g_ref[2:3]).astype(low)
        sums_ref[0:1] += jnp.sum(one * normal, axis=0, keepdims=True)
        sums_ref[1:2] += jnp.sum(one, axis=0, keepdims=True)
        sums_ref[2:3] += jnp.sum(two * normal, axis=0, keepdims=True)
        sums_ref[3:4] += jnp.sum(two, axis=0, keepdims=True)

    row = lambda n: pl.BlockSpec((block, n), lambda i: (i, 0))
    return pl.pallas_call(
        body,
        grid=(group // block,),
        in_specs=[row(width), row(d_packed.shape[1]), row(d_hidden.shape[1])] + [WHOLE] * 3,
        out_specs=[row(width), pl.BlockSpec((4, width), lambda i: (0, 0))],
        out_shape=[
            jax.ShapeDtypeStruct((group, width), low),
            jax.ShapeDtypeStruct((4, width), wide),
        ],
        compiler_params=FAST,
        cost_estimate=SMALL,
    )(x_all, d_packed, d_hidden, w_qkv, w_in, gains)


def local_by_head(
    tokens,
    segments,
    positions,
    ln1_gain,
    ln1_bias,
    ln2_gain,
    ln2_bias,
    qkv_weight,
    qkv_bias,
    dense_weight,
    dense_bias,
    fc_in_weight,
    fc_in_bias,
    fc_out_weight,
    fc_out_bias,
    cotangent,
):
    width = tokens.shape[-1]
    block = tokens.shape[1]
    nf = lax.axis_size("fsdp")
    nc = lax.axis_size("ctx")
    me_c = lax.axis_index("ctx")
    me_f = lax.axis_index("fsdp")
    hd = width // HEADS
    units = fc_in_weight.shape[1] // nf
    group = nf * block
    length = nc * block
    rows = width // nf
    part = rows // nc
    x_own = tokens.reshape(block, width)
    g_own = cotangent.reshape(block, width)
    order = jnp.array([2 * j + kk for kk in range(2) for j in range(4)], jnp.int32)
    owners = jnp.bitwise_xor(order, me_f)
    plane = jnp.bitwise_xor(jnp.arange(nc, dtype=jnp.int32), me_c)

    ints = jnp.concatenate([segments, positions], axis=0)
    digits = jnp.concatenate([ints // 32, ints % 32]).astype(low)
    vectors = [ln1_gain, ln1_bias, ln2_gain, ln2_bias, qkv_bias, dense_bias, fc_out_bias]
    sizes = [v.shape[0] for v in vectors]
    extra = jnp.concatenate([digits.reshape(-1)] + vectors)
    extra = jnp.pad(extra, (0, part * LANES - extra.shape[0])).reshape(part, LANES)

    pieces = cut_weights(
        qkv_weight,
        fc_in_weight,
        extra,
        jnp.concatenate([owners, me_c[None]]).astype(jnp.int32),
        hd,
        units,
        part,
    )
    got = [pieces[0]] + [swap(pieces[j], "fsdp", 2 * j) for j in (1, 2, 3)]
    x_all = lax.all_gather(then(x_own, *got), "fsdp", axis=0, tiled=True)
    across = swap(jnp.stack([g[1] for g in got]), "fsdp", 1)
    g_all = lax.all_gather(then(g_own, across), "fsdp", axis=0, tiled=True)
    quarter = jnp.concatenate([jnp.stack([g[0] for g in got]), across])
    cols = 3 * hd + units
    qkv_parts, in_parts = gather_plane(quarter[..., : 3 * hd], quarter[..., 3 * hd : cols])

    back = (jnp.arange(nf, dtype=jnp.int32)[:, None] == owners[None, :]).astype(low)
    small = dot(back, quarter[..., cols:].reshape(nf, part * LANES))
    count = 4 * block
    digits = small[:, :count].astype(jnp.int32).reshape(nf, 2, 2, block)
    numbers = digits[:, 0] * 32 + digits[:, 1]
    position_group = numbers[:, 1].reshape(group)
    of_chip = numbers.reshape(4, 2, 2, block)
    seq_ints = [at(of_chip, me_c)] + [swap(at(of_chip, plane[m]), "ctx", m) for m in range(1, nc)]
    seq_ints = jnp.stack(seq_ints, axis=2)
    seq_ints = jnp.stack([at(seq_ints, plane[b], 2) for b in range(nc)], axis=2)
    seq_ints = seq_ints.reshape(2, 2, length)
    seg_row = seq_ints[:, 0][:, None, :]
    seg_col = seq_ints[:, 0][:, :, None]
    tables = turn_tables(position_group, hd // 4)
    seq_tables = [
        t.reshape(2, length, LANES) for t in turn_tables(seq_ints[:, 1].reshape(-1), hd // 4)
    ]
    whole, start = [], count
    for size in sizes:
        whole.append(small[:, start : start + size].reshape(-1))
        start += size
    norms = jnp.stack(whole[:4])
    head_bias = at(whole[4].reshape(3, nf, hd), me_f, 1).reshape(1, -1)

    row_places = (owners[None, :] * nc + plane[:, None]).reshape(-1)
    w_qkv = place(qkv_parts, row_places, nf * nc).reshape(width, 3 * hd)
    w_in = place(in_parts, row_places, nf * nc).reshape(width, units)

    first, second, packed = project(
        then(x_all, w_in), w_qkv, head_bias, norms, tables, block, hd
    )

    def to_sequences(values):
        blocks = values.reshape(4, 2, block, values.shape[1])
        return [
            at(blocks, plane[m]) if m == 0 else swap(at(blocks, plane[m]), "ctx", m)
            for m in range(nc)
        ]

    def to_group(values):
        got = [values[m] if m == 0 else swap(values[m], "ctx", m) for m in range(nc)]
        places = (2 * plane[:, None] + jnp.arange(2, dtype=jnp.int32)[None, :]).reshape(-1)
        return place(got, places, nf).reshape(group, values[0].shape[-1])

    parts = to_sequences(packed)
    active, slope = expand(
        then(second, packed), w_in, fc_in_bias.astype(wide).reshape(1, -1), block
    )
    o = attend([then(p, active) for p in parts], plane, seg_row, seg_col, hd)
    o_back = to_group(o)
    x_bit, y_bit = me_c % 2, me_c // 2
    d_o = dot(then(g_all, *o), dense_weight, 1, 1).astype(low)
    d_parts = to_sequences(d_o)
    partial = contract(then(o_back, d_o), active, dense_weight, fc_out_weight, block)
    summed = lax.psum_scatter(partial, "fsdp", scatter_dimension=0, tiled=True)
    d_qkv = attend_back(
        parts, [then(p, partial) for p in d_parts], plane, seg_row, seg_col, seq_tables, hd
    )
    d_packed = to_group(d_qkv)

    rows_of = units // (nc * LANES)
    blocks = [((2 * y) * rows_of, s) for y in range(2) for s in range(rows_of)]
    out_kept, out_sent = grad_pair(
        active,
        then(g_all, *d_qkv),
        [b + x_bit * rows_of + s for b, s in blocks],
        [b + (1 - x_bit) * rows_of + s for b, s in blocks],
        1,
    )
    out_shape = (1, 2, rows_of * LANES, width)
    out_got = swap(out_sent.reshape(out_shape), "ctx", 1)
    out_kept = out_kept.reshape(out_shape)
    d_hidden, hidden_sum = hidden_back(then(g_all, out_sent), fc_out_weight, slope, block)
    by_bit = lambda bit: ([2 * f + bit for f in range(nf)], [2 * f + 1 - bit for f in range(nf)])
    in_kept, in_sent = grad_pair(second, d_hidden, *by_bit(y_bit), 2)
    in_got = swap(in_sent, "ctx", 2)
    qkv_kept, qkv_sent = grad_pair(first, then(d_packed, in_sent), *by_bit(x_bit), 2)
    qkv_got = swap(qkv_sent, "ctx", 1)
    d_partial, sums = norm_back(
        then(x_all, qkv_sent), d_packed, d_hidden, w_qkv, w_in, norms, block
    )
    dense_kept, dense_sent = grad_pair(
        o_back, then(g_all, d_partial), [y_bit], [1 - y_bit], 2
    )
    def spread_out(values, parts):
        whole = jnp.zeros((parts, nf, values.shape[0] // parts), wide)
        return lax.dynamic_update_slice_in_dim(
            whole, values.reshape(parts, 1, -1), me_f, 1
        ).reshape(nf, -1)

    totals = jnp.concatenate(
        [sums[i].reshape(nf, -1) for i in range(4)]
        + [
            spread_out(jnp.sum(d_packed.astype(wide), axis=0), 3),
            spread_out(hidden_sum[0], 1),
            jnp.sum(g_own.astype(wide), axis=0).reshape(nf, -1),
        ],
        axis=1,
    )
    total_1 = swap(totals, "fsdp", 1)
    out_kept, out_sent = add_split(out_kept, then(out_got, dense_sent, total_1), y_bit)
    out_got = swap(out_sent, "ctx", 2)
    totals = totals + total_1
    total_2 = swap(totals, "fsdp", 2)
    in_kept, in_sent = add_split(in_kept, then(in_got, out_sent, total_2), x_bit)
    in_got = swap(in_sent, "ctx", 1)
    totals = totals + total_2
    total_3 = swap(totals, "fsdp", 4)
    qkv_kept, qkv_sent = add_split(qkv_kept, then(qkv_got, in_sent, total_3), y_bit)
    qkv_got = swap(qkv_sent, "ctx", 2)
    d_normal = lax.psum_scatter(
        then(d_partial, summed, qkv_sent), "fsdp", scatter_dimension=0, tiled=True
    ).astype(wide)
    totals = totals + total_3
    total_4 = swap(totals, "ctx", 1)
    dense_got = swap(then(dense_sent, qkv_sent), "ctx", 2)
    out_mine = added(out_kept, then(out_got, qkv_sent, total_4))
    out_x, out_y = swap(out_mine, "ctx", 1), swap(out_mine, "ctx", 2)
    totals = totals + total_4
    total_5 = swap(totals, "ctx", 2)
    dense_kept, dense_sent = add_split(dense_kept, then(dense_got, qkv_sent, total_5), x_bit)
    totals = totals + total_5
    dense_got = swap(dense_sent, "ctx", 1)
    in_mine = added(in_kept, then(in_got, dense_sent))
    in_rows = lax.all_to_all(in_mine, "fsdp", 0, 0, tiled=True)
    qkv_mine = added(qkv_kept, then(qkv_got, in_got))
    dense_mine = added(dense_kept, then(dense_got, qkv_got))
    out_xy = swap(then(out_y, dense_got), "ctx", 1)
    qkv_rows = lax.all_to_all(then(qkv_mine, in_rows), "fsdp", 0, 0, tiled=True)
    dense_x, dense_y = swap(dense_mine, "ctx", 1), swap(dense_mine, "ctx", 2)
    in_x, in_y = swap(in_rows, "ctx", 1), swap(in_rows, "ctx", 2)
    dense_xy = swap(then(dense_x, qkv_rows), "ctx", 2)
    qkv_x, qkv_y = swap(qkv_rows, "ctx", 1), swap(qkv_rows, "ctx", 2)
    in_xy = swap(in_x, "ctx", 2)
    qkv_xy = swap(qkv_y, "ctx", 1)
    out_all = [out_mine, out_x, out_y, out_xy]
    in_all = [in_rows, in_x, in_y, in_xy]
    dense_all = [dense_mine, dense_x, dense_y, dense_xy]
    qkv_all = [qkv_rows, qkv_x, qkv_y, qkv_xy]

    def whole_rows(pieces, shape):
        return finish(pieces, plane, jnp.zeros((nc,), jnp.int32), shape)

    def whole_columns(pieces, places, shape, thirds):
        at_rows = (places[:, None] * jnp.ones((nf,), jnp.int32)).reshape(-1)
        at_cols = jnp.tile(jnp.arange(nf, dtype=jnp.int32), nc)
        return finish(pieces, at_rows, at_cols, shape, thirds)

    grad_fc_out = whole_rows(out_all, fc_out_weight.shape)
    grad_fc_in = whole_columns(in_all, plane, fc_in_weight.shape, 1)
    grad_dense = whole_rows(dense_all, dense_weight.shape)
    grad_qkv = whole_columns(qkv_all, 2 * (plane % 2) + plane // 2, qkv_weight.shape, 3)

    x_wide = x_own.astype(wide)
    output = (x_wide + summed.astype(wide) + whole[5] + whole[6]).astype(low).reshape(tokens.shape)
    own_normal, own_rstd = normalised(x_wide)
    d_x = own_rstd * (
        d_normal
        - jnp.mean(d_normal, axis=-1, keepdims=True)
        - own_normal * jnp.mean(d_normal * own_normal, axis=-1, keepdims=True)
    )
    input_grad = (g_own.astype(wide) + d_x).reshape(tokens.shape)

    totals = at(totals, me_f)
    cuts, start = [], 0
    for size in (rows, rows, rows, rows, 3 * width // nf, units, rows):
        cuts.append(totals[start : start + size])
        start += size
    return (
        output,
        input_grad,
        cuts[0],
        cuts[1],
        cuts[2],
        cuts[3],
        grad_qkv,
        cuts[4],
        grad_dense,
        cuts[6],
        grad_fc_in,
        cuts[5],
        grad_fc_out,
        cuts[6],
    )


def solution(mesh):
    placed = (
        P("fsdp", "ctx", None),
        P("fsdp", "ctx"),
        P("fsdp", "ctx"),
        P("fsdp"),
        P("fsdp"),
        P("fsdp"),
        P("fsdp"),
        P("fsdp", None),
        P("fsdp"),
        P("fsdp", None),
        P("fsdp"),
        P("fsdp", None),
        P("fsdp"),
        P("fsdp", None),
        P("fsdp"),
        P("fsdp", "ctx", None),
    )
    by_head = mesh.shape["fsdp"] == HEADS and mesh.shape["ctx"] == 4
    return jax.shard_map(
        local_by_head if by_head else local,
        mesh=mesh,
        in_specs=placed,
        out_specs=(
            P("fsdp", "ctx", None),
            P("fsdp", "ctx", None),
            P("fsdp"),
            P("fsdp"),
            P("fsdp"),
            P("fsdp"),
            P("fsdp", None),
            P("fsdp"),
            P("fsdp", None),
            P("fsdp"),
            P("fsdp", None),
            P("fsdp"),
            P("fsdp", None),
            P("fsdp"),
        ),
        check_vma=False,
    )
```

```python
import jax
import jax.numpy as jnp
from jax import lax
from jax.experimental import pallas as pl
from jax.experimental.pallas import tpu as pltpu
from jax.sharding import PartitionSpec as P

HEADS = 8


eps_norm = 1e-05


def layer_norm(values, gain_vec, shift_vec):
    row_mean = jnp.mean(values, axis=-1, keepdims=True)
    centred = values - row_mean
    spread = jnp.mean(centred * centred, axis=-1, keepdims=True)
    return centred * lax.rsqrt(spread + eps_norm) * gain_vec + shift_vec


def rotary_tables(position, rotary):
    frequency = 10000.0 ** (-jnp.arange(0, rotary, 2, dtype=jnp.float32) / rotary)
    angles = position.astype(jnp.float32)[:, None] * frequency[None, :]
    angles = jnp.concatenate([angles, angles], axis=-1)
    return (jnp.cos(angles), jnp.sin(angles))


def rotate(values, cosine, sine_table):
    rotary = cosine.shape[-1]
    half_rot = rotary // 2
    turned = jnp.concatenate([-values[..., half_rot:rotary], values[..., :half_rot]], axis=-1)
    rotated_head = values[..., :rotary] * cosine[:, None, :] + turned * sine_table[:, None, :]
    return jnp.concatenate([rotated_head, values[..., rotary:]], axis=-1)


def gelu_exact(tensor):
    return jax.nn.gelu(tensor, approximate=False)


def dot_right(left_side, right_side):
    return lax.dot_general(
        left_side, right_side, (((1,), (1,)), ((), ())), preferred_element_type=jnp.float32
    )


def dot_left(left_side, right_side):
    return lax.dot_general(
        left_side, right_side, (((0,), (0,)), ((), ())), preferred_element_type=jnp.float32
    )


def reduce_grads(weight_one, bias_one, weight_two, bias_two, gain_grad, shift_grad):
    shared = (
        lax.psum_scatter(
            weight_one.astype(jnp.bfloat16), "fsdp", scatter_dimension=0, tiled=True
        ).astype(jnp.float32),
        lax.psum_scatter(
            bias_one.astype(jnp.bfloat16), "fsdp", scatter_dimension=0, tiled=True
        ).astype(jnp.float32),
        lax.psum_scatter(
            weight_two.astype(jnp.bfloat16), "fsdp", scatter_dimension=0, tiled=True
        ).astype(jnp.float32),
        lax.psum_scatter(
            bias_two.astype(jnp.bfloat16), "fsdp", scatter_dimension=0, tiled=True
        ).astype(jnp.float32),
        lax.psum_scatter(
            gain_grad.astype(jnp.bfloat16), "fsdp", scatter_dimension=0, tiled=True
        ).astype(jnp.float32),
        lax.psum_scatter(
            shift_grad.astype(jnp.bfloat16), "fsdp", scatter_dimension=0, tiled=True
        ).astype(jnp.float32),
    )
    return (
        lax.psum(shared[0].astype(jnp.bfloat16), "ctx").astype(jnp.float32),
        lax.psum(shared[1].astype(jnp.bfloat16), "ctx").astype(jnp.float32),
        lax.psum(shared[2].astype(jnp.bfloat16), "ctx").astype(jnp.float32),
        lax.psum(shared[3].astype(jnp.bfloat16), "ctx").astype(jnp.float32),
        lax.psum(shared[4].astype(jnp.bfloat16), "ctx").astype(jnp.float32),
        lax.psum(shared[5].astype(jnp.bfloat16), "ctx").astype(jnp.float32),
    )


def local(
    tokens,
    segments,
    positions,
    ln1_gain,
    ln1_bias,
    ln2_gain,
    ln2_bias,
    qkv_weight,
    qkv_bias,
    dense_weight,
    dense_bias,
    fc_in_weight,
    fc_in_bias,
    fc_out_weight,
    fc_out_bias,
    cotangent,
):
    model_width = tokens.shape[-1]
    values = tokens.reshape(-1, model_width).astype(jnp.float32)
    row_count = values.shape[0]
    head_dim = model_width // HEADS
    score_scale = head_dim ** (-0.5)
    everyone = lax.all_gather(segments, "ctx", axis=1, tiled=True).reshape(-1)
    seq_length = everyone.shape[0]
    own_segment = segments.reshape(-1)
    query_index = lax.axis_index("ctx") * row_count + jnp.arange(row_count, dtype=jnp.int32)
    key_index = jnp.arange(seq_length, dtype=jnp.int32)
    allowed = (own_segment[:, None] == everyone[None, :]) & (
        key_index[None, :] <= query_index[:, None]
    )
    cosine, sine_table = rotary_tables(positions.reshape(-1), head_dim // 4)
    gathered = (
        lax.all_gather(ln1_gain, "fsdp", axis=0, tiled=True),
        lax.all_gather(ln1_bias, "fsdp", axis=0, tiled=True),
        lax.all_gather(ln2_gain, "fsdp", axis=0, tiled=True),
        lax.all_gather(ln2_bias, "fsdp", axis=0, tiled=True),
        lax.all_gather(qkv_weight, "fsdp", axis=0, tiled=True),
        lax.all_gather(qkv_bias, "fsdp", axis=0, tiled=True),
        lax.all_gather(dense_weight, "fsdp", axis=0, tiled=True),
        lax.all_gather(dense_bias, "fsdp", axis=0, tiled=True),
        lax.all_gather(fc_in_weight, "fsdp", axis=0, tiled=True),
        lax.all_gather(fc_in_bias, "fsdp", axis=0, tiled=True),
        lax.all_gather(fc_out_weight, "fsdp", axis=0, tiled=True),
        lax.all_gather(fc_out_bias, "fsdp", axis=0, tiled=True),
    )
    gain_one = gathered[0].astype(jnp.float32)
    shift_one = gathered[1].astype(jnp.float32)
    gain_two = gathered[2].astype(jnp.float32)
    shift_two = gathered[3].astype(jnp.float32)
    normed_one = layer_norm(values, gain_one, shift_one).astype(jnp.bfloat16)
    normed_two = layer_norm(values, gain_two, shift_two).astype(jnp.bfloat16)
    packed = jnp.dot(normed_one, gathered[4], preferred_element_type=jnp.float32) + gathered[
        5
    ].astype(jnp.float32)
    shaped = packed.reshape(row_count, 3, HEADS, head_dim)
    query_low = rotate(shaped[:, 0], cosine, sine_table).astype(jnp.bfloat16)
    key_low = (
        rotate(shaped[:, 1], cosine, sine_table)
        .astype(jnp.bfloat16)
        .reshape(row_count, model_width)
    )
    value_low = shaped[:, 2].astype(jnp.bfloat16).reshape(row_count, model_width)
    keys_all, values_all = (
        lax.all_gather(key_low, "ctx", axis=0, tiled=True),
        lax.all_gather(value_low, "ctx", axis=0, tiled=True),
    )

    def score_block(key_rows):
        raw_scores = jnp.einsum(
            "qhd,khd->hqk",
            query_low,
            key_rows.reshape(seq_length, HEADS, head_dim),
            preferred_element_type=jnp.float32,
        )
        return jnp.where(allowed[None], raw_scores * score_scale, -1e30)

    scores = score_block(keys_all)
    row_max = jnp.max(scores, axis=-1, keepdims=True)
    exp_scores = jnp.exp(scores - row_max)
    row_total = jnp.sum(exp_scores, axis=-1, keepdims=True)
    probs_low = (exp_scores / row_total).astype(jnp.bfloat16)
    log_total = row_max + jnp.log(row_total)
    mixed_heads = jnp.einsum(
        "hqk,khd->qhd",
        probs_low,
        values_all.reshape(seq_length, HEADS, head_dim),
        preferred_element_type=jnp.float32,
    )
    mixed_low = mixed_heads.reshape(row_count, model_width).astype(jnp.bfloat16)
    attn_out = jnp.dot(mixed_low, gathered[6], preferred_element_type=jnp.float32) + gathered[
        7
    ].astype(jnp.float32)
    hidden = jnp.dot(normed_two, gathered[8], preferred_element_type=jnp.float32) + gathered[
        9
    ].astype(jnp.float32)
    active_low = gelu_exact(hidden).astype(jnp.bfloat16)
    mlp_out = jnp.dot(active_low, gathered[10], preferred_element_type=jnp.float32) + gathered[
        11
    ].astype(jnp.float32)
    output = (values + attn_out + mlp_out).astype(jnp.bfloat16).reshape(tokens.shape)
    regathered = (
        lax.all_gather(ln1_gain, "fsdp", axis=0, tiled=True),
        lax.all_gather(ln1_bias, "fsdp", axis=0, tiled=True),
        lax.all_gather(ln2_gain, "fsdp", axis=0, tiled=True),
        lax.all_gather(ln2_bias, "fsdp", axis=0, tiled=True),
        lax.all_gather(qkv_weight, "fsdp", axis=0, tiled=True),
        lax.all_gather(qkv_bias, "fsdp", axis=0, tiled=True),
        lax.all_gather(dense_weight, "fsdp", axis=0, tiled=True),
        lax.all_gather(dense_bias, "fsdp", axis=0, tiled=True),
        lax.all_gather(fc_in_weight, "fsdp", axis=0, tiled=True),
        lax.all_gather(fc_in_bias, "fsdp", axis=0, tiled=True),
        lax.all_gather(fc_out_weight, "fsdp", axis=0, tiled=True),
        lax.all_gather(fc_out_bias, "fsdp", axis=0, tiled=True),
    )
    keys_back, values_back = (
        lax.all_gather(key_low, "ctx", axis=0, tiled=True),
        lax.all_gather(value_low, "ctx", axis=0, tiled=True),
    )
    grad_out = cotangent.reshape(row_count, model_width)
    grad_wide = grad_out.astype(jnp.float32)
    d_active = dot_right(grad_out, regathered[10])
    d_hidden_low = jax.vjp(gelu_exact, hidden)[1](d_active)[0].astype(jnp.bfloat16)
    d_second = dot_right(d_hidden_low, regathered[8])
    d_mixed_low = (
        dot_right(grad_out, regathered[6]).astype(jnp.bfloat16).reshape(row_count, HEADS, head_dim)
    )
    probs_again = jnp.exp(score_block(keys_back) - log_total)
    probs_again_low = probs_again.astype(jnp.bfloat16)
    grad_probs = jnp.einsum(
        "qhd,khd->hqk",
        d_mixed_low,
        values_back.reshape(seq_length, HEADS, head_dim),
        preferred_element_type=jnp.float32,
    )
    row_delta = jnp.sum(probs_again * grad_probs, axis=-1, keepdims=True)
    grad_scores = (probs_again * (grad_probs - row_delta) * score_scale).astype(jnp.bfloat16)
    d_query = jnp.einsum(
        "hqk,khd->qhd",
        grad_scores,
        keys_back.reshape(seq_length, HEADS, head_dim),
        preferred_element_type=jnp.float32,
    )
    d_key = jnp.einsum(
        "hqk,qhd->khd", grad_scores, query_low, preferred_element_type=jnp.float32
    ).reshape(row_count * lax.axis_size("ctx"), model_width)
    d_value = jnp.einsum(
        "hqk,qhd->khd", probs_again_low, d_mixed_low, preferred_element_type=jnp.float32
    ).reshape(row_count * lax.axis_size("ctx"), model_width)
    kv_grad = lax.psum_scatter(
        jnp.concatenate([d_key, d_value], axis=1).astype(jnp.bfloat16),
        "ctx",
        scatter_dimension=0,
        tiled=True,
    ).astype(jnp.float32)
    d_key_own = kv_grad[:, :model_width].reshape(row_count, HEADS, head_dim)
    d_packed = jnp.concatenate(
        [
            rotate(d_query, cosine, -sine_table).reshape(row_count, model_width),
            rotate(d_key_own, cosine, -sine_table).reshape(row_count, model_width),
            kv_grad[:, model_width:],
        ],
        axis=1,
    )
    d_packed_low = d_packed.astype(jnp.bfloat16)
    d_first = dot_right(d_packed_low, regathered[4])
    norm_back_one = jax.vjp(layer_norm, values, gain_one, shift_one)[1]
    d_values_one, d_gain_one, d_shift_one = norm_back_one(d_first)
    norm_back_two = jax.vjp(layer_norm, values, gain_two, shift_two)[1]
    d_values_two, d_gain_two, d_shift_two = norm_back_two(d_second)
    input_grad = (grad_wide + d_values_one + d_values_two).reshape(tokens.shape)
    grad_sum = jnp.sum(grad_wide, axis=0)
    mlp_grads = reduce_grads(
        dot_left(normed_two, d_hidden_low),
        jnp.sum(d_hidden_low.astype(jnp.float32), axis=0),
        dot_left(active_low, grad_out),
        grad_sum,
        d_gain_two,
        d_shift_two,
    )
    attn_grads = reduce_grads(
        dot_left(normed_one, d_packed_low),
        jnp.sum(d_packed_low.astype(jnp.float32), axis=0),
        dot_left(mixed_low, grad_out),
        grad_sum,
        d_gain_one,
        d_shift_one,
    )
    return (
        output,
        input_grad,
        attn_grads[4],
        attn_grads[5],
        mlp_grads[4],
        mlp_grads[5],
        attn_grads[0],
        attn_grads[1],
        attn_grads[2],
        attn_grads[3],
        mlp_grads[0],
        mlp_grads[1],
        mlp_grads[2],
        mlp_grads[3],
    )


LANES = 128
FAST = pltpu.CompilerParams(vmem_limit_bytes=56 * 1024 * 1024)
SMALL = pl.CostEstimate(flops=1, bytes_accessed=1, transcendentals=0)
ANY = pl.BlockSpec(memory_space=pl.ANY)
SCALARS = pl.BlockSpec(memory_space=pltpu.SMEM)
WHOLE = pl.BlockSpec(memory_space=pltpu.VMEM)
low = jnp.bfloat16
wide = jnp.float32


def dot(a, b, left=1, right=0):
    return lax.dot_general(a, b, (((left,), (right,)), ((), ())), preferred_element_type=wide)


def swap(values, axis, mask):
    return lax.ppermute(values, axis, [(i, i ^ mask) for i in range(lax.axis_size(axis))])


def at(values, index, axis=0):
    return lax.dynamic_index_in_dim(values, index, axis, keepdims=False)


def added(*values):
    total = values[0].astype(wide)
    for v in values[1:]:
        total = total + v.astype(wide)
    return total.astype(low)


def then(value, *events):
    return lax.optimization_barrier((value,) + events)[0]


def gather_plane(first, second):
    first_x, second_y = swap(first, "ctx", 1), swap(second, "ctx", 2)
    first_y, second_x = swap(first, "ctx", 2), swap(second, "ctx", 1)
    first_xy = swap(first_y, "ctx", 1)
    second_xy = swap(second_x, "ctx", 2)
    return [first, first_x, first_y, first_xy], [second, second_x, second_y, second_xy]


def place(pieces, places, count):
    sizes = [p.shape[0] for p in pieces]

    total = sum(sizes)

    def body(places_ref, *refs):
        out, buf, sems_in, sems_out = refs[-4:]
        copies = []
        for ref, size in zip(refs, sizes):
            for i in range(size):
                n = len(copies)
                copies.append(pltpu.make_async_copy(ref.at[i], buf.at[n], sems_in.at[n]))
                copies[n].start()
        leaving = []
        for n in range(total):
            copies[n].wait()
            copy = pltpu.make_async_copy(buf.at[n], out.at[places_ref[n]], sems_out.at[n])
            copy.start()
            leaving.append(copy)
        for copy in leaving:
            copy.wait()

    return pl.pallas_call(
        body,
        name="place",
        out_shape=jax.ShapeDtypeStruct((count,) + pieces[0].shape[1:], pieces[0].dtype),
        in_specs=[SCALARS] + [ANY] * len(pieces),
        out_specs=ANY,
        scratch_shapes=[
            pltpu.VMEM((total,) + pieces[0].shape[1:], pieces[0].dtype),
            pltpu.SemaphoreType.DMA((total,)),
            pltpu.SemaphoreType.DMA((total,)),
        ],
        compiler_params=FAST,
        cost_estimate=SMALL,
    )(places, *pieces)


def cut_weights(qkv_weight, fc_in_weight, extra, places, hd, units, part):
    span = qkv_weight.shape[1] // 3
    cols = 3 * hd + units

    def body(places_ref, qkv_ref, in_ref, extra_ref, *refs):
        outs, buf, sems_in, sems_out = refs[:4], refs[4], refs[5], refs[6]
        row = pl.ds(pl.multiple_of(places_ref[8] * part, part), part)
        copies = []
        for n in range(8):
            f = places_ref[n]
            for t in range(3):
                copies.append(
                    pltpu.make_async_copy(
                        qkv_ref.at[row, pl.ds(pl.multiple_of(t * span + f * hd, LANES), hd)],
                        buf.at[n, :, pl.ds(t * hd, hd)],
                        sems_in.at[len(copies)],
                    )
                )
                copies[-1].start()
            copies.append(
                pltpu.make_async_copy(
                    in_ref.at[row, pl.ds(pl.multiple_of(f * units, LANES), units)],
                    buf.at[n, :, pl.ds(3 * hd, units)],
                    sems_in.at[len(copies)],
                )
            )
            copies[-1].start()
            copies.append(
                pltpu.make_async_copy(
                    extra_ref, buf.at[n, :, pl.ds(cols, LANES)], sems_in.at[len(copies)]
                )
            )
            copies[-1].start()
        leaving = []
        for n in range(8):
            for copy in copies[5 * n : 5 * n + 5]:
                copy.wait()
            copy = pltpu.make_async_copy(buf.at[n], outs[n % 4].at[n // 4], sems_out.at[n])
            copy.start()
            leaving.append(copy)
        for copy in leaving:
            copy.wait()

    return pl.pallas_call(
        body,
        name="cut_weights",
        out_shape=[jax.ShapeDtypeStruct((2, part, cols + LANES), low)] * 4,
        in_specs=[SCALARS, ANY, ANY, ANY],
        out_specs=[ANY] * 4,
        scratch_shapes=[
            pltpu.VMEM((8, part, cols + LANES), low),
            pltpu.SemaphoreType.DMA((40,)),
            pltpu.SemaphoreType.DMA((8,)),
        ],
        compiler_params=FAST,
        cost_estimate=SMALL,
    )(places, qkv_weight, fc_in_weight, extra)


def finish(pieces, rows_at, cols_at, shape, thirds=1, chosen=None):
    begin, size = chosen or (0, pieces[0].shape[0])
    total = size * len(pieces)
    rows, cols = pieces[0].shape[1:]
    span = cols // thirds

    def body(rows_ref, cols_ref, *refs):
        out, narrow, full, sems_in, sems_out = refs[-5:]
        copies = []
        for ref in refs[: len(pieces)]:
            for i in range(begin, begin + size):
                n = len(copies)
                copies.append(pltpu.make_async_copy(ref.at[i], narrow.at[n], sems_in.at[n]))
                copies[n].start()
        leaving = []
        for n in range(total):
            copies[n].wait()
            full[n] = narrow[n].astype(wide)
            row = pl.ds(pl.multiple_of(rows_ref[n] * rows, rows), rows)
            for t in range(thirds):
                start = t * (shape[1] // thirds) + cols_ref[n] * span
                copy = pltpu.make_async_copy(
                    full.at[n, :, pl.ds(t * span, span)],
                    out.at[row, pl.ds(pl.multiple_of(start, LANES), span)],
                    sems_out.at[n * thirds + t],
                )
                copy.start()
                leaving.append(copy)
        for copy in leaving:
            copy.wait()

    return pl.pallas_call(
        body,
        name="finish",
        out_shape=jax.ShapeDtypeStruct(shape, wide),
        in_specs=[SCALARS, SCALARS] + [ANY] * len(pieces),
        out_specs=ANY,
        scratch_shapes=[
            pltpu.VMEM((total, rows, cols), low),
            pltpu.VMEM((total, rows, cols), wide),
            pltpu.SemaphoreType.DMA((total,)),
            pltpu.SemaphoreType.DMA((total * thirds,)),
        ],
        compiler_params=FAST,
        cost_estimate=SMALL,
    )(rows_at, cols_at, *pieces)


def normalised(values):
    centred = values - jnp.mean(values, axis=-1, keepdims=True)
    spread = jnp.mean(centred * centred, axis=-1, keepdims=True)
    rstd = lax.rsqrt(spread + eps_norm)
    return centred * rstd, rstd


def turn_tables(position, rotary):
    cosine, sine = rotary_tables(position, rotary)
    half = rotary // 2
    zero = jnp.zeros((position.shape[0], LANES - rotary), wide)
    none = jnp.zeros_like(sine[:, :half])
    return (
        jnp.concatenate([cosine, zero + 1.0], axis=1),
        jnp.concatenate([-sine[:, :half], none, zero], axis=1),
        jnp.concatenate([none, sine[:, half:], zero], axis=1),
    )


def turn(values, here, above, below, half):
    return (
        values * here
        + pltpu.roll(values, LANES - half, 1) * above
        + pltpu.roll(values, half, 1) * below
    )


def project(x_all, weight, bias, norms, tables, block, hd):
    group, width = x_all.shape
    cols = weight.shape[1]
    half = hd // 8

    def body(x_ref, w_ref, b_ref, n_ref, t0, t1, t2, first_ref, second_ref, out_ref):
        normal, _ = normalised(x_ref[...].astype(wide))
        first = (normal * n_ref[0:1] + n_ref[1:2]).astype(low)
        second_ref[...] = (normal * n_ref[2:3] + n_ref[3:4]).astype(low)
        first_ref[...] = first
        packed = dot(first, w_ref[...]) + b_ref[...]
        for i in range(3):
            lead = packed[:, i * hd : i * hd + LANES]
            if i < 2:
                lead = turn(lead, t0[...], t1[...], t2[...], half)
            out_ref[:, i * hd : i * hd + LANES] = lead.astype(low)
            out_ref[:, i * hd + LANES : (i + 1) * hd] = packed[
                :, i * hd + LANES : (i + 1) * hd
            ].astype(low)

    row = lambda n: pl.BlockSpec((block, n), lambda i: (i, 0))
    return pl.pallas_call(
        body,
        name="project",
        grid=(group // block,),
        in_specs=[row(width), WHOLE, WHOLE, WHOLE, row(LANES), row(LANES), row(LANES)],
        out_specs=[row(width), row(width), row(cols)],
        out_shape=[
            jax.ShapeDtypeStruct((group, width), low),
            jax.ShapeDtypeStruct((group, width), low),
            jax.ShapeDtypeStruct((group, cols), low),
        ],
        compiler_params=FAST,
        cost_estimate=SMALL,
    )(x_all, weight, bias, norms, *tables)


def expand(second, weight, bias, block):
    group, width = second.shape
    cols = weight.shape[1]

    def body(s_ref, w_ref, b_ref, active_ref, slope_ref):
        hidden = dot(s_ref[...], w_ref[...]) + b_ref[...]
        upper = 0.5 * (1.0 + lax.erf(hidden * (0.5**0.5)))
        active_ref[...] = (hidden * upper).astype(low)
        bell = jnp.exp(-0.5 * hidden * hidden) * ((2.0 * jnp.pi) ** -0.5)
        slope_ref[...] = (upper + hidden * bell).astype(low)

    row = lambda n: pl.BlockSpec((block, n), lambda i: (i, 0))
    return pl.pallas_call(
        body,
        name="expand",
        grid=(group // block,),
        in_specs=[row(width), WHOLE, WHOLE],
        out_specs=[row(cols), row(cols)],
        out_shape=[jax.ShapeDtypeStruct((group, cols), low)] * 2,
        compiler_params=FAST,
        cost_estimate=SMALL,
    )(second, weight, bias)


def contract(left, weight, block, more=None):
    group = left.shape[0]
    width = weight.shape[1]

    def body(left_ref, weight_ref, *refs):
        total = dot(left_ref[...], weight_ref[...])
        if more is not None:
            total = total + refs[0][...].astype(wide)
        refs[-1][...] = total.astype(low)

    row = lambda n: pl.BlockSpec((block, n), lambda i: (i, 0))
    return pl.pallas_call(
        body,
        name="contract",
        grid=(group // block,),
        in_specs=[row(left.shape[1]), WHOLE] + ([] if more is None else [row(width)]),
        out_specs=row(width),
        out_shape=jax.ShapeDtypeStruct((group, width), low),
        compiler_params=FAST,
        cost_estimate=SMALL,
    )(left, weight, *(() if more is None else (more,)))


def hidden_back(g_all, fc_out_weight, slope, block):
    group, width = g_all.shape
    units = fc_out_weight.shape[0]

    def body(g_ref, w_ref, s_ref, out_ref, sum_ref):
        @pl.when(pl.program_id(0) == 0)
        def _():
            sum_ref[...] = jnp.zeros_like(sum_ref)

        d_hidden = (dot(g_ref[...], w_ref[...], 1, 1) * s_ref[...].astype(wide)).astype(low)
        out_ref[...] = d_hidden
        sum_ref[...] += jnp.sum(d_hidden.astype(wide), axis=0, keepdims=True)

    row = lambda n: pl.BlockSpec((block, n), lambda i: (i, 0))
    return pl.pallas_call(
        body,
        name="hidden_back",
        grid=(group // block,),
        in_specs=[row(width), WHOLE, row(units)],
        out_specs=[row(units), pl.BlockSpec((1, units), lambda i: (0, 0))],
        out_shape=[
            jax.ShapeDtypeStruct((group, units), low),
            jax.ShapeDtypeStruct((1, units), wide),
        ],
        compiler_params=FAST,
        cost_estimate=SMALL,
    )(g_all, fc_out_weight, slope)


def grad_pair(left, right, keep, send, parts):
    tokens = left.shape[0]
    cols = right.shape[1]
    n = len(keep)
    size = LANES // parts

    def body(keep_ref, send_ref, a_ref, b_ref, right_ref, keep_out, send_out):
        both = jnp.concatenate([a_ref[...], b_ref[...]], axis=1)
        result = dot(both, right_ref[...], 0, 0).astype(low)
        keep_out[...] = result[:LANES].reshape(1, parts, size, cols)
        send_out[...] = result[LANES:].reshape(1, parts, size, cols)

    shape = jax.ShapeDtypeStruct((n, parts, size, cols), low)
    out = pl.BlockSpec((1, parts, size, cols), lambda i, k, s: (i, 0, 0, 0))
    return pl.pallas_call(
        body,
        name="grad_pair",
        grid_spec=pltpu.PrefetchScalarGridSpec(
            num_scalar_prefetch=2,
            grid=(n,),
            in_specs=[
                pl.BlockSpec((tokens, LANES), lambda i, k, s: (0, k[i])),
                pl.BlockSpec((tokens, LANES), lambda i, k, s: (0, s[i])),
                pl.BlockSpec((tokens, cols), lambda i, k, s: (0, 0)),
            ],
            out_specs=[out, out],
        ),
        out_shape=[shape, shape],
        compiler_params=FAST,
        cost_estimate=SMALL,
    )(jnp.stack(keep).astype(jnp.int32), jnp.stack(send).astype(jnp.int32), left, left, right)


def add_split(kept, got, bit):
    n, _, rows, cols = kept.shape

    def body(bit_ref, a_ref, b_ref, keep_out, send_out):
        for out, half in ((keep_out, bit_ref[0]), (send_out, 1 - bit_ref[0])):
            out[...] = (a_ref[:, half].astype(wide) + b_ref[:, half].astype(wide)).astype(low)

    shape = jax.ShapeDtypeStruct((n, rows, cols), low)
    both = pl.BlockSpec((n // 2 if n > 1 else 1, 2, rows, cols), lambda i: (i, 0, 0, 0))
    out = pl.BlockSpec((n // 2 if n > 1 else 1, rows, cols), lambda i: (i, 0, 0))
    return pl.pallas_call(
        body,
        name="add_split",
        grid=(2 if n > 1 else 1,),
        in_specs=[SCALARS, both, both],
        out_specs=[out, out],
        out_shape=[shape, shape],
        compiler_params=FAST,
        cost_estimate=SMALL,
    )(bit[None].astype(jnp.int32), kept, got)


def add_split_two(kept, got, other_kept, other_got, bit):
    n, _, rows, cols = kept.shape
    more = other_kept.shape[3] // cols

    def body(bit_ref, a_ref, b_ref, c_ref, d_ref, keep_out, send_out):
        for out, half in ((keep_out, bit_ref[0]), (send_out, 1 - bit_ref[0])):
            out[:n] = (a_ref[:, half].astype(wide) + b_ref[:, half].astype(wide)).astype(low)
            other = (c_ref[0, half].astype(wide) + d_ref[0, half].astype(wide)).astype(low)
            for i in range(more):
                out[n + i] = other[:, i * cols : (i + 1) * cols]

    shape = jax.ShapeDtypeStruct((n + more, rows, cols), low)
    return pl.pallas_call(
        body,
        name="add_split_two",
        in_specs=[SCALARS] + [WHOLE] * 4,
        out_specs=[WHOLE] * 2,
        out_shape=[shape, shape],
        compiler_params=FAST,
        cost_estimate=SMALL,
    )(bit[None].astype(jnp.int32), kept, got, other_kept, other_got)


def fetch(places_ref, sources, target, sems, block, sequences):
    copies = []
    for m, source in enumerate(sources):
        for s in range(sequences):
            n = len(copies)
            start = pl.multiple_of(places_ref[m] * block, block)
            copies.append(
                pltpu.make_async_copy(source.at[s], target.at[s, pl.ds(start, block)], sems.at[n])
            )
            copies[n].start()
    return copies


def send(places_ref, source, targets, sems):
    copies = [
        pltpu.make_async_copy(source.at[places_ref[m]], target, sems.at[m])
        for m, target in enumerate(targets)
    ]
    for copy in copies:
        copy.start()
    for copy in copies:
        copy.wait()


def block_scores(buf, row_ref, col_ref, s, i, block, hd, scale):
    count = (i + 1) * block
    query = buf[s, i * block : count, 0:hd]
    key = buf[s, 0:count, hd : 2 * hd]
    scores = dot(query, key, 1, 1) * scale
    q_index = lax.broadcasted_iota(jnp.int32, (block, count), 0) + i * block
    k_index = lax.broadcasted_iota(jnp.int32, (block, count), 1)
    allowed = (col_ref[s, i * block : count, :] == row_ref[s, :, 0:count]) & (k_index <= q_index)
    scores = jnp.where(allowed, scores, -1e30)
    probs = jnp.exp(scores - jnp.max(scores, axis=-1, keepdims=True))
    return query, key, probs / jnp.sum(probs, axis=-1, keepdims=True)


def attend(parts, places, seg_row, seg_col, hd):
    count = len(parts)
    sequences, block, cols = parts[0].shape
    scale = hd ** (-0.5)

    def body(places_ref, row_ref, col_ref, *refs):
        outs, (buf, mixed, sems_in, sems_out) = refs[-4 - count : -4], refs[-4:]
        for copy in fetch(places_ref, refs[:count], buf, sems_in, block, sequences):
            copy.wait()
        for s in range(sequences):
            for i in range(count):
                _, _, probs = block_scores(buf, row_ref, col_ref, s, i, block, hd, scale)
                value = buf[s, 0 : (i + 1) * block, 2 * hd : 3 * hd]
                mixed[i, s] = dot(probs.astype(low), value).astype(low)
        send(places_ref, mixed, outs, sems_out)

    return pl.pallas_call(
        body,
        name="attend",
        out_shape=[jax.ShapeDtypeStruct((sequences, block, hd), low)] * count,
        in_specs=[SCALARS, WHOLE, WHOLE] + [ANY] * count,
        out_specs=[ANY] * count,
        scratch_shapes=[
            pltpu.VMEM((sequences, count * block, cols), low),
            pltpu.VMEM((count, sequences, block, hd), low),
            pltpu.SemaphoreType.DMA((count * sequences,)),
            pltpu.SemaphoreType.DMA((count,)),
        ],
        compiler_params=FAST,
        cost_estimate=SMALL,
    )(places, seg_row, seg_col, *parts)


def attend_back(parts, d_parts, places, seg_row, seg_col, tables, hd):
    count = len(parts)
    sequences, block, cols = parts[0].shape
    length = count * block
    scale = hd ** (-0.5)
    half = hd // 8

    def body(places_ref, row_ref, col_ref, t0, t1, t2, *refs):
        outs = refs[2 * count : 3 * count]
        buf, d_buf, key_sum, value_sum, done, sems_in, sems_d, sems_out = refs[3 * count :]
        waits = fetch(places_ref, refs[:count], buf, sems_in, block, sequences)
        waits += fetch(places_ref, refs[count : 2 * count], d_buf, sems_d, block, sequences)
        for copy in waits:
            copy.wait()

        def put(values, s, i, which):
            lead = values[:, 0:LANES]
            if which < 2:
                rows = slice(i * block, (i + 1) * block)
                lead = turn(lead, t0[s, rows], -t1[s, rows], -t2[s, rows], half)
            done[i, s, :, which * hd : which * hd + LANES] = lead.astype(low)
            done[i, s, :, which * hd + LANES : (which + 1) * hd] = values[:, LANES:].astype(low)

        for s in range(sequences):
            for i in reversed(range(count)):
                n = (i + 1) * block
                query, key, probs = block_scores(buf, row_ref, col_ref, s, i, block, hd, scale)
                value = buf[s, 0:n, 2 * hd : 3 * hd]
                d_out = d_buf[s, i * block : n]
                d_probs = dot(d_out, value, 1, 1)
                delta = jnp.sum(probs * d_probs, axis=-1, keepdims=True)
                d_scores = (probs * (d_probs - delta) * scale).astype(low)
                put(dot(d_scores, key), s, i, 0)
                key_part = dot(d_scores, query, 0, 0)
                value_part = dot(probs.astype(low), d_out, 0, 0)
                if i == count - 1:
                    key_sum[...] = key_part
                    value_sum[...] = value_part
                else:
                    key_sum[0:n] += key_part
                    value_sum[0:n] += value_part
                put(key_sum[i * block : n], s, i, 1)
                put(value_sum[i * block : n], s, i, 2)
        send(places_ref, done, outs, sems_out)

    return pl.pallas_call(
        body,
        name="attend_back",
        out_shape=[jax.ShapeDtypeStruct((sequences, block, cols), low)] * count,
        in_specs=[SCALARS] + [WHOLE] * 5 + [ANY] * (2 * count),
        out_specs=[ANY] * count,
        scratch_shapes=[
            pltpu.VMEM((sequences, length, cols), low),
            pltpu.VMEM((sequences, length, hd), low),
            pltpu.VMEM((length, hd), wide),
            pltpu.VMEM((length, hd), wide),
            pltpu.VMEM((count, sequences, block, cols), low),
            pltpu.SemaphoreType.DMA((count * sequences,)),
            pltpu.SemaphoreType.DMA((count * sequences,)),
            pltpu.SemaphoreType.DMA((count,)),
        ],
        compiler_params=FAST,
        cost_estimate=SMALL,
    )(places, seg_row, seg_col, *tables, *parts, *d_parts)


def norm_back(x_all, d_packed, d_hidden, w_qkv, w_in, gains, block):
    group, width = x_all.shape

    def body(x_ref, p_ref, h_ref, w1_ref, w2_ref, g_ref, out_ref, sums_ref):
        @pl.when(pl.program_id(0) == 0)
        def _():
            sums_ref[...] = jnp.zeros_like(sums_ref)

        normal, _ = normalised(x_ref[...].astype(wide))
        one = dot(p_ref[...], w1_ref[...], 1, 1)
        two = dot(h_ref[...], w2_ref[...], 1, 1)
        out_ref[...] = (one * g_ref[0:1] + two * g_ref[2:3]).astype(low)
        sums_ref[0:1] += jnp.sum(one * normal, axis=0, keepdims=True)
        sums_ref[1:2] += jnp.sum(one, axis=0, keepdims=True)
        sums_ref[2:3] += jnp.sum(two * normal, axis=0, keepdims=True)
        sums_ref[3:4] += jnp.sum(two, axis=0, keepdims=True)

    row = lambda n: pl.BlockSpec((block, n), lambda i: (i, 0))
    return pl.pallas_call(
        body,
        name="norm_back",
        grid=(group // block,),
        in_specs=[row(width), row(d_packed.shape[1]), row(d_hidden.shape[1])] + [WHOLE] * 3,
        out_specs=[row(width), pl.BlockSpec((4, width), lambda i: (0, 0))],
        out_shape=[
            jax.ShapeDtypeStruct((group, width), low),
            jax.ShapeDtypeStruct((4, width), wide),
        ],
        compiler_params=FAST,
        cost_estimate=SMALL,
    )(x_all, d_packed, d_hidden, w_qkv, w_in, gains)


def local_by_head(
    tokens,
    segments,
    positions,
    ln1_gain,
    ln1_bias,
    ln2_gain,
    ln2_bias,
    qkv_weight,
    qkv_bias,
    dense_weight,
    dense_bias,
    fc_in_weight,
    fc_in_bias,
    fc_out_weight,
    fc_out_bias,
    cotangent,
):
    width = tokens.shape[-1]
    block = tokens.shape[1]
    nf = lax.axis_size("fsdp")
    nc = lax.axis_size("ctx")
    me_c = lax.axis_index("ctx")
    me_f = lax.axis_index("fsdp")
    hd = width // HEADS
    units = fc_in_weight.shape[1] // nf
    group = nf * block
    length = nc * block
    rows = width // nf
    part = rows // nc
    x_own = tokens.reshape(block, width)
    g_own = cotangent.reshape(block, width)
    order = jnp.array([2 * j + kk for kk in range(2) for j in range(4)], jnp.int32)
    owners = jnp.bitwise_xor(order, me_f)
    plane = jnp.bitwise_xor(jnp.arange(nc, dtype=jnp.int32), me_c)

    ints = jnp.concatenate([segments, positions], axis=0)
    digits = jnp.concatenate([ints // 32, ints % 32]).astype(low)
    vectors = [ln1_gain, ln1_bias, ln2_gain, ln2_bias, qkv_bias, dense_bias, fc_out_bias]
    sizes = [v.shape[0] for v in vectors]
    extra = jnp.concatenate([digits.reshape(-1)] + vectors)
    extra = jnp.pad(extra, (0, part * LANES - extra.shape[0])).reshape(part, LANES)

    pieces = cut_weights(
        qkv_weight,
        fc_in_weight,
        extra,
        jnp.concatenate([owners, me_c[None]]).astype(jnp.int32),
        hd,
        units,
        part,
    )
    got = [pieces[0]] + [swap(pieces[j], "fsdp", 2 * j) for j in (1, 2, 3)]
    x_all = lax.all_gather(then(x_own, *got), "fsdp", axis=0, tiled=True)
    across = swap(jnp.stack([g[1] for g in got]), "fsdp", 1)
    g_all = lax.all_gather(then(g_own, across), "fsdp", axis=0, tiled=True)
    quarter = jnp.concatenate([jnp.stack([g[0] for g in got]), across])
    cols = 3 * hd + units
    qkv_parts, in_parts = gather_plane(quarter[..., : 3 * hd], quarter[..., 3 * hd : cols])

    back = (jnp.arange(nf, dtype=jnp.int32)[:, None] == owners[None, :]).astype(low)
    small = dot(back, quarter[..., cols:].reshape(nf, part * LANES))
    count = 4 * block
    digits = small[:, :count].astype(jnp.int32).reshape(nf, 2, 2, block)
    numbers = digits[:, 0] * 32 + digits[:, 1]
    position_group = numbers[:, 1].reshape(group)
    of_chip = numbers.reshape(4, 2, 2, block)
    seq_ints = [at(of_chip, me_c)] + [swap(at(of_chip, plane[m]), "ctx", m) for m in range(1, nc)]
    seq_ints = jnp.stack(seq_ints, axis=2)
    seq_ints = jnp.stack([at(seq_ints, plane[b], 2) for b in range(nc)], axis=2)
    seq_ints = seq_ints.reshape(2, 2, length)
    seg_row = seq_ints[:, 0][:, None, :]
    seg_col = seq_ints[:, 0][:, :, None]
    tables = turn_tables(position_group, hd // 4)
    seq_tables = [
        t.reshape(2, length, LANES) for t in turn_tables(seq_ints[:, 1].reshape(-1), hd // 4)
    ]
    whole, start = [], count
    for size in sizes:
        whole.append(small[:, start : start + size].reshape(-1))
        start += size
    norms = jnp.stack(whole[:4])
    head_bias = at(whole[4].reshape(3, nf, hd), me_f, 1).reshape(1, -1)

    row_places = (owners[None, :] * nc + plane[:, None]).reshape(-1)
    w_qkv = place(qkv_parts, row_places, nf * nc).reshape(width, 3 * hd)
    w_in = place(in_parts, row_places, nf * nc).reshape(width, units)

    first, second, packed = project(
        then(x_all, w_in), w_qkv, head_bias, norms, tables, block, hd
    )

    def to_sequences(values):
        blocks = values.reshape(4, 2, block, values.shape[1])
        return [
            at(blocks, plane[m]) if m == 0 else swap(at(blocks, plane[m]), "ctx", m)
            for m in range(nc)
        ]

    def to_group(values):
        got = [values[m] if m == 0 else swap(values[m], "ctx", m) for m in range(nc)]
        places = (2 * plane[:, None] + jnp.arange(2, dtype=jnp.int32)[None, :]).reshape(-1)
        return place(got, places, nf).reshape(group, values[0].shape[-1])

    parts = to_sequences(packed)
    active, slope = expand(
        then(second, packed), w_in, fc_in_bias.astype(wide).reshape(1, -1), block
    )
    mlp = contract(active, fc_out_weight, block)
    o = attend([then(p, mlp) for p in parts], plane, seg_row, seg_col, hd)
    o_back = to_group(o)
    x_bit, y_bit = me_c % 2, me_c // 2
    d_o = dot(then(g_all, *o), dense_weight, 1, 1).astype(low)
    d_parts = to_sequences(d_o)
    partial = contract(then(o_back, d_o), dense_weight, block, mlp)
    dense_kept, dense_sent = grad_pair(o_back, then(g_all, partial), [y_bit], [1 - y_bit], 2)
    dense_got = swap(dense_sent, "ctx", 2)
    d_qkv = attend_back(
        parts, [then(p, dense_sent) for p in d_parts], plane, seg_row, seg_col, seq_tables, hd
    )
    d_packed = to_group(d_qkv)
    summed = lax.psum_scatter(then(partial, *d_qkv), "fsdp", scatter_dimension=0, tiled=True)

    rows_of = units // (nc * LANES)
    blocks = [((2 * y) * rows_of, s) for y in range(2) for s in range(rows_of)]
    d_hidden, hidden_sum = hidden_back(then(g_all, *d_qkv), fc_out_weight, slope, block)
    out_kept, out_sent = grad_pair(
        active,
        then(g_all, d_hidden),
        [b + x_bit * rows_of + s for b, s in blocks],
        [b + (1 - x_bit) * rows_of + s for b, s in blocks],
        1,
    )
    out_shape = (1, 2, rows_of * LANES, width)
    out_got = swap(out_sent.reshape(out_shape), "ctx", 1)
    out_kept = out_kept.reshape(out_shape)
    by_y = [2 * f + y_bit for f in range(nf)], [2 * f + 1 - y_bit for f in range(nf)]
    in_kept, in_sent = grad_pair(second, then(d_hidden, out_sent), *by_y, 2)
    in_got = swap(in_sent, "ctx", 2)
    to_x = [2 * f + x_bit for f in range(nf)], [2 * f + 1 - x_bit for f in range(nf)]
    qkv_kept, qkv_sent = grad_pair(first, then(d_packed, in_sent), *to_x, 2)
    qkv_got = swap(qkv_sent, "ctx", 1)
    d_partial, sums = norm_back(
        then(x_all, qkv_sent), d_packed, d_hidden, w_qkv, w_in, norms, block
    )
    def spread_out(values, parts):
        whole = jnp.zeros((parts, nf, values.shape[0] // parts), wide)
        return lax.dynamic_update_slice_in_dim(
            whole, values.reshape(parts, 1, -1), me_f, 1
        ).reshape(nf, -1)

    totals = jnp.concatenate(
        [sums[i].reshape(nf, -1) for i in range(4)]
        + [
            spread_out(jnp.sum(d_packed.astype(wide), axis=0), 3),
            spread_out(hidden_sum[0], 1),
            jnp.sum(g_own.astype(wide), axis=0).reshape(nf, -1),
        ],
        axis=1,
    )
    rows_kept, rows_sent = add_split(out_kept, then(out_got, d_partial), y_bit)
    rows_got = swap(rows_sent, "ctx", 2)
    both_kept, both_sent = add_split_two(
        in_kept, then(in_got, rows_sent), dense_kept, dense_got, x_bit
    )
    both_got = swap(both_sent, "ctx", 1)
    qkv_kept2, qkv_sent2 = add_split(qkv_kept, then(qkv_got, both_sent), y_bit)
    qkv_got2 = swap(qkv_sent2, "ctx", 2)
    d_normal = lax.psum_scatter(
        then(d_partial, summed, qkv_sent2), "fsdp", scatter_dimension=0, tiled=True
    )

    def with_totals(values):
        rest = jnp.pad(totals.astype(low).reshape(nf, -1, values.shape[2]), ((0, 0), (0, 4), (0, 0)))
        return jnp.concatenate([values, rest], axis=1)

    both_got = then(both_got, rows_got, qkv_got2)
    in_mine = added(both_kept, both_got)
    rows_mine = added(rows_kept, then(rows_got, both_got))
    rows_x, rows_y = swap(rows_mine, "ctx", 1), swap(rows_mine, "ctx", 2)
    in_rows = lax.all_to_all(in_mine[:nf], "fsdp", 0, 0, tiled=True)
    qkv_mine = added(qkv_kept2, then(qkv_got2, both_got, rows_x, rows_y))
    qkv_rows = lax.all_to_all(with_totals(qkv_mine), "fsdp", 0, 0, tiled=True)
    rows_xy = swap(rows_y, "ctx", 1)
    in_rows = jnp.concatenate([then(in_rows, rows_x, rows_y), in_mine[nf:]])
    in_x, in_y = swap(in_rows, "ctx", 1), swap(in_rows, "ctx", 2)
    totals = jnp.sum(qkv_rows[:, part:].astype(wide), axis=0).astype(low)
    totals = jnp.pad(totals, ((0, part - totals.shape[0]), (0, 0)))[None]
    qkv_rows = then(jnp.concatenate([qkv_rows[:, :part], totals]), rows_xy, in_y)
    qkv_x, qkv_y = swap(qkv_rows, "ctx", 1), swap(qkv_rows, "ctx", 2)
    in_xy = swap(then(in_x, qkv_rows), "ctx", 2)
    qkv_xy = swap(qkv_y, "ctx", 1)
    rows_all = [rows_mine, rows_x, rows_y, rows_xy]
    in_all = [in_rows, in_x, in_y, in_xy]
    qkv_all = [qkv_rows, qkv_x, qkv_y, qkv_xy]
    by_x = 2 * (plane % 2) + plane // 2

    def whole_columns(pieces, places, shape, thirds, begin=0, count=nf):
        at_rows = (places[:, None] * jnp.ones((count,), jnp.int32)).reshape(-1)
        at_cols = jnp.tile(jnp.arange(count, dtype=jnp.int32), nc)
        return finish(pieces, at_rows, at_cols, shape, thirds, (begin, count))

    grad_fc_out = whole_columns(rows_all, plane, fc_out_weight.shape, 1, 0, 1)
    grad_fc_in = whole_columns(in_all, plane, fc_in_weight.shape, 1)
    grad_dense = whole_columns(in_all, plane, dense_weight.shape, 1, nf, width // units)
    grad_qkv = whole_columns(qkv_all, by_x, qkv_weight.shape, 3)

    x_wide = x_own.astype(wide)
    d_normal = then(d_normal, qkv_x).astype(wide)
    output = (x_wide + summed.astype(wide) + whole[5] + whole[6]).astype(low).reshape(tokens.shape)
    own_normal, own_rstd = normalised(x_wide)
    d_x = own_rstd * (
        d_normal
        - jnp.mean(d_normal, axis=-1, keepdims=True)
        - own_normal * jnp.mean(d_normal * own_normal, axis=-1, keepdims=True)
    )
    input_grad = (g_own.astype(wide) + d_x).reshape(tokens.shape)

    totals = sum(r[-1, :4].astype(wide) for r in qkv_all).reshape(-1)
    cuts, start = [], 0
    for size in (rows, rows, rows, rows, 3 * width // nf, units, rows):
        cuts.append(totals[start : start + size])
        start += size
    return (
        output,
        input_grad,
        cuts[0],
        cuts[1],
        cuts[2],
        cuts[3],
        grad_qkv,
        cuts[4],
        grad_dense,
        cuts[6],
        grad_fc_in,
        cuts[5],
        grad_fc_out,
        cuts[6],
    )


def solution(mesh):
    placed = (
        P("fsdp", "ctx", None),
        P("fsdp", "ctx"),
        P("fsdp", "ctx"),
        P("fsdp"),
        P("fsdp"),
        P("fsdp"),
        P("fsdp"),
        P("fsdp", None),
        P("fsdp"),
        P("fsdp", None),
        P("fsdp"),
        P("fsdp", None),
        P("fsdp"),
        P("fsdp", None),
        P("fsdp"),
        P("fsdp", "ctx", None),
    )
    by_head = mesh.shape["fsdp"] == HEADS and mesh.shape["ctx"] == 4
    return jax.shard_map(
        local_by_head if by_head else local,
        mesh=mesh,
        in_specs=placed,
        out_specs=(
            P("fsdp", "ctx", None),
            P("fsdp", "ctx", None),
            P("fsdp"),
            P("fsdp"),
            P("fsdp"),
            P("fsdp"),
            P("fsdp", None),
            P("fsdp"),
            P("fsdp", None),
            P("fsdp"),
            P("fsdp", None),
            P("fsdp"),
            P("fsdp", None),
            P("fsdp"),
        ),
        check_vma=False,
    )
```

```python
import jax
import jax.numpy as jnp
from jax import lax
from jax.experimental import pallas as pl
from jax.experimental.pallas import tpu as pltpu
from jax.sharding import PartitionSpec as P

HEADS = 8


eps_norm = 1e-05


def layer_norm(values, gain_vec, shift_vec):
    row_mean = jnp.mean(values, axis=-1, keepdims=True)
    centred = values - row_mean
    spread = jnp.mean(centred * centred, axis=-1, keepdims=True)
    return centred * lax.rsqrt(spread + eps_norm) * gain_vec + shift_vec


def rotary_tables(position, rotary):
    frequency = 10000.0 ** (-jnp.arange(0, rotary, 2, dtype=jnp.float32) / rotary)
    angles = position.astype(jnp.float32)[:, None] * frequency[None, :]
    angles = jnp.concatenate([angles, angles], axis=-1)
    return (jnp.cos(angles), jnp.sin(angles))


def rotate(values, cosine, sine_table):
    rotary = cosine.shape[-1]
    half_rot = rotary // 2
    turned = jnp.concatenate([-values[..., half_rot:rotary], values[..., :half_rot]], axis=-1)
    rotated_head = values[..., :rotary] * cosine[:, None, :] + turned * sine_table[:, None, :]
    return jnp.concatenate([rotated_head, values[..., rotary:]], axis=-1)


def gelu_exact(tensor):
    return jax.nn.gelu(tensor, approximate=False)


def dot_right(left_side, right_side):
    return lax.dot_general(
        left_side, right_side, (((1,), (1,)), ((), ())), preferred_element_type=jnp.float32
    )


def dot_left(left_side, right_side):
    return lax.dot_general(
        left_side, right_side, (((0,), (0,)), ((), ())), preferred_element_type=jnp.float32
    )


def reduce_grads(weight_one, bias_one, weight_two, bias_two, gain_grad, shift_grad):
    shared = (
        lax.psum_scatter(
            weight_one.astype(jnp.bfloat16), "fsdp", scatter_dimension=0, tiled=True
        ).astype(jnp.float32),
        lax.psum_scatter(
            bias_one.astype(jnp.bfloat16), "fsdp", scatter_dimension=0, tiled=True
        ).astype(jnp.float32),
        lax.psum_scatter(
            weight_two.astype(jnp.bfloat16), "fsdp", scatter_dimension=0, tiled=True
        ).astype(jnp.float32),
        lax.psum_scatter(
            bias_two.astype(jnp.bfloat16), "fsdp", scatter_dimension=0, tiled=True
        ).astype(jnp.float32),
        lax.psum_scatter(
            gain_grad.astype(jnp.bfloat16), "fsdp", scatter_dimension=0, tiled=True
        ).astype(jnp.float32),
        lax.psum_scatter(
            shift_grad.astype(jnp.bfloat16), "fsdp", scatter_dimension=0, tiled=True
        ).astype(jnp.float32),
    )
    return (
        lax.psum(shared[0].astype(jnp.bfloat16), "ctx").astype(jnp.float32),
        lax.psum(shared[1].astype(jnp.bfloat16), "ctx").astype(jnp.float32),
        lax.psum(shared[2].astype(jnp.bfloat16), "ctx").astype(jnp.float32),
        lax.psum(shared[3].astype(jnp.bfloat16), "ctx").astype(jnp.float32),
        lax.psum(shared[4].astype(jnp.bfloat16), "ctx").astype(jnp.float32),
        lax.psum(shared[5].astype(jnp.bfloat16), "ctx").astype(jnp.float32),
    )


def local(
    tokens,
    segments,
    positions,
    ln1_gain,
    ln1_bias,
    ln2_gain,
    ln2_bias,
    qkv_weight,
    qkv_bias,
    dense_weight,
    dense_bias,
    fc_in_weight,
    fc_in_bias,
    fc_out_weight,
    fc_out_bias,
    cotangent,
):
    model_width = tokens.shape[-1]
    values = tokens.reshape(-1, model_width).astype(jnp.float32)
    row_count = values.shape[0]
    head_dim = model_width // HEADS
    score_scale = head_dim ** (-0.5)
    everyone = lax.all_gather(segments, "ctx", axis=1, tiled=True).reshape(-1)
    seq_length = everyone.shape[0]
    own_segment = segments.reshape(-1)
    query_index = lax.axis_index("ctx") * row_count + jnp.arange(row_count, dtype=jnp.int32)
    key_index = jnp.arange(seq_length, dtype=jnp.int32)
    allowed = (own_segment[:, None] == everyone[None, :]) & (
        key_index[None, :] <= query_index[:, None]
    )
    cosine, sine_table = rotary_tables(positions.reshape(-1), head_dim // 4)
    gathered = (
        lax.all_gather(ln1_gain, "fsdp", axis=0, tiled=True),
        lax.all_gather(ln1_bias, "fsdp", axis=0, tiled=True),
        lax.all_gather(ln2_gain, "fsdp", axis=0, tiled=True),
        lax.all_gather(ln2_bias, "fsdp", axis=0, tiled=True),
        lax.all_gather(qkv_weight, "fsdp", axis=0, tiled=True),
        lax.all_gather(qkv_bias, "fsdp", axis=0, tiled=True),
        lax.all_gather(dense_weight, "fsdp", axis=0, tiled=True),
        lax.all_gather(dense_bias, "fsdp", axis=0, tiled=True),
        lax.all_gather(fc_in_weight, "fsdp", axis=0, tiled=True),
        lax.all_gather(fc_in_bias, "fsdp", axis=0, tiled=True),
        lax.all_gather(fc_out_weight, "fsdp", axis=0, tiled=True),
        lax.all_gather(fc_out_bias, "fsdp", axis=0, tiled=True),
    )
    gain_one = gathered[0].astype(jnp.float32)
    shift_one = gathered[1].astype(jnp.float32)
    gain_two = gathered[2].astype(jnp.float32)
    shift_two = gathered[3].astype(jnp.float32)
    normed_one = layer_norm(values, gain_one, shift_one).astype(jnp.bfloat16)
    normed_two = layer_norm(values, gain_two, shift_two).astype(jnp.bfloat16)
    packed = jnp.dot(normed_one, gathered[4], preferred_element_type=jnp.float32) + gathered[
        5
    ].astype(jnp.float32)
    shaped = packed.reshape(row_count, 3, HEADS, head_dim)
    query_low = rotate(shaped[:, 0], cosine, sine_table).astype(jnp.bfloat16)
    key_low = (
        rotate(shaped[:, 1], cosine, sine_table)
        .astype(jnp.bfloat16)
        .reshape(row_count, model_width)
    )
    value_low = shaped[:, 2].astype(jnp.bfloat16).reshape(row_count, model_width)
    keys_all, values_all = (
        lax.all_gather(key_low, "ctx", axis=0, tiled=True),
        lax.all_gather(value_low, "ctx", axis=0, tiled=True),
    )

    def score_block(key_rows):
        raw_scores = jnp.einsum(
            "qhd,khd->hqk",
            query_low,
            key_rows.reshape(seq_length, HEADS, head_dim),
            preferred_element_type=jnp.float32,
        )
        return jnp.where(allowed[None], raw_scores * score_scale, -1e30)

    scores = score_block(keys_all)
    row_max = jnp.max(scores, axis=-1, keepdims=True)
    exp_scores = jnp.exp(scores - row_max)
    row_total = jnp.sum(exp_scores, axis=-1, keepdims=True)
    probs_low = (exp_scores / row_total).astype(jnp.bfloat16)
    log_total = row_max + jnp.log(row_total)
    mixed_heads = jnp.einsum(
        "hqk,khd->qhd",
        probs_low,
        values_all.reshape(seq_length, HEADS, head_dim),
        preferred_element_type=jnp.float32,
    )
    mixed_low = mixed_heads.reshape(row_count, model_width).astype(jnp.bfloat16)
    attn_out = jnp.dot(mixed_low, gathered[6], preferred_element_type=jnp.float32) + gathered[
        7
    ].astype(jnp.float32)
    hidden = jnp.dot(normed_two, gathered[8], preferred_element_type=jnp.float32) + gathered[
        9
    ].astype(jnp.float32)
    active_low = gelu_exact(hidden).astype(jnp.bfloat16)
    mlp_out = jnp.dot(active_low, gathered[10], preferred_element_type=jnp.float32) + gathered[
        11
    ].astype(jnp.float32)
    output = (values + attn_out + mlp_out).astype(jnp.bfloat16).reshape(tokens.shape)
    regathered = (
        lax.all_gather(ln1_gain, "fsdp", axis=0, tiled=True),
        lax.all_gather(ln1_bias, "fsdp", axis=0, tiled=True),
        lax.all_gather(ln2_gain, "fsdp", axis=0, tiled=True),
        lax.all_gather(ln2_bias, "fsdp", axis=0, tiled=True),
        lax.all_gather(qkv_weight, "fsdp", axis=0, tiled=True),
        lax.all_gather(qkv_bias, "fsdp", axis=0, tiled=True),
        lax.all_gather(dense_weight, "fsdp", axis=0, tiled=True),
        lax.all_gather(dense_bias, "fsdp", axis=0, tiled=True),
        lax.all_gather(fc_in_weight, "fsdp", axis=0, tiled=True),
        lax.all_gather(fc_in_bias, "fsdp", axis=0, tiled=True),
        lax.all_gather(fc_out_weight, "fsdp", axis=0, tiled=True),
        lax.all_gather(fc_out_bias, "fsdp", axis=0, tiled=True),
    )
    keys_back, values_back = (
        lax.all_gather(key_low, "ctx", axis=0, tiled=True),
        lax.all_gather(value_low, "ctx", axis=0, tiled=True),
    )
    grad_out = cotangent.reshape(row_count, model_width)
    grad_wide = grad_out.astype(jnp.float32)
    d_active = dot_right(grad_out, regathered[10])
    d_hidden_low = jax.vjp(gelu_exact, hidden)[1](d_active)[0].astype(jnp.bfloat16)
    d_second = dot_right(d_hidden_low, regathered[8])
    d_mixed_low = (
        dot_right(grad_out, regathered[6]).astype(jnp.bfloat16).reshape(row_count, HEADS, head_dim)
    )
    probs_again = jnp.exp(score_block(keys_back) - log_total)
    probs_again_low = probs_again.astype(jnp.bfloat16)
    grad_probs = jnp.einsum(
        "qhd,khd->hqk",
        d_mixed_low,
        values_back.reshape(seq_length, HEADS, head_dim),
        preferred_element_type=jnp.float32,
    )
    row_delta = jnp.sum(probs_again * grad_probs, axis=-1, keepdims=True)
    grad_scores = (probs_again * (grad_probs - row_delta) * score_scale).astype(jnp.bfloat16)
    d_query = jnp.einsum(
        "hqk,khd->qhd",
        grad_scores,
        keys_back.reshape(seq_length, HEADS, head_dim),
        preferred_element_type=jnp.float32,
    )
    d_key = jnp.einsum(
        "hqk,qhd->khd", grad_scores, query_low, preferred_element_type=jnp.float32
    ).reshape(row_count * lax.axis_size("ctx"), model_width)
    d_value = jnp.einsum(
        "hqk,qhd->khd", probs_again_low, d_mixed_low, preferred_element_type=jnp.float32
    ).reshape(row_count * lax.axis_size("ctx"), model_width)
    kv_grad = lax.psum_scatter(
        jnp.concatenate([d_key, d_value], axis=1).astype(jnp.bfloat16),
        "ctx",
        scatter_dimension=0,
        tiled=True,
    ).astype(jnp.float32)
    d_key_own = kv_grad[:, :model_width].reshape(row_count, HEADS, head_dim)
    d_packed = jnp.concatenate(
        [
            rotate(d_query, cosine, -sine_table).reshape(row_count, model_width),
            rotate(d_key_own, cosine, -sine_table).reshape(row_count, model_width),
            kv_grad[:, model_width:],
        ],
        axis=1,
    )
    d_packed_low = d_packed.astype(jnp.bfloat16)
    d_first = dot_right(d_packed_low, regathered[4])
    norm_back_one = jax.vjp(layer_norm, values, gain_one, shift_one)[1]
    d_values_one, d_gain_one, d_shift_one = norm_back_one(d_first)
    norm_back_two = jax.vjp(layer_norm, values, gain_two, shift_two)[1]
    d_values_two, d_gain_two, d_shift_two = norm_back_two(d_second)
    input_grad = (grad_wide + d_values_one + d_values_two).reshape(tokens.shape)
    grad_sum = jnp.sum(grad_wide, axis=0)
    mlp_grads = reduce_grads(
        dot_left(normed_two, d_hidden_low),
        jnp.sum(d_hidden_low.astype(jnp.float32), axis=0),
        dot_left(active_low, grad_out),
        grad_sum,
        d_gain_two,
        d_shift_two,
    )
    attn_grads = reduce_grads(
        dot_left(normed_one, d_packed_low),
        jnp.sum(d_packed_low.astype(jnp.float32), axis=0),
        dot_left(mixed_low, grad_out),
        grad_sum,
        d_gain_one,
        d_shift_one,
    )
    return (
        output,
        input_grad,
        attn_grads[4],
        attn_grads[5],
        mlp_grads[4],
        mlp_grads[5],
        attn_grads[0],
        attn_grads[1],
        attn_grads[2],
        attn_grads[3],
        mlp_grads[0],
        mlp_grads[1],
        mlp_grads[2],
        mlp_grads[3],
    )


LANES = 128
FAST = pltpu.CompilerParams(vmem_limit_bytes=56 * 1024 * 1024)
SMALL = pl.CostEstimate(flops=1, bytes_accessed=1, transcendentals=0)
ANY = pl.BlockSpec(memory_space=pl.ANY)
SCALARS = pl.BlockSpec(memory_space=pltpu.SMEM)
WHOLE = pl.BlockSpec(memory_space=pltpu.VMEM)
low = jnp.bfloat16
wide = jnp.float32


def dot(a, b, left=1, right=0):
    return lax.dot_general(a, b, (((left,), (right,)), ((), ())), preferred_element_type=wide)


def swap(values, axis, mask):
    return lax.ppermute(values, axis, [(i, i ^ mask) for i in range(lax.axis_size(axis))])


def at(values, index, axis=0):
    return lax.dynamic_index_in_dim(values, index, axis, keepdims=False)


def added(*values):
    total = values[0].astype(wide)
    for v in values[1:]:
        total = total + v.astype(wide)
    return total.astype(low)


def then(value, *events):
    return lax.optimization_barrier((value,) + events)[0]


def gather_plane(first, second):
    first_x, second_y = swap(first, "ctx", 1), swap(second, "ctx", 2)
    first_y, second_x = swap(first, "ctx", 2), swap(second, "ctx", 1)
    first_xy = swap(first_y, "ctx", 1)
    second_xy = swap(second_x, "ctx", 2)
    return [first, first_x, first_y, first_xy], [second, second_x, second_y, second_xy]


def place(pieces, places, count):
    sizes = [p.shape[0] for p in pieces]

    total = sum(sizes)

    def body(places_ref, *refs):
        out, buf, sems_in, sems_out = refs[-4:]
        copies = []
        for ref, size in zip(refs, sizes):
            for i in range(size):
                n = len(copies)
                copies.append(pltpu.make_async_copy(ref.at[i], buf.at[n], sems_in.at[n]))
                copies[n].start()
        leaving = []
        for n in range(total):
            copies[n].wait()
            copy = pltpu.make_async_copy(buf.at[n], out.at[places_ref[n]], sems_out.at[n])
            copy.start()
            leaving.append(copy)
        for copy in leaving:
            copy.wait()

    return pl.pallas_call(
        body,
        name="place",
        out_shape=jax.ShapeDtypeStruct((count,) + pieces[0].shape[1:], pieces[0].dtype),
        in_specs=[SCALARS] + [ANY] * len(pieces),
        out_specs=ANY,
        scratch_shapes=[
            pltpu.VMEM((total,) + pieces[0].shape[1:], pieces[0].dtype),
            pltpu.SemaphoreType.DMA((total,)),
            pltpu.SemaphoreType.DMA((total,)),
        ],
        compiler_params=FAST,
        cost_estimate=SMALL,
    )(places, *pieces)


def cut_weights(qkv_weight, fc_in_weight, extra, places, hd, units, part):
    span = qkv_weight.shape[1] // 3
    cols = 3 * hd + units

    def body(places_ref, qkv_ref, in_ref, extra_ref, *refs):
        outs, buf, sems_in, sems_out = refs[:4], refs[4], refs[5], refs[6]
        row = pl.ds(pl.multiple_of(places_ref[8] * part, part), part)
        copies = []
        for n in range(8):
            f = places_ref[n]
            for t in range(3):
                copies.append(
                    pltpu.make_async_copy(
                        qkv_ref.at[row, pl.ds(pl.multiple_of(t * span + f * hd, LANES), hd)],
                        buf.at[n, :, pl.ds(t * hd, hd)],
                        sems_in.at[len(copies)],
                    )
                )
                copies[-1].start()
            copies.append(
                pltpu.make_async_copy(
                    in_ref.at[row, pl.ds(pl.multiple_of(f * units, LANES), units)],
                    buf.at[n, :, pl.ds(3 * hd, units)],
                    sems_in.at[len(copies)],
                )
            )
            copies[-1].start()
            copies.append(
                pltpu.make_async_copy(
                    extra_ref, buf.at[n, :, pl.ds(cols, LANES)], sems_in.at[len(copies)]
                )
            )
            copies[-1].start()
        leaving = []
        for n in range(8):
            for copy in copies[5 * n : 5 * n + 5]:
                copy.wait()
            copy = pltpu.make_async_copy(buf.at[n], outs[n % 4].at[n // 4], sems_out.at[n])
            copy.start()
            leaving.append(copy)
        for copy in leaving:
            copy.wait()

    return pl.pallas_call(
        body,
        name="cut_weights",
        out_shape=[jax.ShapeDtypeStruct((2, part, cols + LANES), low)] * 4,
        in_specs=[SCALARS, ANY, ANY, ANY],
        out_specs=[ANY] * 4,
        scratch_shapes=[
            pltpu.VMEM((8, part, cols + LANES), low),
            pltpu.SemaphoreType.DMA((40,)),
            pltpu.SemaphoreType.DMA((8,)),
        ],
        compiler_params=FAST,
        cost_estimate=SMALL,
    )(places, qkv_weight, fc_in_weight, extra)


def finish(pieces, rows_at, cols_at, shape, thirds=1, chosen=None):
    begin, size = chosen or (0, pieces[0].shape[0])
    total = size * len(pieces)
    rows, cols = pieces[0].shape[1:]
    span = cols // thirds

    def body(rows_ref, cols_ref, *refs):
        out, narrow, full, sems_in, sems_out = refs[-5:]
        copies = []
        for ref in refs[: len(pieces)]:
            for i in range(begin, begin + size):
                n = len(copies)
                copies.append(pltpu.make_async_copy(ref.at[i], narrow.at[n], sems_in.at[n]))
                copies[n].start()
        leaving = []
        for n in range(total):
            copies[n].wait()
            full[n] = narrow[n].astype(wide)
            row = pl.ds(pl.multiple_of(rows_ref[n] * rows, rows), rows)
            for t in range(thirds):
                start = t * (shape[1] // thirds) + cols_ref[n] * span
                copy = pltpu.make_async_copy(
                    full.at[n, :, pl.ds(t * span, span)],
                    out.at[row, pl.ds(pl.multiple_of(start, LANES), span)],
                    sems_out.at[n * thirds + t],
                )
                copy.start()
                leaving.append(copy)
        for copy in leaving:
            copy.wait()

    return pl.pallas_call(
        body,
        name="finish",
        out_shape=jax.ShapeDtypeStruct(shape, wide),
        in_specs=[SCALARS, SCALARS] + [ANY] * len(pieces),
        out_specs=ANY,
        scratch_shapes=[
            pltpu.VMEM((total, rows, cols), low),
            pltpu.VMEM((total, rows, cols), wide),
            pltpu.SemaphoreType.DMA((total,)),
            pltpu.SemaphoreType.DMA((total * thirds,)),
        ],
        compiler_params=FAST,
        cost_estimate=SMALL,
    )(rows_at, cols_at, *pieces)


def normalised(values):
    centred = values - jnp.mean(values, axis=-1, keepdims=True)
    spread = jnp.mean(centred * centred, axis=-1, keepdims=True)
    rstd = lax.rsqrt(spread + eps_norm)
    return centred * rstd, rstd


def turn_tables(position, rotary):
    cosine, sine = rotary_tables(position, rotary)
    half = rotary // 2
    zero = jnp.zeros((position.shape[0], LANES - rotary), wide)
    none = jnp.zeros_like(sine[:, :half])
    return (
        jnp.concatenate([cosine, zero + 1.0], axis=1),
        jnp.concatenate([-sine[:, :half], none, zero], axis=1),
        jnp.concatenate([none, sine[:, half:], zero], axis=1),
    )


def turn(values, here, above, below, half):
    return (
        values * here
        + pltpu.roll(values, LANES - half, 1) * above
        + pltpu.roll(values, half, 1) * below
    )


def project(x_all, weight, bias, norms, tables, block, hd):
    group, width = x_all.shape
    cols = weight.shape[1]
    half = hd // 8

    def body(x_ref, w_ref, b_ref, n_ref, t0, t1, t2, first_ref, second_ref, out_ref):
        normal, _ = normalised(x_ref[...].astype(wide))
        first = (normal * n_ref[0:1] + n_ref[1:2]).astype(low)
        second_ref[...] = (normal * n_ref[2:3] + n_ref[3:4]).astype(low)
        first_ref[...] = first
        packed = dot(first, w_ref[...]) + b_ref[...]
        for i in range(3):
            lead = packed[:, i * hd : i * hd + LANES]
            if i < 2:
                lead = turn(lead, t0[...], t1[...], t2[...], half)
            out_ref[:, i * hd : i * hd + LANES] = lead.astype(low)
            out_ref[:, i * hd + LANES : (i + 1) * hd] = packed[
                :, i * hd + LANES : (i + 1) * hd
            ].astype(low)

    row = lambda n: pl.BlockSpec((block, n), lambda i: (i, 0))
    return pl.pallas_call(
        body,
        name="project",
        grid=(group // block,),
        in_specs=[row(width), WHOLE, WHOLE, WHOLE, row(LANES), row(LANES), row(LANES)],
        out_specs=[row(width), row(width), row(cols)],
        out_shape=[
            jax.ShapeDtypeStruct((group, width), low),
            jax.ShapeDtypeStruct((group, width), low),
            jax.ShapeDtypeStruct((group, cols), low),
        ],
        compiler_params=FAST,
        cost_estimate=SMALL,
    )(x_all, weight, bias, norms, *tables)


def expand(second, weight, bias, block):
    group, width = second.shape
    cols = weight.shape[1]

    def body(s_ref, w_ref, b_ref, active_ref, slope_ref):
        hidden = dot(s_ref[...], w_ref[...]) + b_ref[...]
        upper = 0.5 * (1.0 + lax.erf(hidden * (0.5**0.5)))
        active_ref[...] = (hidden * upper).astype(low)
        bell = jnp.exp(-0.5 * hidden * hidden) * ((2.0 * jnp.pi) ** -0.5)
        slope_ref[...] = (upper + hidden * bell).astype(low)

    row = lambda n: pl.BlockSpec((block, n), lambda i: (i, 0))
    return pl.pallas_call(
        body,
        name="expand",
        grid=(group // block,),
        in_specs=[row(width), WHOLE, WHOLE],
        out_specs=[row(cols), row(cols)],
        out_shape=[jax.ShapeDtypeStruct((group, cols), low)] * 2,
        compiler_params=FAST,
        cost_estimate=SMALL,
    )(second, weight, bias)


def contract(left, weight, block, more=None):
    group = left.shape[0]
    width = weight.shape[1]

    def body(left_ref, weight_ref, *refs):
        total = dot(left_ref[...], weight_ref[...])
        if more is not None:
            total = total + refs[0][...].astype(wide)
        refs[-1][...] = total.astype(low)

    row = lambda n: pl.BlockSpec((block, n), lambda i: (i, 0))
    return pl.pallas_call(
        body,
        name="contract",
        grid=(group // block,),
        in_specs=[row(left.shape[1]), WHOLE] + ([] if more is None else [row(width)]),
        out_specs=row(width),
        out_shape=jax.ShapeDtypeStruct((group, width), low),
        compiler_params=FAST,
        cost_estimate=SMALL,
    )(left, weight, *(() if more is None else (more,)))


def hidden_back(g_all, fc_out_weight, slope, block):
    group, width = g_all.shape
    units = fc_out_weight.shape[0]

    def body(g_ref, w_ref, s_ref, out_ref, sum_ref):
        @pl.when(pl.program_id(0) == 0)
        def _():
            sum_ref[...] = jnp.zeros_like(sum_ref)

        d_hidden = (dot(g_ref[...], w_ref[...], 1, 1) * s_ref[...].astype(wide)).astype(low)
        out_ref[...] = d_hidden
        sum_ref[...] += jnp.sum(d_hidden.astype(wide), axis=0, keepdims=True)

    row = lambda n: pl.BlockSpec((block, n), lambda i: (i, 0))
    return pl.pallas_call(
        body,
        name="hidden_back",
        grid=(group // block,),
        in_specs=[row(width), WHOLE, row(units)],
        out_specs=[row(units), pl.BlockSpec((1, units), lambda i: (0, 0))],
        out_shape=[
            jax.ShapeDtypeStruct((group, units), low),
            jax.ShapeDtypeStruct((1, units), wide),
        ],
        compiler_params=FAST,
        cost_estimate=SMALL,
    )(g_all, fc_out_weight, slope)


def grad_pair(left, right, keep, send, parts):
    tokens = left.shape[0]
    cols = right.shape[1]
    n = len(keep)
    size = LANES // parts

    def body(keep_ref, send_ref, a_ref, b_ref, right_ref, keep_out, send_out):
        both = jnp.concatenate([a_ref[...], b_ref[...]], axis=1)
        result = dot(both, right_ref[...], 0, 0).astype(low)
        keep_out[...] = result[:LANES].reshape(1, parts, size, cols)
        send_out[...] = result[LANES:].reshape(1, parts, size, cols)

    shape = jax.ShapeDtypeStruct((n, parts, size, cols), low)
    out = pl.BlockSpec((1, parts, size, cols), lambda i, k, s: (i, 0, 0, 0))
    return pl.pallas_call(
        body,
        name="grad_pair",
        grid_spec=pltpu.PrefetchScalarGridSpec(
            num_scalar_prefetch=2,
            grid=(n,),
            in_specs=[
                pl.BlockSpec((tokens, LANES), lambda i, k, s: (0, k[i])),
                pl.BlockSpec((tokens, LANES), lambda i, k, s: (0, s[i])),
                pl.BlockSpec((tokens, cols), lambda i, k, s: (0, 0)),
            ],
            out_specs=[out, out],
        ),
        out_shape=[shape, shape],
        compiler_params=FAST,
        cost_estimate=SMALL,
    )(jnp.stack(keep).astype(jnp.int32), jnp.stack(send).astype(jnp.int32), left, left, right)


def add_split(kept, got, bit):
    n, _, rows, cols = kept.shape

    def body(bit_ref, a_ref, b_ref, keep_out, send_out):
        for out, half in ((keep_out, bit_ref[0]), (send_out, 1 - bit_ref[0])):
            out[...] = (a_ref[:, half].astype(wide) + b_ref[:, half].astype(wide)).astype(low)

    shape = jax.ShapeDtypeStruct((n, rows, cols), low)
    both = pl.BlockSpec((n // 2 if n > 1 else 1, 2, rows, cols), lambda i: (i, 0, 0, 0))
    out = pl.BlockSpec((n // 2 if n > 1 else 1, rows, cols), lambda i: (i, 0, 0))
    return pl.pallas_call(
        body,
        name="add_split",
        grid=(2 if n > 1 else 1,),
        in_specs=[SCALARS, both, both],
        out_specs=[out, out],
        out_shape=[shape, shape],
        compiler_params=FAST,
        cost_estimate=SMALL,
    )(bit[None].astype(jnp.int32), kept, got)


def add_split_two(kept, got, other_kept, other_got, bit):
    n, _, rows, cols = kept.shape
    more = other_kept.shape[3] // cols

    def body(bit_ref, a_ref, b_ref, c_ref, d_ref, keep_out, send_out):
        for out, half in ((keep_out, bit_ref[0]), (send_out, 1 - bit_ref[0])):
            out[:n] = (a_ref[:, half].astype(wide) + b_ref[:, half].astype(wide)).astype(low)
            other = (c_ref[0, half].astype(wide) + d_ref[0, half].astype(wide)).astype(low)
            for i in range(more):
                out[n + i] = other[:, i * cols : (i + 1) * cols]

    shape = jax.ShapeDtypeStruct((n + more, rows, cols), low)
    return pl.pallas_call(
        body,
        name="add_split_two",
        in_specs=[SCALARS] + [WHOLE] * 4,
        out_specs=[WHOLE] * 2,
        out_shape=[shape, shape],
        compiler_params=FAST,
        cost_estimate=SMALL,
    )(bit[None].astype(jnp.int32), kept, got, other_kept, other_got)


def fetch(source, target, sems):
    count, sequences, block, _ = source.shape
    copies = []
    for m in range(count):
        for s in range(sequences):
            n = len(copies)
            copies.append(
                pltpu.make_async_copy(
                    source.at[m, s], target.at[s, pl.ds(m * block, block)], sems.at[n]
                )
            )
            copies[n].start()
    return copies


def block_scores(buf, row_ref, col_ref, s, i, block, hd, scale):
    count = (i + 1) * block
    query = buf[s, i * block : count, 0:hd]
    key = buf[s, 0:count, hd : 2 * hd]
    scores = dot(query, key, 1, 1) * scale
    q_index = lax.broadcasted_iota(jnp.int32, (block, count), 0) + i * block
    k_index = lax.broadcasted_iota(jnp.int32, (block, count), 1)
    allowed = (col_ref[s, i * block : count, :] == row_ref[s, :, 0:count]) & (k_index <= q_index)
    scores = jnp.where(allowed, scores, -1e30)
    probs = jnp.exp(scores - jnp.max(scores, axis=-1, keepdims=True))
    return query, key, probs / jnp.sum(probs, axis=-1, keepdims=True)


def attend(parts, seg_row, seg_col, hd):
    count, sequences, block, cols = parts.shape
    scale = hd ** (-0.5)

    def body(row_ref, col_ref, parts_ref, out, buf, mixed, sems_in, sem_out):
        for copy in fetch(parts_ref, buf, sems_in):
            copy.wait()
        for s in range(sequences):
            for i in range(count):
                _, _, probs = block_scores(buf, row_ref, col_ref, s, i, block, hd, scale)
                value = buf[s, 0 : (i + 1) * block, 2 * hd : 3 * hd]
                mixed[i, s] = dot(probs.astype(low), value).astype(low)
        copy = pltpu.make_async_copy(mixed, out, sem_out)
        copy.start()
        copy.wait()

    return pl.pallas_call(
        body,
        name="attend",
        out_shape=jax.ShapeDtypeStruct((count, sequences, block, hd), low),
        in_specs=[WHOLE, WHOLE, ANY],
        out_specs=ANY,
        scratch_shapes=[
            pltpu.VMEM((sequences, count * block, cols), low),
            pltpu.VMEM((count, sequences, block, hd), low),
            pltpu.SemaphoreType.DMA((count * sequences,)),
            pltpu.SemaphoreType.DMA,
        ],
        compiler_params=FAST,
        cost_estimate=SMALL,
    )(seg_row, seg_col, parts)


def attend_back(parts, d_parts, seg_row, seg_col, tables, hd):
    count, sequences, block, cols = parts.shape
    length = count * block
    scale = hd ** (-0.5)
    half = hd // 8

    def body(row_ref, col_ref, t0, t1, t2, parts_ref, d_ref, out, *scratch):
        buf, d_buf, key_sum, value_sum, done, sems_in, sems_d, sem_out = scratch
        for copy in fetch(parts_ref, buf, sems_in) + fetch(d_ref, d_buf, sems_d):
            copy.wait()

        def put(values, s, i, which):
            lead = values[:, 0:LANES]
            if which < 2:
                rows = slice(i * block, (i + 1) * block)
                lead = turn(lead, t0[s, rows], -t1[s, rows], -t2[s, rows], half)
            done[i, s, :, which * hd : which * hd + LANES] = lead.astype(low)
            done[i, s, :, which * hd + LANES : (which + 1) * hd] = values[:, LANES:].astype(low)

        for s in range(sequences):
            for i in reversed(range(count)):
                n = (i + 1) * block
                query, key, probs = block_scores(buf, row_ref, col_ref, s, i, block, hd, scale)
                value = buf[s, 0:n, 2 * hd : 3 * hd]
                d_out = d_buf[s, i * block : n]
                d_probs = dot(d_out, value, 1, 1)
                delta = jnp.sum(probs * d_probs, axis=-1, keepdims=True)
                d_scores = (probs * (d_probs - delta) * scale).astype(low)
                put(dot(d_scores, key), s, i, 0)
                key_part = dot(d_scores, query, 0, 0)
                value_part = dot(probs.astype(low), d_out, 0, 0)
                if i == count - 1:
                    key_sum[...] = key_part
                    value_sum[...] = value_part
                else:
                    key_sum[0:n] += key_part
                    value_sum[0:n] += value_part
                put(key_sum[i * block : n], s, i, 1)
                put(value_sum[i * block : n], s, i, 2)
        copy = pltpu.make_async_copy(done, out, sem_out)
        copy.start()
        copy.wait()

    return pl.pallas_call(
        body,
        name="attend_back",
        out_shape=jax.ShapeDtypeStruct((count, sequences, block, cols), low),
        in_specs=[WHOLE] * 5 + [ANY] * 2,
        out_specs=ANY,
        scratch_shapes=[
            pltpu.VMEM((sequences, length, cols), low),
            pltpu.VMEM((sequences, length, hd), low),
            pltpu.VMEM((length, hd), wide),
            pltpu.VMEM((length, hd), wide),
            pltpu.VMEM((count, sequences, block, cols), low),
            pltpu.SemaphoreType.DMA((count * sequences,)),
            pltpu.SemaphoreType.DMA((count * sequences,)),
            pltpu.SemaphoreType.DMA,
        ],
        compiler_params=FAST,
        cost_estimate=SMALL,
    )(seg_row, seg_col, *tables, parts, d_parts)


def norm_back(x_all, d_packed, d_hidden, w_qkv, w_in, gains, block):
    group, width = x_all.shape

    def body(x_ref, p_ref, h_ref, w1_ref, w2_ref, g_ref, out_ref, sums_ref):
        @pl.when(pl.program_id(0) == 0)
        def _():
            sums_ref[...] = jnp.zeros_like(sums_ref)

        normal, _ = normalised(x_ref[...].astype(wide))
        one = dot(p_ref[...], w1_ref[...], 1, 1)
        two = dot(h_ref[...], w2_ref[...], 1, 1)
        out_ref[...] = (one * g_ref[0:1] + two * g_ref[2:3]).astype(low)
        sums_ref[0:1] += jnp.sum(one * normal, axis=0, keepdims=True)
        sums_ref[1:2] += jnp.sum(one, axis=0, keepdims=True)
        sums_ref[2:3] += jnp.sum(two * normal, axis=0, keepdims=True)
        sums_ref[3:4] += jnp.sum(two, axis=0, keepdims=True)

    row = lambda n: pl.BlockSpec((block, n), lambda i: (i, 0))
    return pl.pallas_call(
        body,
        name="norm_back",
        grid=(group // block,),
        in_specs=[row(width), row(d_packed.shape[1]), row(d_hidden.shape[1])] + [WHOLE] * 3,
        out_specs=[row(width), pl.BlockSpec((4, width), lambda i: (0, 0))],
        out_shape=[
            jax.ShapeDtypeStruct((group, width), low),
            jax.ShapeDtypeStruct((4, width), wide),
        ],
        compiler_params=FAST,
        cost_estimate=SMALL,
    )(x_all, d_packed, d_hidden, w_qkv, w_in, gains)


def local_by_head(
    tokens,
    segments,
    positions,
    ln1_gain,
    ln1_bias,
    ln2_gain,
    ln2_bias,
    qkv_weight,
    qkv_bias,
    dense_weight,
    dense_bias,
    fc_in_weight,
    fc_in_bias,
    fc_out_weight,
    fc_out_bias,
    cotangent,
):
    width = tokens.shape[-1]
    block = tokens.shape[1]
    nf = lax.axis_size("fsdp")
    nc = lax.axis_size("ctx")
    me_c = lax.axis_index("ctx")
    me_f = lax.axis_index("fsdp")
    hd = width // HEADS
    units = fc_in_weight.shape[1] // nf
    group = nf * block
    length = nc * block
    rows = width // nf
    part = rows // nc
    x_own = tokens.reshape(block, width)
    g_own = cotangent.reshape(block, width)
    order = jnp.array([2 * j + kk for kk in range(2) for j in range(4)], jnp.int32)
    owners = jnp.bitwise_xor(order, me_f)
    plane = jnp.bitwise_xor(jnp.arange(nc, dtype=jnp.int32), me_c)

    ints = jnp.concatenate([segments, positions], axis=0)
    digits = jnp.concatenate([ints // 32, ints % 32]).astype(low)
    vectors = [ln1_gain, ln1_bias, ln2_gain, ln2_bias, qkv_bias, dense_bias, fc_out_bias]
    sizes = [v.shape[0] for v in vectors]
    extra = jnp.concatenate([digits.reshape(-1)] + vectors)
    extra = jnp.pad(extra, (0, part * LANES - extra.shape[0])).reshape(part, LANES)

    pieces = cut_weights(
        qkv_weight,
        fc_in_weight,
        extra,
        jnp.concatenate([owners, me_c[None]]).astype(jnp.int32),
        hd,
        units,
        part,
    )
    got = [pieces[0]] + [swap(pieces[j], "fsdp", 2 * j) for j in (1, 2, 3)]
    x_all = lax.all_gather(then(x_own, *got), "fsdp", axis=0, tiled=True)
    across = swap(jnp.stack([g[1] for g in got]), "fsdp", 1)
    g_all = lax.all_gather(then(g_own, across), "fsdp", axis=0, tiled=True)
    quarter = jnp.concatenate([jnp.stack([g[0] for g in got]), across])
    cols = 3 * hd + units
    qkv_parts, in_parts = gather_plane(quarter[..., : 3 * hd], quarter[..., 3 * hd : cols])

    back = (jnp.arange(nf, dtype=jnp.int32)[:, None] == owners[None, :]).astype(low)
    small = dot(back, quarter[..., cols:].reshape(nf, part * LANES))
    count = 4 * block
    digits = small[:, :count].astype(jnp.int32).reshape(nf, 2, 2, block)
    numbers = digits[:, 0] * 32 + digits[:, 1]
    position_group = numbers[:, 1].reshape(group)
    of_chip = numbers.reshape(4, 2, 2, block)
    seq_ints = [at(of_chip, me_c)] + [swap(at(of_chip, plane[m]), "ctx", m) for m in range(1, nc)]
    seq_ints = jnp.stack(seq_ints, axis=2)
    seq_ints = jnp.stack([at(seq_ints, plane[b], 2) for b in range(nc)], axis=2)
    seq_ints = seq_ints.reshape(2, 2, length)
    seg_row = seq_ints[:, 0][:, None, :]
    seg_col = seq_ints[:, 0][:, :, None]
    tables = turn_tables(position_group, hd // 4)
    seq_tables = [
        t.reshape(2, length, LANES) for t in turn_tables(seq_ints[:, 1].reshape(-1), hd // 4)
    ]
    whole, start = [], count
    for size in sizes:
        whole.append(small[:, start : start + size].reshape(-1))
        start += size
    norms = jnp.stack(whole[:4])
    head_bias = at(whole[4].reshape(3, nf, hd), me_f, 1).reshape(1, -1)

    row_places = (owners[None, :] * nc + plane[:, None]).reshape(-1)
    w_qkv = place(qkv_parts, row_places, nf * nc).reshape(width, 3 * hd)
    w_in = place(in_parts, row_places, nf * nc).reshape(width, units)

    first, second, packed = project(
        then(x_all, w_in), w_qkv, head_bias, norms, tables, block, hd
    )

    def to_sequences(values):
        return lax.all_to_all(
            values.reshape(4, 2, block, values.shape[1]), "ctx", 0, 0, tiled=True
        )

    def to_group(values):
        moved = lax.all_to_all(values, "ctx", 0, 0, tiled=True)
        return moved.reshape(group, values.shape[-1])

    parts = to_sequences(packed)
    active, slope = expand(
        then(second, packed), w_in, fc_in_bias.astype(wide).reshape(1, -1), block
    )
    mlp = contract(active, fc_out_weight, block)
    o = attend(then(parts, mlp), seg_row, seg_col, hd)
    o_back = to_group(o)
    x_bit, y_bit = me_c % 2, me_c // 2
    d_o = dot(then(g_all, o), dense_weight, 1, 1).astype(low)
    d_parts = to_sequences(d_o)
    partial = contract(then(o_back, d_o), dense_weight, block, mlp)
    dense_kept, dense_sent = grad_pair(o_back, then(g_all, partial), [y_bit], [1 - y_bit], 2)
    dense_got = swap(dense_sent, "ctx", 2)
    d_qkv = attend_back(
        parts, then(d_parts, dense_sent), seg_row, seg_col, seq_tables, hd
    )
    d_packed = to_group(d_qkv)
    summed = lax.psum_scatter(then(partial, d_qkv), "fsdp", scatter_dimension=0, tiled=True)

    rows_of = units // (nc * LANES)
    blocks = [((2 * y) * rows_of, s) for y in range(2) for s in range(rows_of)]
    d_hidden, hidden_sum = hidden_back(then(g_all, d_qkv), fc_out_weight, slope, block)
    out_kept, out_sent = grad_pair(
        active,
        then(g_all, d_hidden),
        [b + x_bit * rows_of + s for b, s in blocks],
        [b + (1 - x_bit) * rows_of + s for b, s in blocks],
        1,
    )
    out_shape = (1, 2, rows_of * LANES, width)
    out_got = swap(out_sent.reshape(out_shape), "ctx", 1)
    out_kept = out_kept.reshape(out_shape)
    by_y = [2 * f + y_bit for f in range(nf)], [2 * f + 1 - y_bit for f in range(nf)]
    in_kept, in_sent = grad_pair(second, then(d_hidden, out_sent), *by_y, 2)
    in_got = swap(in_sent, "ctx", 2)
    to_x = [2 * f + x_bit for f in range(nf)], [2 * f + 1 - x_bit for f in range(nf)]
    qkv_kept, qkv_sent = grad_pair(first, then(d_packed, in_sent, dense_got), *to_x, 2)
    qkv_got = swap(qkv_sent, "ctx", 1)
    rows_kept, rows_sent = add_split(out_kept, then(out_got, qkv_sent), y_bit)
    rows_got = swap(rows_sent, "ctx", 2)
    d_partial, sums = norm_back(
        then(x_all, rows_sent), d_packed, d_hidden, w_qkv, w_in, norms, block
    )
    def spread_out(values, parts):
        whole = jnp.zeros((parts, nf, values.shape[0] // parts), wide)
        return lax.dynamic_update_slice_in_dim(
            whole, values.reshape(parts, 1, -1), me_f, 1
        ).reshape(nf, -1)

    totals = jnp.concatenate(
        [sums[i].reshape(nf, -1) for i in range(4)]
        + [
            spread_out(jnp.sum(d_packed.astype(wide), axis=0), 3),
            spread_out(hidden_sum[0], 1),
            jnp.sum(g_own.astype(wide), axis=0).reshape(nf, -1),
        ],
        axis=1,
    )
    both_kept, both_sent = add_split_two(
        in_kept, then(in_got, d_partial), dense_kept, dense_got, x_bit
    )
    both_got = swap(both_sent, "ctx", 1)
    qkv_kept2, qkv_sent2 = add_split(qkv_kept, then(qkv_got, both_sent, rows_got), y_bit)
    qkv_got2 = swap(qkv_sent2, "ctx", 2)
    d_normal = lax.psum_scatter(
        then(d_partial, summed, qkv_sent2), "fsdp", scatter_dimension=0, tiled=True
    )

    def with_totals(values):
        rest = jnp.pad(totals.astype(low).reshape(nf, -1, values.shape[2]), ((0, 0), (0, 4), (0, 0)))
        return jnp.concatenate([values, rest], axis=1)

    both_got = then(both_got, rows_got, qkv_got2)
    in_mine = added(both_kept, both_got)
    rows_mine = added(rows_kept, then(rows_got, both_got))
    rows_x, rows_y = swap(rows_mine, "ctx", 1), swap(rows_mine, "ctx", 2)
    in_rows = lax.all_to_all(in_mine[:nf], "fsdp", 0, 0, tiled=True)
    qkv_mine = added(qkv_kept2, then(qkv_got2, both_got, rows_x, rows_y))
    qkv_rows = lax.all_to_all(with_totals(qkv_mine), "fsdp", 0, 0, tiled=True)
    rows_xy = swap(rows_y, "ctx", 1)
    in_rows = jnp.concatenate([then(in_rows, rows_x, rows_y, rows_xy), in_mine[nf:]])
    in_x, in_y = swap(in_rows, "ctx", 1), swap(in_rows, "ctx", 2)
    totals = jnp.sum(qkv_rows[:, part:].astype(wide), axis=0).astype(low)
    totals = jnp.pad(totals, ((0, part - totals.shape[0]), (0, 0)))[None]
    qkv_rows = then(jnp.concatenate([qkv_rows[:, :part], totals]), in_y)
    qkv_x, qkv_y = swap(qkv_rows, "ctx", 1), swap(qkv_rows, "ctx", 2)
    in_xy = swap(then(in_x, qkv_rows), "ctx", 2)
    qkv_xy = swap(qkv_y, "ctx", 1)
    rows_all = [rows_mine, rows_x, rows_y, rows_xy]
    in_all = [in_rows, in_x, in_y, in_xy]
    qkv_all = [qkv_rows, qkv_x, qkv_y, qkv_xy]
    by_x = 2 * (plane % 2) + plane // 2

    def whole_columns(pieces, places, shape, thirds, begin=0, count=nf):
        at_rows = (places[:, None] * jnp.ones((count,), jnp.int32)).reshape(-1)
        at_cols = jnp.tile(jnp.arange(count, dtype=jnp.int32), nc)
        return finish(pieces, at_rows, at_cols, shape, thirds, (begin, count))

    x_wide = x_own.astype(wide)
    d_normal = then(d_normal, qkv_x).astype(wide)
    output = (x_wide + summed.astype(wide) + whole[5] + whole[6]).astype(low).reshape(tokens.shape)
    own_normal, own_rstd = normalised(x_wide)
    d_x = own_rstd * (
        d_normal
        - jnp.mean(d_normal, axis=-1, keepdims=True)
        - own_normal * jnp.mean(d_normal * own_normal, axis=-1, keepdims=True)
    )
    input_grad = (g_own.astype(wide) + d_x).reshape(tokens.shape)

    totals = sum(r[-1, :4].astype(wide) for r in qkv_all).reshape(-1)
    grad_fc_out = whole_columns(rows_all, plane, fc_out_weight.shape, 1, 0, 1)
    grad_dense = whole_columns(in_all, plane, dense_weight.shape, 1, nf, width // units)
    in_all[3] = then(in_all[3], grad_fc_out, grad_dense, input_grad, output)
    grad_fc_in = whole_columns(in_all, plane, fc_in_weight.shape, 1)
    qkv_all[3] = then(qkv_all[3], grad_fc_in)
    grad_qkv = whole_columns(qkv_all, by_x, qkv_weight.shape, 3)

    cuts, start = [], 0
    for size in (rows, rows, rows, rows, 3 * width // nf, units, rows):
        cuts.append(totals[start : start + size])
        start += size
    return (
        output,
        input_grad,
        cuts[0],
        cuts[1],
        cuts[2],
        cuts[3],
        grad_qkv,
        cuts[4],
        grad_dense,
        cuts[6],
        grad_fc_in,
        cuts[5],
        grad_fc_out,
        cuts[6],
    )


def solution(mesh):
    placed = (
        P("fsdp", "ctx", None),
        P("fsdp", "ctx"),
        P("fsdp", "ctx"),
        P("fsdp"),
        P("fsdp"),
        P("fsdp"),
        P("fsdp"),
        P("fsdp", None),
        P("fsdp"),
        P("fsdp", None),
        P("fsdp"),
        P("fsdp", None),
        P("fsdp"),
        P("fsdp", None),
        P("fsdp"),
        P("fsdp", "ctx", None),
    )
    by_head = mesh.shape["fsdp"] == HEADS and mesh.shape["ctx"] == 4
    return jax.shard_map(
        local_by_head if by_head else local,
        mesh=mesh,
        in_specs=placed,
        out_specs=(
            P("fsdp", "ctx", None),
            P("fsdp", "ctx", None),
            P("fsdp"),
            P("fsdp"),
            P("fsdp"),
            P("fsdp"),
            P("fsdp", None),
            P("fsdp"),
            P("fsdp", None),
            P("fsdp"),
            P("fsdp", None),
            P("fsdp"),
            P("fsdp", None),
            P("fsdp"),
        ),
        check_vma=False,
    )
```

```python
import jax
import jax.numpy as jnp
from jax import lax
from jax.experimental import pallas as pl
from jax.experimental.pallas import tpu as pltpu
from jax.sharding import PartitionSpec as P

HEADS = 8


eps_norm = 1e-05


def layer_norm(values, gain_vec, shift_vec):
    row_mean = jnp.mean(values, axis=-1, keepdims=True)
    centred = values - row_mean
    spread = jnp.mean(centred * centred, axis=-1, keepdims=True)
    return centred * lax.rsqrt(spread + eps_norm) * gain_vec + shift_vec


def rotary_tables(position, rotary):
    frequency = 10000.0 ** (-jnp.arange(0, rotary, 2, dtype=jnp.float32) / rotary)
    angles = position.astype(jnp.float32)[:, None] * frequency[None, :]
    angles = jnp.concatenate([angles, angles], axis=-1)
    return (jnp.cos(angles), jnp.sin(angles))


def rotate(values, cosine, sine_table):
    rotary = cosine.shape[-1]
    half_rot = rotary // 2
    turned = jnp.concatenate([-values[..., half_rot:rotary], values[..., :half_rot]], axis=-1)
    rotated_head = values[..., :rotary] * cosine[:, None, :] + turned * sine_table[:, None, :]
    return jnp.concatenate([rotated_head, values[..., rotary:]], axis=-1)


def gelu_exact(tensor):
    return jax.nn.gelu(tensor, approximate=False)


def dot_right(left_side, right_side):
    return lax.dot_general(
        left_side, right_side, (((1,), (1,)), ((), ())), preferred_element_type=jnp.float32
    )


def dot_left(left_side, right_side):
    return lax.dot_general(
        left_side, right_side, (((0,), (0,)), ((), ())), preferred_element_type=jnp.float32
    )


def reduce_grads(weight_one, bias_one, weight_two, bias_two, gain_grad, shift_grad):
    shared = (
        lax.psum_scatter(
            weight_one.astype(jnp.bfloat16), "fsdp", scatter_dimension=0, tiled=True
        ).astype(jnp.float32),
        lax.psum_scatter(
            bias_one.astype(jnp.bfloat16), "fsdp", scatter_dimension=0, tiled=True
        ).astype(jnp.float32),
        lax.psum_scatter(
            weight_two.astype(jnp.bfloat16), "fsdp", scatter_dimension=0, tiled=True
        ).astype(jnp.float32),
        lax.psum_scatter(
            bias_two.astype(jnp.bfloat16), "fsdp", scatter_dimension=0, tiled=True
        ).astype(jnp.float32),
        lax.psum_scatter(
            gain_grad.astype(jnp.bfloat16), "fsdp", scatter_dimension=0, tiled=True
        ).astype(jnp.float32),
        lax.psum_scatter(
            shift_grad.astype(jnp.bfloat16), "fsdp", scatter_dimension=0, tiled=True
        ).astype(jnp.float32),
    )
    return (
        lax.psum(shared[0].astype(jnp.bfloat16), "ctx").astype(jnp.float32),
        lax.psum(shared[1].astype(jnp.bfloat16), "ctx").astype(jnp.float32),
        lax.psum(shared[2].astype(jnp.bfloat16), "ctx").astype(jnp.float32),
        lax.psum(shared[3].astype(jnp.bfloat16), "ctx").astype(jnp.float32),
        lax.psum(shared[4].astype(jnp.bfloat16), "ctx").astype(jnp.float32),
        lax.psum(shared[5].astype(jnp.bfloat16), "ctx").astype(jnp.float32),
    )


def local(
    tokens,
    segments,
    positions,
    ln1_gain,
    ln1_bias,
    ln2_gain,
    ln2_bias,
    qkv_weight,
    qkv_bias,
    dense_weight,
    dense_bias,
    fc_in_weight,
    fc_in_bias,
    fc_out_weight,
    fc_out_bias,
    cotangent,
):
    model_width = tokens.shape[-1]
    values = tokens.reshape(-1, model_width).astype(jnp.float32)
    row_count = values.shape[0]
    head_dim = model_width // HEADS
    score_scale = head_dim ** (-0.5)
    everyone = lax.all_gather(segments, "ctx", axis=1, tiled=True).reshape(-1)
    seq_length = everyone.shape[0]
    own_segment = segments.reshape(-1)
    query_index = lax.axis_index("ctx") * row_count + jnp.arange(row_count, dtype=jnp.int32)
    key_index = jnp.arange(seq_length, dtype=jnp.int32)
    allowed = (own_segment[:, None] == everyone[None, :]) & (
        key_index[None, :] <= query_index[:, None]
    )
    cosine, sine_table = rotary_tables(positions.reshape(-1), head_dim // 4)
    gathered = (
        lax.all_gather(ln1_gain, "fsdp", axis=0, tiled=True),
        lax.all_gather(ln1_bias, "fsdp", axis=0, tiled=True),
        lax.all_gather(ln2_gain, "fsdp", axis=0, tiled=True),
        lax.all_gather(ln2_bias, "fsdp", axis=0, tiled=True),
        lax.all_gather(qkv_weight, "fsdp", axis=0, tiled=True),
        lax.all_gather(qkv_bias, "fsdp", axis=0, tiled=True),
        lax.all_gather(dense_weight, "fsdp", axis=0, tiled=True),
        lax.all_gather(dense_bias, "fsdp", axis=0, tiled=True),
        lax.all_gather(fc_in_weight, "fsdp", axis=0, tiled=True),
        lax.all_gather(fc_in_bias, "fsdp", axis=0, tiled=True),
        lax.all_gather(fc_out_weight, "fsdp", axis=0, tiled=True),
        lax.all_gather(fc_out_bias, "fsdp", axis=0, tiled=True),
    )
    gain_one = gathered[0].astype(jnp.float32)
    shift_one = gathered[1].astype(jnp.float32)
    gain_two = gathered[2].astype(jnp.float32)
    shift_two = gathered[3].astype(jnp.float32)
    normed_one = layer_norm(values, gain_one, shift_one).astype(jnp.bfloat16)
    normed_two = layer_norm(values, gain_two, shift_two).astype(jnp.bfloat16)
    packed = jnp.dot(normed_one, gathered[4], preferred_element_type=jnp.float32) + gathered[
        5
    ].astype(jnp.float32)
    shaped = packed.reshape(row_count, 3, HEADS, head_dim)
    query_low = rotate(shaped[:, 0], cosine, sine_table).astype(jnp.bfloat16)
    key_low = (
        rotate(shaped[:, 1], cosine, sine_table)
        .astype(jnp.bfloat16)
        .reshape(row_count, model_width)
    )
    value_low = shaped[:, 2].astype(jnp.bfloat16).reshape(row_count, model_width)
    keys_all, values_all = (
        lax.all_gather(key_low, "ctx", axis=0, tiled=True),
        lax.all_gather(value_low, "ctx", axis=0, tiled=True),
    )

    def score_block(key_rows):
        raw_scores = jnp.einsum(
            "qhd,khd->hqk",
            query_low,
            key_rows.reshape(seq_length, HEADS, head_dim),
            preferred_element_type=jnp.float32,
        )
        return jnp.where(allowed[None], raw_scores * score_scale, -1e30)

    scores = score_block(keys_all)
    row_max = jnp.max(scores, axis=-1, keepdims=True)
    exp_scores = jnp.exp(scores - row_max)
    row_total = jnp.sum(exp_scores, axis=-1, keepdims=True)
    probs_low = (exp_scores / row_total).astype(jnp.bfloat16)
    log_total = row_max + jnp.log(row_total)
    mixed_heads = jnp.einsum(
        "hqk,khd->qhd",
        probs_low,
        values_all.reshape(seq_length, HEADS, head_dim),
        preferred_element_type=jnp.float32,
    )
    mixed_low = mixed_heads.reshape(row_count, model_width).astype(jnp.bfloat16)
    attn_out = jnp.dot(mixed_low, gathered[6], preferred_element_type=jnp.float32) + gathered[
        7
    ].astype(jnp.float32)
    hidden = jnp.dot(normed_two, gathered[8], preferred_element_type=jnp.float32) + gathered[
        9
    ].astype(jnp.float32)
    active_low = gelu_exact(hidden).astype(jnp.bfloat16)
    mlp_out = jnp.dot(active_low, gathered[10], preferred_element_type=jnp.float32) + gathered[
        11
    ].astype(jnp.float32)
    output = (values + attn_out + mlp_out).astype(jnp.bfloat16).reshape(tokens.shape)
    regathered = (
        lax.all_gather(ln1_gain, "fsdp", axis=0, tiled=True),
        lax.all_gather(ln1_bias, "fsdp", axis=0, tiled=True),
        lax.all_gather(ln2_gain, "fsdp", axis=0, tiled=True),
        lax.all_gather(ln2_bias, "fsdp", axis=0, tiled=True),
        lax.all_gather(qkv_weight, "fsdp", axis=0, tiled=True),
        lax.all_gather(qkv_bias, "fsdp", axis=0, tiled=True),
        lax.all_gather(dense_weight, "fsdp", axis=0, tiled=True),
        lax.all_gather(dense_bias, "fsdp", axis=0, tiled=True),
        lax.all_gather(fc_in_weight, "fsdp", axis=0, tiled=True),
        lax.all_gather(fc_in_bias, "fsdp", axis=0, tiled=True),
        lax.all_gather(fc_out_weight, "fsdp", axis=0, tiled=True),
        lax.all_gather(fc_out_bias, "fsdp", axis=0, tiled=True),
    )
    keys_back, values_back = (
        lax.all_gather(key_low, "ctx", axis=0, tiled=True),
        lax.all_gather(value_low, "ctx", axis=0, tiled=True),
    )
    grad_out = cotangent.reshape(row_count, model_width)
    grad_wide = grad_out.astype(jnp.float32)
    d_active = dot_right(grad_out, regathered[10])
    d_hidden_low = jax.vjp(gelu_exact, hidden)[1](d_active)[0].astype(jnp.bfloat16)
    d_second = dot_right(d_hidden_low, regathered[8])
    d_mixed_low = (
        dot_right(grad_out, regathered[6]).astype(jnp.bfloat16).reshape(row_count, HEADS, head_dim)
    )
    probs_again = jnp.exp(score_block(keys_back) - log_total)
    probs_again_low = probs_again.astype(jnp.bfloat16)
    grad_probs = jnp.einsum(
        "qhd,khd->hqk",
        d_mixed_low,
        values_back.reshape(seq_length, HEADS, head_dim),
        preferred_element_type=jnp.float32,
    )
    row_delta = jnp.sum(probs_again * grad_probs, axis=-1, keepdims=True)
    grad_scores = (probs_again * (grad_probs - row_delta) * score_scale).astype(jnp.bfloat16)
    d_query = jnp.einsum(
        "hqk,khd->qhd",
        grad_scores,
        keys_back.reshape(seq_length, HEADS, head_dim),
        preferred_element_type=jnp.float32,
    )
    d_key = jnp.einsum(
        "hqk,qhd->khd", grad_scores, query_low, preferred_element_type=jnp.float32
    ).reshape(row_count * lax.axis_size("ctx"), model_width)
    d_value = jnp.einsum(
        "hqk,qhd->khd", probs_again_low, d_mixed_low, preferred_element_type=jnp.float32
    ).reshape(row_count * lax.axis_size("ctx"), model_width)
    kv_grad = lax.psum_scatter(
        jnp.concatenate([d_key, d_value], axis=1).astype(jnp.bfloat16),
        "ctx",
        scatter_dimension=0,
        tiled=True,
    ).astype(jnp.float32)
    d_key_own = kv_grad[:, :model_width].reshape(row_count, HEADS, head_dim)
    d_packed = jnp.concatenate(
        [
            rotate(d_query, cosine, -sine_table).reshape(row_count, model_width),
            rotate(d_key_own, cosine, -sine_table).reshape(row_count, model_width),
            kv_grad[:, model_width:],
        ],
        axis=1,
    )
    d_packed_low = d_packed.astype(jnp.bfloat16)
    d_first = dot_right(d_packed_low, regathered[4])
    norm_back_one = jax.vjp(layer_norm, values, gain_one, shift_one)[1]
    d_values_one, d_gain_one, d_shift_one = norm_back_one(d_first)
    norm_back_two = jax.vjp(layer_norm, values, gain_two, shift_two)[1]
    d_values_two, d_gain_two, d_shift_two = norm_back_two(d_second)
    input_grad = (grad_wide + d_values_one + d_values_two).reshape(tokens.shape)
    grad_sum = jnp.sum(grad_wide, axis=0)
    mlp_grads = reduce_grads(
        dot_left(normed_two, d_hidden_low),
        jnp.sum(d_hidden_low.astype(jnp.float32), axis=0),
        dot_left(active_low, grad_out),
        grad_sum,
        d_gain_two,
        d_shift_two,
    )
    attn_grads = reduce_grads(
        dot_left(normed_one, d_packed_low),
        jnp.sum(d_packed_low.astype(jnp.float32), axis=0),
        dot_left(mixed_low, grad_out),
        grad_sum,
        d_gain_one,
        d_shift_one,
    )
    return (
        output,
        input_grad,
        attn_grads[4],
        attn_grads[5],
        mlp_grads[4],
        mlp_grads[5],
        attn_grads[0],
        attn_grads[1],
        attn_grads[2],
        attn_grads[3],
        mlp_grads[0],
        mlp_grads[1],
        mlp_grads[2],
        mlp_grads[3],
    )


LANES = 128
FAST = pltpu.CompilerParams(vmem_limit_bytes=56 * 1024 * 1024)
SMALL = pl.CostEstimate(flops=1, bytes_accessed=1, transcendentals=0)
ANY = pl.BlockSpec(memory_space=pl.ANY)
SCALARS = pl.BlockSpec(memory_space=pltpu.SMEM)
WHOLE = pl.BlockSpec(memory_space=pltpu.VMEM)
low = jnp.bfloat16
wide = jnp.float32


def dot(a, b, left=1, right=0):
    return lax.dot_general(a, b, (((left,), (right,)), ((), ())), preferred_element_type=wide)


def swap(values, axis, mask):
    return lax.ppermute(values, axis, [(i, i ^ mask) for i in range(lax.axis_size(axis))])


def at(values, index, axis=0):
    return lax.dynamic_index_in_dim(values, index, axis, keepdims=False)


def added(*values):
    total = values[0].astype(wide)
    for v in values[1:]:
        total = total + v.astype(wide)
    return total.astype(low)


def then(value, *events):
    return lax.optimization_barrier((value,) + events)[0]


def gather_plane(first, second):
    first_x, second_y = swap(first, "ctx", 1), swap(second, "ctx", 2)
    first_y, second_x = swap(first, "ctx", 2), swap(second, "ctx", 1)
    first_xy = swap(first_y, "ctx", 1)
    second_xy = swap(second_x, "ctx", 2)
    return [first, first_x, first_y, first_xy], [second, second_x, second_y, second_xy]


def place(pieces, places, count):
    sizes = [p.shape[0] for p in pieces]

    total = sum(sizes)

    def body(places_ref, *refs):
        out, buf, sems_in, sems_out = refs[-4:]
        copies = []
        for ref, size in zip(refs, sizes):
            for i in range(size):
                n = len(copies)
                copies.append(pltpu.make_async_copy(ref.at[i], buf.at[n], sems_in.at[n]))
                copies[n].start()
        leaving = []
        for n in range(total):
            copies[n].wait()
            copy = pltpu.make_async_copy(buf.at[n], out.at[places_ref[n]], sems_out.at[n])
            copy.start()
            leaving.append(copy)
        for copy in leaving:
            copy.wait()

    return pl.pallas_call(
        body,
        name="place",
        out_shape=jax.ShapeDtypeStruct((count,) + pieces[0].shape[1:], pieces[0].dtype),
        in_specs=[SCALARS] + [ANY] * len(pieces),
        out_specs=ANY,
        scratch_shapes=[
            pltpu.VMEM((total,) + pieces[0].shape[1:], pieces[0].dtype),
            pltpu.SemaphoreType.DMA((total,)),
            pltpu.SemaphoreType.DMA((total,)),
        ],
        compiler_params=FAST,
        cost_estimate=SMALL,
    )(places, *pieces)


def cut_weights(qkv_weight, fc_in_weight, extra, places, hd, units, part):
    span = qkv_weight.shape[1] // 3
    cols = 3 * hd + units

    def body(places_ref, qkv_ref, in_ref, extra_ref, *refs):
        outs, buf, sems_in, sems_out = refs[:4], refs[4], refs[5], refs[6]
        row = pl.ds(pl.multiple_of(places_ref[8] * part, part), part)
        copies = []
        for n in range(8):
            f = places_ref[n]
            for t in range(3):
                copies.append(
                    pltpu.make_async_copy(
                        qkv_ref.at[row, pl.ds(pl.multiple_of(t * span + f * hd, LANES), hd)],
                        buf.at[n, :, pl.ds(t * hd, hd)],
                        sems_in.at[len(copies)],
                    )
                )
                copies[-1].start()
            copies.append(
                pltpu.make_async_copy(
                    in_ref.at[row, pl.ds(pl.multiple_of(f * units, LANES), units)],
                    buf.at[n, :, pl.ds(3 * hd, units)],
                    sems_in.at[len(copies)],
                )
            )
            copies[-1].start()
            copies.append(
                pltpu.make_async_copy(
                    extra_ref, buf.at[n, :, pl.ds(cols, LANES)], sems_in.at[len(copies)]
                )
            )
            copies[-1].start()
        leaving = []
        for n in range(8):
            for copy in copies[5 * n : 5 * n + 5]:
                copy.wait()
            copy = pltpu.make_async_copy(buf.at[n], outs[n % 4].at[n // 4], sems_out.at[n])
            copy.start()
            leaving.append(copy)
        for copy in leaving:
            copy.wait()

    return pl.pallas_call(
        body,
        name="cut_weights",
        out_shape=[jax.ShapeDtypeStruct((2, part, cols + LANES), low)] * 4,
        in_specs=[SCALARS, ANY, ANY, ANY],
        out_specs=[ANY] * 4,
        scratch_shapes=[
            pltpu.VMEM((8, part, cols + LANES), low),
            pltpu.SemaphoreType.DMA((40,)),
            pltpu.SemaphoreType.DMA((8,)),
        ],
        compiler_params=FAST,
        cost_estimate=SMALL,
    )(places, qkv_weight, fc_in_weight, extra)


def finish(pieces, rows_at, cols_at, shape, thirds=1, chosen=None):
    begin, size = chosen or (0, pieces[0].shape[0])
    total = size * len(pieces)
    rows, cols = pieces[0].shape[1:]
    span = cols // thirds

    def body(rows_ref, cols_ref, *refs):
        out, narrow, full, sems_in, sems_out = refs[-5:]
        copies = []
        for ref in refs[: len(pieces)]:
            for i in range(begin, begin + size):
                n = len(copies)
                copies.append(pltpu.make_async_copy(ref.at[i], narrow.at[n], sems_in.at[n]))
                copies[n].start()
        leaving = []
        for n in range(total):
            copies[n].wait()
            full[n] = narrow[n].astype(wide)
            row = pl.ds(pl.multiple_of(rows_ref[n] * rows, rows), rows)
            for t in range(thirds):
                start = t * (shape[1] // thirds) + cols_ref[n] * span
                copy = pltpu.make_async_copy(
                    full.at[n, :, pl.ds(t * span, span)],
                    out.at[row, pl.ds(pl.multiple_of(start, LANES), span)],
                    sems_out.at[n * thirds + t],
                )
                copy.start()
                leaving.append(copy)
        for copy in leaving:
            copy.wait()

    return pl.pallas_call(
        body,
        name="finish",
        out_shape=jax.ShapeDtypeStruct(shape, wide),
        in_specs=[SCALARS, SCALARS] + [ANY] * len(pieces),
        out_specs=ANY,
        scratch_shapes=[
            pltpu.VMEM((total, rows, cols), low),
            pltpu.VMEM((total, rows, cols), wide),
            pltpu.SemaphoreType.DMA((total,)),
            pltpu.SemaphoreType.DMA((total * thirds,)),
        ],
        compiler_params=FAST,
        cost_estimate=SMALL,
    )(rows_at, cols_at, *pieces)


def normalised(values):
    centred = values - jnp.mean(values, axis=-1, keepdims=True)
    spread = jnp.mean(centred * centred, axis=-1, keepdims=True)
    rstd = lax.rsqrt(spread + eps_norm)
    return centred * rstd, rstd


def turn_tables(position, rotary):
    cosine, sine = rotary_tables(position, rotary)
    half = rotary // 2
    zero = jnp.zeros((position.shape[0], LANES - rotary), wide)
    none = jnp.zeros_like(sine[:, :half])
    return (
        jnp.concatenate([cosine, zero + 1.0], axis=1),
        jnp.concatenate([-sine[:, :half], none, zero], axis=1),
        jnp.concatenate([none, sine[:, half:], zero], axis=1),
    )


def turn(values, here, above, below, half):
    return (
        values * here
        + pltpu.roll(values, LANES - half, 1) * above
        + pltpu.roll(values, half, 1) * below
    )


def project(x_all, weight, bias, norms, tables, block, hd):
    group, width = x_all.shape
    cols = weight.shape[1]
    half = hd // 8

    def body(x_ref, w_ref, b_ref, n_ref, t0, t1, t2, first_ref, second_ref, out_ref):
        normal, _ = normalised(x_ref[...].astype(wide))
        first = (normal * n_ref[0:1] + n_ref[1:2]).astype(low)
        second_ref[...] = (normal * n_ref[2:3] + n_ref[3:4]).astype(low)
        first_ref[...] = first
        packed = dot(first, w_ref[...]) + b_ref[...]
        for i in range(3):
            lead = packed[:, i * hd : i * hd + LANES]
            if i < 2:
                lead = turn(lead, t0[...], t1[...], t2[...], half)
            out_ref[:, i * hd : i * hd + LANES] = lead.astype(low)
            out_ref[:, i * hd + LANES : (i + 1) * hd] = packed[
                :, i * hd + LANES : (i + 1) * hd
            ].astype(low)

    row = lambda n: pl.BlockSpec((block, n), lambda i: (i, 0))
    return pl.pallas_call(
        body,
        name="project",
        grid=(group // block,),
        in_specs=[row(width), WHOLE, WHOLE, WHOLE, row(LANES), row(LANES), row(LANES)],
        out_specs=[row(width), row(width), row(cols)],
        out_shape=[
            jax.ShapeDtypeStruct((group, width), low),
            jax.ShapeDtypeStruct((group, width), low),
            jax.ShapeDtypeStruct((group, cols), low),
        ],
        compiler_params=FAST,
        cost_estimate=SMALL,
    )(x_all, weight, bias, norms, *tables)


def expand(second, weight, bias, block):
    group, width = second.shape
    cols = weight.shape[1]

    def body(s_ref, w_ref, b_ref, active_ref, slope_ref):
        hidden = dot(s_ref[...], w_ref[...]) + b_ref[...]
        upper = 0.5 * (1.0 + lax.erf(hidden * (0.5**0.5)))
        active_ref[...] = (hidden * upper).astype(low)
        bell = jnp.exp(-0.5 * hidden * hidden) * ((2.0 * jnp.pi) ** -0.5)
        slope_ref[...] = (upper + hidden * bell).astype(low)

    row = lambda n: pl.BlockSpec((block, n), lambda i: (i, 0))
    return pl.pallas_call(
        body,
        name="expand",
        grid=(group // block,),
        in_specs=[row(width), WHOLE, WHOLE],
        out_specs=[row(cols), row(cols)],
        out_shape=[jax.ShapeDtypeStruct((group, cols), low)] * 2,
        compiler_params=FAST,
        cost_estimate=SMALL,
    )(second, weight, bias)


def contract(left, weight, block, more=None):
    group = left.shape[0]
    width = weight.shape[1]

    def body(left_ref, weight_ref, *refs):
        total = dot(left_ref[...], weight_ref[...])
        if more is not None:
            total = total + refs[0][...].astype(wide)
        refs[-1][...] = total.astype(low)

    row = lambda n: pl.BlockSpec((block, n), lambda i: (i, 0))
    return pl.pallas_call(
        body,
        name="contract",
        grid=(group // block,),
        in_specs=[row(left.shape[1]), WHOLE] + ([] if more is None else [row(width)]),
        out_specs=row(width),
        out_shape=jax.ShapeDtypeStruct((group, width), low),
        compiler_params=FAST,
        cost_estimate=SMALL,
    )(left, weight, *(() if more is None else (more,)))


def hidden_back(g_all, fc_out_weight, slope, block):
    group, width = g_all.shape
    units = fc_out_weight.shape[0]

    def body(g_ref, w_ref, s_ref, out_ref, sum_ref):
        @pl.when(pl.program_id(0) == 0)
        def _():
            sum_ref[...] = jnp.zeros_like(sum_ref)

        d_hidden = (dot(g_ref[...], w_ref[...], 1, 1) * s_ref[...].astype(wide)).astype(low)
        out_ref[...] = d_hidden
        sum_ref[...] += jnp.sum(d_hidden.astype(wide), axis=0, keepdims=True)

    row = lambda n: pl.BlockSpec((block, n), lambda i: (i, 0))
    return pl.pallas_call(
        body,
        name="hidden_back",
        grid=(group // block,),
        in_specs=[row(width), WHOLE, row(units)],
        out_specs=[row(units), pl.BlockSpec((1, units), lambda i: (0, 0))],
        out_shape=[
            jax.ShapeDtypeStruct((group, units), low),
            jax.ShapeDtypeStruct((1, units), wide),
        ],
        compiler_params=FAST,
        cost_estimate=SMALL,
    )(g_all, fc_out_weight, slope)


def grad_pair(left, right, keep, send, parts):
    tokens = left.shape[0]
    cols = right.shape[1]
    n = len(keep)
    size = LANES // parts

    def body(keep_ref, send_ref, a_ref, b_ref, right_ref, keep_out, send_out):
        both = jnp.concatenate([a_ref[...], b_ref[...]], axis=1)
        result = dot(both, right_ref[...], 0, 0).astype(low)
        keep_out[...] = result[:LANES].reshape(1, parts, size, cols)
        send_out[...] = result[LANES:].reshape(1, parts, size, cols)

    shape = jax.ShapeDtypeStruct((n, parts, size, cols), low)
    out = pl.BlockSpec((1, parts, size, cols), lambda i, k, s: (i, 0, 0, 0))
    return pl.pallas_call(
        body,
        name="grad_pair",
        grid_spec=pltpu.PrefetchScalarGridSpec(
            num_scalar_prefetch=2,
            grid=(n,),
            in_specs=[
                pl.BlockSpec((tokens, LANES), lambda i, k, s: (0, k[i])),
                pl.BlockSpec((tokens, LANES), lambda i, k, s: (0, s[i])),
                pl.BlockSpec((tokens, cols), lambda i, k, s: (0, 0)),
            ],
            out_specs=[out, out],
        ),
        out_shape=[shape, shape],
        compiler_params=FAST,
        cost_estimate=SMALL,
    )(jnp.stack(keep).astype(jnp.int32), jnp.stack(send).astype(jnp.int32), left, left, right)


def add_split(kept, got, bit):
    n, _, rows, cols = kept.shape

    def body(bit_ref, a_ref, b_ref, keep_out, send_out):
        for out, half in ((keep_out, bit_ref[0]), (send_out, 1 - bit_ref[0])):
            out[...] = (a_ref[:, half].astype(wide) + b_ref[:, half].astype(wide)).astype(low)

    shape = jax.ShapeDtypeStruct((n, rows, cols), low)
    both = pl.BlockSpec((n // 2 if n > 1 else 1, 2, rows, cols), lambda i: (i, 0, 0, 0))
    out = pl.BlockSpec((n // 2 if n > 1 else 1, rows, cols), lambda i: (i, 0, 0))
    return pl.pallas_call(
        body,
        name="add_split",
        grid=(2 if n > 1 else 1,),
        in_specs=[SCALARS, both, both],
        out_specs=[out, out],
        out_shape=[shape, shape],
        compiler_params=FAST,
        cost_estimate=SMALL,
    )(bit[None].astype(jnp.int32), kept, got)


def add_split_two(kept, got, other_kept, other_got, bit):
    n, _, rows, cols = kept.shape
    more = other_kept.shape[3] // cols

    def body(bit_ref, a_ref, b_ref, c_ref, d_ref, keep_out, send_out):
        for out, half in ((keep_out, bit_ref[0]), (send_out, 1 - bit_ref[0])):
            out[:n] = (a_ref[:, half].astype(wide) + b_ref[:, half].astype(wide)).astype(low)
            other = (c_ref[0, half].astype(wide) + d_ref[0, half].astype(wide)).astype(low)
            for i in range(more):
                out[n + i] = other[:, i * cols : (i + 1) * cols]

    shape = jax.ShapeDtypeStruct((n + more, rows, cols), low)
    return pl.pallas_call(
        body,
        name="add_split_two",
        in_specs=[SCALARS] + [WHOLE] * 4,
        out_specs=[WHOLE] * 2,
        out_shape=[shape, shape],
        compiler_params=FAST,
        cost_estimate=SMALL,
    )(bit[None].astype(jnp.int32), kept, got, other_kept, other_got)


def fetch(source, target, sems):
    count, sequences, block, _ = source.shape
    copies = []
    for m in range(count):
        for s in range(sequences):
            n = len(copies)
            copies.append(
                pltpu.make_async_copy(
                    source.at[m, s], target.at[s, pl.ds(m * block, block)], sems.at[n]
                )
            )
            copies[n].start()
    return copies


def block_scores(buf, row_ref, col_ref, s, i, block, hd, scale):
    count = (i + 1) * block
    query = buf[s, i * block : count, 0:hd]
    key = buf[s, 0:count, hd : 2 * hd]
    scores = dot(query, key, 1, 1) * scale
    q_index = lax.broadcasted_iota(jnp.int32, (block, count), 0) + i * block
    k_index = lax.broadcasted_iota(jnp.int32, (block, count), 1)
    allowed = (col_ref[s, i * block : count, :] == row_ref[s, :, 0:count]) & (k_index <= q_index)
    scores = jnp.where(allowed, scores, -1e30)
    probs = jnp.exp(scores - jnp.max(scores, axis=-1, keepdims=True))
    return query, key, probs / jnp.sum(probs, axis=-1, keepdims=True)


def attend(parts, seg_row, seg_col, hd):
    count, sequences, block, cols = parts.shape
    scale = hd ** (-0.5)

    def body(row_ref, col_ref, parts_ref, out, buf, mixed, sems_in, sem_out):
        for copy in fetch(parts_ref, buf, sems_in):
            copy.wait()
        for s in range(sequences):
            for i in range(count):
                _, _, probs = block_scores(buf, row_ref, col_ref, s, i, block, hd, scale)
                value = buf[s, 0 : (i + 1) * block, 2 * hd : 3 * hd]
                mixed[i, s] = dot(probs.astype(low), value).astype(low)
        copy = pltpu.make_async_copy(mixed, out, sem_out)
        copy.start()
        copy.wait()

    return pl.pallas_call(
        body,
        name="attend",
        out_shape=jax.ShapeDtypeStruct((count, sequences, block, hd), low),
        in_specs=[WHOLE, WHOLE, ANY],
        out_specs=ANY,
        scratch_shapes=[
            pltpu.VMEM((sequences, count * block, cols), low),
            pltpu.VMEM((count, sequences, block, hd), low),
            pltpu.SemaphoreType.DMA((count * sequences,)),
            pltpu.SemaphoreType.DMA,
        ],
        compiler_params=FAST,
        cost_estimate=SMALL,
    )(seg_row, seg_col, parts)


def attend_back(parts, d_parts, seg_row, seg_col, tables, hd):
    count, sequences, block, cols = parts.shape
    length = count * block
    scale = hd ** (-0.5)
    half = hd // 8

    def body(row_ref, col_ref, t0, t1, t2, parts_ref, d_ref, out, *scratch):
        buf, d_buf, key_sum, value_sum, done, sems_in, sems_d, sem_out = scratch
        for copy in fetch(parts_ref, buf, sems_in) + fetch(d_ref, d_buf, sems_d):
            copy.wait()

        def put(values, s, i, which):
            lead = values[:, 0:LANES]
            if which < 2:
                rows = slice(i * block, (i + 1) * block)
                lead = turn(lead, t0[s, rows], -t1[s, rows], -t2[s, rows], half)
            done[i, s, :, which * hd : which * hd + LANES] = lead.astype(low)
            done[i, s, :, which * hd + LANES : (which + 1) * hd] = values[:, LANES:].astype(low)

        for s in range(sequences):
            for i in reversed(range(count)):
                n = (i + 1) * block
                query, key, probs = block_scores(buf, row_ref, col_ref, s, i, block, hd, scale)
                value = buf[s, 0:n, 2 * hd : 3 * hd]
                d_out = d_buf[s, i * block : n]
                d_probs = dot(d_out, value, 1, 1)
                delta = jnp.sum(probs * d_probs, axis=-1, keepdims=True)
                d_scores = (probs * (d_probs - delta) * scale).astype(low)
                put(dot(d_scores, key), s, i, 0)
                key_part = dot(d_scores, query, 0, 0)
                value_part = dot(probs.astype(low), d_out, 0, 0)
                if i == count - 1:
                    key_sum[...] = key_part
                    value_sum[...] = value_part
                else:
                    key_sum[0:n] += key_part
                    value_sum[0:n] += value_part
                put(key_sum[i * block : n], s, i, 1)
                put(value_sum[i * block : n], s, i, 2)
        copy = pltpu.make_async_copy(done, out, sem_out)
        copy.start()
        copy.wait()

    return pl.pallas_call(
        body,
        name="attend_back",
        out_shape=jax.ShapeDtypeStruct((count, sequences, block, cols), low),
        in_specs=[WHOLE] * 5 + [ANY] * 2,
        out_specs=ANY,
        scratch_shapes=[
            pltpu.VMEM((sequences, length, cols), low),
            pltpu.VMEM((sequences, length, hd), low),
            pltpu.VMEM((length, hd), wide),
            pltpu.VMEM((length, hd), wide),
            pltpu.VMEM((count, sequences, block, cols), low),
            pltpu.SemaphoreType.DMA((count * sequences,)),
            pltpu.SemaphoreType.DMA((count * sequences,)),
            pltpu.SemaphoreType.DMA,
        ],
        compiler_params=FAST,
        cost_estimate=SMALL,
    )(seg_row, seg_col, *tables, parts, d_parts)


def norm_back(x_all, d_packed, d_hidden, w_qkv, w_in, gains, block, half, before=()):
    group, width = x_all.shape
    steps = group // block // 2

    def body(x_ref, p_ref, h_ref, w1_ref, w2_ref, g_ref, *refs):
        out_ref, sums_ref = refs[-2:]

        @pl.when(pl.program_id(0) == 0)
        def _():
            sums_ref[...] = refs[1][...] if before else jnp.zeros_like(sums_ref)

        normal, _ = normalised(x_ref[...].astype(wide))
        one = dot(p_ref[...], w1_ref[...], 1, 1)
        two = dot(h_ref[...], w2_ref[...], 1, 1)
        out_ref[...] = (one * g_ref[0:1] + two * g_ref[2:3]).astype(low)
        sums_ref[0:1] += jnp.sum(one * normal, axis=0, keepdims=True)
        sums_ref[1:2] += jnp.sum(one, axis=0, keepdims=True)
        sums_ref[2:3] += jnp.sum(two * normal, axis=0, keepdims=True)
        sums_ref[3:4] += jnp.sum(two, axis=0, keepdims=True)

    row = lambda n: pl.BlockSpec((block, n), lambda i: (i + half * steps, 0))
    return pl.pallas_call(
        body,
        name="norm_back",
        grid=(steps,),
        in_specs=[row(width), row(d_packed.shape[1]), row(d_hidden.shape[1])] + [WHOLE] * 3
        + ([ANY, WHOLE] if before else []),
        out_specs=[row(width), pl.BlockSpec((4, width), lambda i: (0, 0))],
        out_shape=[
            jax.ShapeDtypeStruct((group, width), low),
            jax.ShapeDtypeStruct((4, width), wide),
        ],
        input_output_aliases={6: 0} if before else {},
        compiler_params=FAST,
        cost_estimate=SMALL,
    )(x_all, d_packed, d_hidden, w_qkv, w_in, gains, *before)


def local_by_head(
    tokens,
    segments,
    positions,
    ln1_gain,
    ln1_bias,
    ln2_gain,
    ln2_bias,
    qkv_weight,
    qkv_bias,
    dense_weight,
    dense_bias,
    fc_in_weight,
    fc_in_bias,
    fc_out_weight,
    fc_out_bias,
    cotangent,
):
    width = tokens.shape[-1]
    block = tokens.shape[1]
    nf = lax.axis_size("fsdp")
    nc = lax.axis_size("ctx")
    me_c = lax.axis_index("ctx")
    me_f = lax.axis_index("fsdp")
    hd = width // HEADS
    units = fc_in_weight.shape[1] // nf
    group = nf * block
    length = nc * block
    rows = width // nf
    part = rows // nc
    x_own = tokens.reshape(block, width)
    g_own = cotangent.reshape(block, width)
    order = jnp.array([2 * j + kk for kk in range(2) for j in range(4)], jnp.int32)
    owners = jnp.bitwise_xor(order, me_f)
    plane = jnp.bitwise_xor(jnp.arange(nc, dtype=jnp.int32), me_c)

    ints = jnp.concatenate([segments, positions], axis=0)
    digits = jnp.concatenate([ints // 32, ints % 32]).astype(low)
    vectors = [ln1_gain, ln1_bias, ln2_gain, ln2_bias, qkv_bias, dense_bias, fc_out_bias]
    sizes = [v.shape[0] for v in vectors]
    extra = jnp.concatenate([digits.reshape(-1)] + vectors)
    extra = jnp.pad(extra, (0, part * LANES - extra.shape[0])).reshape(part, LANES)

    pieces = cut_weights(
        qkv_weight,
        fc_in_weight,
        extra,
        jnp.concatenate([owners, me_c[None]]).astype(jnp.int32),
        hd,
        units,
        part,
    )
    got = [pieces[0]] + [swap(pieces[j], "fsdp", 2 * j) for j in (1, 2, 3)]
    x_all = lax.all_gather(then(x_own, *got), "fsdp", axis=0, tiled=True)
    across = swap(jnp.stack([g[1] for g in got]), "fsdp", 1)
    g_all = lax.all_gather(then(g_own, across), "fsdp", axis=0, tiled=True)
    quarter = jnp.concatenate([jnp.stack([g[0] for g in got]), across])
    cols = 3 * hd + units
    qkv_parts, in_parts = gather_plane(quarter[..., : 3 * hd], quarter[..., 3 * hd : cols])

    back = (jnp.arange(nf, dtype=jnp.int32)[:, None] == owners[None, :]).astype(low)
    small = dot(back, quarter[..., cols:].reshape(nf, part * LANES))
    count = 4 * block
    digits = small[:, :count].astype(jnp.int32).reshape(nf, 2, 2, block)
    numbers = digits[:, 0] * 32 + digits[:, 1]
    position_group = numbers[:, 1].reshape(group)
    of_chip = numbers.reshape(4, 2, 2, block)
    seq_ints = [at(of_chip, me_c)] + [swap(at(of_chip, plane[m]), "ctx", m) for m in range(1, nc)]
    seq_ints = jnp.stack(seq_ints, axis=2)
    seq_ints = jnp.stack([at(seq_ints, plane[b], 2) for b in range(nc)], axis=2)
    seq_ints = seq_ints.reshape(2, 2, length)
    seg_row = seq_ints[:, 0][:, None, :]
    seg_col = seq_ints[:, 0][:, :, None]
    tables = turn_tables(position_group, hd // 4)
    seq_tables = [
        t.reshape(2, length, LANES) for t in turn_tables(seq_ints[:, 1].reshape(-1), hd // 4)
    ]
    whole, start = [], count
    for size in sizes:
        whole.append(small[:, start : start + size].reshape(-1))
        start += size
    norms = jnp.stack(whole[:4])
    head_bias = at(whole[4].reshape(3, nf, hd), me_f, 1).reshape(1, -1)

    row_places = (owners[None, :] * nc + plane[:, None]).reshape(-1)
    w_qkv = place(qkv_parts, row_places, nf * nc).reshape(width, 3 * hd)
    w_in = place(in_parts, row_places, nf * nc).reshape(width, units)

    first, second, packed = project(
        then(x_all, w_in), w_qkv, head_bias, norms, tables, block, hd
    )

    def to_sequences(values):
        return lax.all_to_all(
            values.reshape(4, 2, block, values.shape[1]), "ctx", 0, 0, tiled=True
        )

    def to_group(values):
        moved = lax.all_to_all(values, "ctx", 0, 0, tiled=True)
        return moved.reshape(group, values.shape[-1])

    parts = to_sequences(packed)
    active, slope = expand(
        then(second, packed), w_in, fc_in_bias.astype(wide).reshape(1, -1), block
    )
    mlp = contract(active, fc_out_weight, block)
    o = attend(then(parts, mlp), seg_row, seg_col, hd)
    o_back = to_group(o)
    x_bit, y_bit = me_c % 2, me_c // 2
    d_o = dot(then(g_all, o), dense_weight, 1, 1).astype(low)
    d_parts = to_sequences(d_o)
    partial = contract(then(o_back, d_o), dense_weight, block, mlp)
    dense_kept, dense_sent = grad_pair(o_back, then(g_all, partial), [y_bit], [1 - y_bit], 2)
    dense_got = swap(dense_sent, "ctx", 2)
    d_qkv = attend_back(
        parts, then(d_parts, dense_sent), seg_row, seg_col, seq_tables, hd
    )
    d_packed = to_group(d_qkv)
    summed = lax.psum_scatter(then(partial, d_qkv), "fsdp", scatter_dimension=0, tiled=True)

    rows_of = units // (nc * LANES)
    blocks = [((2 * y) * rows_of, s) for y in range(2) for s in range(rows_of)]
    d_hidden, hidden_sum = hidden_back(then(g_all, d_qkv), fc_out_weight, slope, block)
    out_kept, out_sent = grad_pair(
        active,
        then(g_all, d_hidden),
        [b + x_bit * rows_of + s for b, s in blocks],
        [b + (1 - x_bit) * rows_of + s for b, s in blocks],
        1,
    )
    out_shape = (1, 2, rows_of * LANES, width)
    out_got = swap(out_sent.reshape(out_shape), "ctx", 1)
    out_kept = out_kept.reshape(out_shape)
    by_y = [2 * f + y_bit for f in range(nf)], [2 * f + 1 - y_bit for f in range(nf)]
    in_kept, in_sent = grad_pair(second, then(d_hidden, out_sent), *by_y, 2)
    in_got = swap(in_sent, "ctx", 2)
    to_x = [2 * f + x_bit for f in range(nf)], [2 * f + 1 - x_bit for f in range(nf)]
    qkv_kept, qkv_sent = grad_pair(first, then(d_packed, in_sent, dense_got), *to_x, 2)
    qkv_got = swap(qkv_sent, "ctx", 1)
    d_half = norm_back(then(x_all, qkv_sent), d_packed, d_hidden, w_qkv, w_in, norms, block, 0)
    rows_kept, rows_sent = add_split(out_kept, then(out_got, d_half[0]), y_bit)
    rows_got = swap(rows_sent, "ctx", 2)
    d_partial, sums = norm_back(
        then(x_all, rows_sent), d_packed, d_hidden, w_qkv, w_in, norms, block, 1, d_half
    )
    def spread_out(values, parts):
        whole = jnp.zeros((parts, nf, values.shape[0] // parts), wide)
        return lax.dynamic_update_slice_in_dim(
            whole, values.reshape(parts, 1, -1), me_f, 1
        ).reshape(nf, -1)

    totals = jnp.concatenate(
        [sums[i].reshape(nf, -1) for i in range(4)]
        + [
            spread_out(jnp.sum(d_packed.astype(wide), axis=0), 3),
            spread_out(hidden_sum[0], 1),
            jnp.sum(g_own.astype(wide), axis=0).reshape(nf, -1),
        ],
        axis=1,
    )
    both_kept, both_sent = add_split_two(
        in_kept, then(in_got, d_partial), dense_kept, dense_got, x_bit
    )
    both_got = swap(both_sent, "ctx", 1)
    qkv_kept2, qkv_sent2 = add_split(qkv_kept, then(qkv_got, both_sent), y_bit)
    qkv_got2 = swap(qkv_sent2, "ctx", 2)
    d_normal = lax.psum_scatter(
        then(d_partial, summed, qkv_sent2, rows_got), "fsdp", scatter_dimension=0, tiled=True
    )

    def with_totals(values):
        rest = jnp.pad(totals.astype(low).reshape(nf, -1, values.shape[2]), ((0, 0), (0, 4), (0, 0)))
        return jnp.concatenate([values, rest], axis=1)

    both_got = then(both_got, rows_got, qkv_got2)
    in_mine = added(both_kept, both_got)
    rows_mine = added(rows_kept, then(rows_got, both_got))
    rows_x, rows_y = swap(rows_mine, "ctx", 1), swap(rows_mine, "ctx", 2)
    in_rows = lax.all_to_all(in_mine[:nf], "fsdp", 0, 0, tiled=True)
    qkv_mine = added(qkv_kept2, then(qkv_got2, both_got, rows_x, rows_y))
    qkv_rows = lax.all_to_all(with_totals(qkv_mine), "fsdp", 0, 0, tiled=True)
    rows_xy = swap(rows_y, "ctx", 1)
    in_rows = jnp.concatenate([then(in_rows, rows_x, rows_y, rows_xy), in_mine[nf:]])
    in_x, in_y = swap(in_rows, "ctx", 1), swap(in_rows, "ctx", 2)
    totals = jnp.sum(qkv_rows[:, part:].astype(wide), axis=0).astype(low)
    totals = jnp.pad(totals, ((0, part - totals.shape[0]), (0, 0)))[None]
    qkv_rows = then(jnp.concatenate([qkv_rows[:, :part], totals]), in_y)
    qkv_x, qkv_y = swap(qkv_rows, "ctx", 1), swap(qkv_rows, "ctx", 2)
    in_xy = swap(then(in_x, qkv_rows), "ctx", 2)
    qkv_xy = swap(qkv_y, "ctx", 1)
    rows_all = [rows_mine, rows_x, rows_y, rows_xy]
    in_all = [in_rows, in_x, in_y, in_xy]
    qkv_all = [qkv_rows, qkv_x, qkv_y, qkv_xy]
    by_x = 2 * (plane % 2) + plane // 2

    def whole_columns(pieces, places, shape, thirds, begin=0, count=nf):
        at_rows = (places[:, None] * jnp.ones((count,), jnp.int32)).reshape(-1)
        at_cols = jnp.tile(jnp.arange(count, dtype=jnp.int32), nc)
        return finish(pieces, at_rows, at_cols, shape, thirds, (begin, count))

    x_wide = x_own.astype(wide)
    d_normal = then(d_normal, qkv_x).astype(wide)
    output = (x_wide + summed.astype(wide) + whole[5] + whole[6]).astype(low).reshape(tokens.shape)
    own_normal, own_rstd = normalised(x_wide)
    d_x = own_rstd * (
        d_normal
        - jnp.mean(d_normal, axis=-1, keepdims=True)
        - own_normal * jnp.mean(d_normal * own_normal, axis=-1, keepdims=True)
    )
    input_grad = (g_own.astype(wide) + d_x).reshape(tokens.shape)

    totals = sum(r[-1, :4].astype(wide) for r in qkv_all).reshape(-1)
    grad_fc_out = whole_columns(rows_all, plane, fc_out_weight.shape, 1, 0, 1)
    grad_dense = whole_columns(in_all, plane, dense_weight.shape, 1, nf, width // units)
    in_all[3] = then(in_all[3], grad_fc_out, grad_dense, input_grad, output)
    grad_fc_in = whole_columns(in_all, plane, fc_in_weight.shape, 1)
    qkv_all[3] = then(qkv_all[3], grad_fc_in)
    grad_qkv = whole_columns(qkv_all, by_x, qkv_weight.shape, 3)

    cuts, start = [], 0
    for size in (rows, rows, rows, rows, 3 * width // nf, units, rows):
        cuts.append(totals[start : start + size])
        start += size
    return (
        output,
        input_grad,
        cuts[0],
        cuts[1],
        cuts[2],
        cuts[3],
        grad_qkv,
        cuts[4],
        grad_dense,
        cuts[6],
        grad_fc_in,
        cuts[5],
        grad_fc_out,
        cuts[6],
    )


def solution(mesh):
    placed = (
        P("fsdp", "ctx", None),
        P("fsdp", "ctx"),
        P("fsdp", "ctx"),
        P("fsdp"),
        P("fsdp"),
        P("fsdp"),
        P("fsdp"),
        P("fsdp", None),
        P("fsdp"),
        P("fsdp", None),
        P("fsdp"),
        P("fsdp", None),
        P("fsdp"),
        P("fsdp", None),
        P("fsdp"),
        P("fsdp", "ctx", None),
    )
    by_head = mesh.shape["fsdp"] == HEADS and mesh.shape["ctx"] == 4
    return jax.shard_map(
        local_by_head if by_head else local,
        mesh=mesh,
        in_specs=placed,
        out_specs=(
            P("fsdp", "ctx", None),
            P("fsdp", "ctx", None),
            P("fsdp"),
            P("fsdp"),
            P("fsdp"),
            P("fsdp"),
            P("fsdp", None),
            P("fsdp"),
            P("fsdp", None),
            P("fsdp"),
            P("fsdp", None),
            P("fsdp"),
            P("fsdp", None),
            P("fsdp"),
        ),
        check_vma=False,
    )
```

```python
import jax
import jax.numpy as jnp
from jax import lax
from jax.experimental import pallas as pl
from jax.experimental.pallas import tpu as pltpu
from jax.sharding import PartitionSpec as P

HEADS = 8


eps_norm = 1e-05


def layer_norm(values, gain_vec, shift_vec):
    row_mean = jnp.mean(values, axis=-1, keepdims=True)
    centred = values - row_mean
    spread = jnp.mean(centred * centred, axis=-1, keepdims=True)
    return centred * lax.rsqrt(spread + eps_norm) * gain_vec + shift_vec


def rotary_tables(position, rotary):
    frequency = 10000.0 ** (-jnp.arange(0, rotary, 2, dtype=jnp.float32) / rotary)
    angles = position.astype(jnp.float32)[:, None] * frequency[None, :]
    angles = jnp.concatenate([angles, angles], axis=-1)
    return (jnp.cos(angles), jnp.sin(angles))


def rotate(values, cosine, sine_table):
    rotary = cosine.shape[-1]
    half_rot = rotary // 2
    turned = jnp.concatenate([-values[..., half_rot:rotary], values[..., :half_rot]], axis=-1)
    rotated_head = values[..., :rotary] * cosine[:, None, :] + turned * sine_table[:, None, :]
    return jnp.concatenate([rotated_head, values[..., rotary:]], axis=-1)


def gelu_exact(tensor):
    return jax.nn.gelu(tensor, approximate=False)


def dot_right(left_side, right_side):
    return lax.dot_general(
        left_side, right_side, (((1,), (1,)), ((), ())), preferred_element_type=jnp.float32
    )


def dot_left(left_side, right_side):
    return lax.dot_general(
        left_side, right_side, (((0,), (0,)), ((), ())), preferred_element_type=jnp.float32
    )


def reduce_grads(weight_one, bias_one, weight_two, bias_two, gain_grad, shift_grad):
    shared = (
        lax.psum_scatter(
            weight_one.astype(jnp.bfloat16), "fsdp", scatter_dimension=0, tiled=True
        ).astype(jnp.float32),
        lax.psum_scatter(
            bias_one.astype(jnp.bfloat16), "fsdp", scatter_dimension=0, tiled=True
        ).astype(jnp.float32),
        lax.psum_scatter(
            weight_two.astype(jnp.bfloat16), "fsdp", scatter_dimension=0, tiled=True
        ).astype(jnp.float32),
        lax.psum_scatter(
            bias_two.astype(jnp.bfloat16), "fsdp", scatter_dimension=0, tiled=True
        ).astype(jnp.float32),
        lax.psum_scatter(
            gain_grad.astype(jnp.bfloat16), "fsdp", scatter_dimension=0, tiled=True
        ).astype(jnp.float32),
        lax.psum_scatter(
            shift_grad.astype(jnp.bfloat16), "fsdp", scatter_dimension=0, tiled=True
        ).astype(jnp.float32),
    )
    return (
        lax.psum(shared[0].astype(jnp.bfloat16), "ctx").astype(jnp.float32),
        lax.psum(shared[1].astype(jnp.bfloat16), "ctx").astype(jnp.float32),
        lax.psum(shared[2].astype(jnp.bfloat16), "ctx").astype(jnp.float32),
        lax.psum(shared[3].astype(jnp.bfloat16), "ctx").astype(jnp.float32),
        lax.psum(shared[4].astype(jnp.bfloat16), "ctx").astype(jnp.float32),
        lax.psum(shared[5].astype(jnp.bfloat16), "ctx").astype(jnp.float32),
    )


def local(
    tokens,
    segments,
    positions,
    ln1_gain,
    ln1_bias,
    ln2_gain,
    ln2_bias,
    qkv_weight,
    qkv_bias,
    dense_weight,
    dense_bias,
    fc_in_weight,
    fc_in_bias,
    fc_out_weight,
    fc_out_bias,
    cotangent,
):
    model_width = tokens.shape[-1]
    values = tokens.reshape(-1, model_width).astype(jnp.float32)
    row_count = values.shape[0]
    head_dim = model_width // HEADS
    score_scale = head_dim ** (-0.5)
    everyone = lax.all_gather(segments, "ctx", axis=1, tiled=True).reshape(-1)
    seq_length = everyone.shape[0]
    own_segment = segments.reshape(-1)
    query_index = lax.axis_index("ctx") * row_count + jnp.arange(row_count, dtype=jnp.int32)
    key_index = jnp.arange(seq_length, dtype=jnp.int32)
    allowed = (own_segment[:, None] == everyone[None, :]) & (
        key_index[None, :] <= query_index[:, None]
    )
    cosine, sine_table = rotary_tables(positions.reshape(-1), head_dim // 4)
    gathered = (
        lax.all_gather(ln1_gain, "fsdp", axis=0, tiled=True),
        lax.all_gather(ln1_bias, "fsdp", axis=0, tiled=True),
        lax.all_gather(ln2_gain, "fsdp", axis=0, tiled=True),
        lax.all_gather(ln2_bias, "fsdp", axis=0, tiled=True),
        lax.all_gather(qkv_weight, "fsdp", axis=0, tiled=True),
        lax.all_gather(qkv_bias, "fsdp", axis=0, tiled=True),
        lax.all_gather(dense_weight, "fsdp", axis=0, tiled=True),
        lax.all_gather(dense_bias, "fsdp", axis=0, tiled=True),
        lax.all_gather(fc_in_weight, "fsdp", axis=0, tiled=True),
        lax.all_gather(fc_in_bias, "fsdp", axis=0, tiled=True),
        lax.all_gather(fc_out_weight, "fsdp", axis=0, tiled=True),
        lax.all_gather(fc_out_bias, "fsdp", axis=0, tiled=True),
    )
    gain_one = gathered[0].astype(jnp.float32)
    shift_one = gathered[1].astype(jnp.float32)
    gain_two = gathered[2].astype(jnp.float32)
    shift_two = gathered[3].astype(jnp.float32)
    normed_one = layer_norm(values, gain_one, shift_one).astype(jnp.bfloat16)
    normed_two = layer_norm(values, gain_two, shift_two).astype(jnp.bfloat16)
    packed = jnp.dot(normed_one, gathered[4], preferred_element_type=jnp.float32) + gathered[
        5
    ].astype(jnp.float32)
    shaped = packed.reshape(row_count, 3, HEADS, head_dim)
    query_low = rotate(shaped[:, 0], cosine, sine_table).astype(jnp.bfloat16)
    key_low = (
        rotate(shaped[:, 1], cosine, sine_table)
        .astype(jnp.bfloat16)
        .reshape(row_count, model_width)
    )
    value_low = shaped[:, 2].astype(jnp.bfloat16).reshape(row_count, model_width)
    keys_all, values_all = (
        lax.all_gather(key_low, "ctx", axis=0, tiled=True),
        lax.all_gather(value_low, "ctx", axis=0, tiled=True),
    )

    def score_block(key_rows):
        raw_scores = jnp.einsum(
            "qhd,khd->hqk",
            query_low,
            key_rows.reshape(seq_length, HEADS, head_dim),
            preferred_element_type=jnp.float32,
        )
        return jnp.where(allowed[None], raw_scores * score_scale, -1e30)

    scores = score_block(keys_all)
    row_max = jnp.max(scores, axis=-1, keepdims=True)
    exp_scores = jnp.exp(scores - row_max)
    row_total = jnp.sum(exp_scores, axis=-1, keepdims=True)
    probs_low = (exp_scores / row_total).astype(jnp.bfloat16)
    log_total = row_max + jnp.log(row_total)
    mixed_heads = jnp.einsum(
        "hqk,khd->qhd",
        probs_low,
        values_all.reshape(seq_length, HEADS, head_dim),
        preferred_element_type=jnp.float32,
    )
    mixed_low = mixed_heads.reshape(row_count, model_width).astype(jnp.bfloat16)
    attn_out = jnp.dot(mixed_low, gathered[6], preferred_element_type=jnp.float32) + gathered[
        7
    ].astype(jnp.float32)
    hidden = jnp.dot(normed_two, gathered[8], preferred_element_type=jnp.float32) + gathered[
        9
    ].astype(jnp.float32)
    active_low = gelu_exact(hidden).astype(jnp.bfloat16)
    mlp_out = jnp.dot(active_low, gathered[10], preferred_element_type=jnp.float32) + gathered[
        11
    ].astype(jnp.float32)
    output = (values + attn_out + mlp_out).astype(jnp.bfloat16).reshape(tokens.shape)
    regathered = (
        lax.all_gather(ln1_gain, "fsdp", axis=0, tiled=True),
        lax.all_gather(ln1_bias, "fsdp", axis=0, tiled=True),
        lax.all_gather(ln2_gain, "fsdp", axis=0, tiled=True),
        lax.all_gather(ln2_bias, "fsdp", axis=0, tiled=True),
        lax.all_gather(qkv_weight, "fsdp", axis=0, tiled=True),
        lax.all_gather(qkv_bias, "fsdp", axis=0, tiled=True),
        lax.all_gather(dense_weight, "fsdp", axis=0, tiled=True),
        lax.all_gather(dense_bias, "fsdp", axis=0, tiled=True),
        lax.all_gather(fc_in_weight, "fsdp", axis=0, tiled=True),
        lax.all_gather(fc_in_bias, "fsdp", axis=0, tiled=True),
        lax.all_gather(fc_out_weight, "fsdp", axis=0, tiled=True),
        lax.all_gather(fc_out_bias, "fsdp", axis=0, tiled=True),
    )
    keys_back, values_back = (
        lax.all_gather(key_low, "ctx", axis=0, tiled=True),
        lax.all_gather(value_low, "ctx", axis=0, tiled=True),
    )
    grad_out = cotangent.reshape(row_count, model_width)
    grad_wide = grad_out.astype(jnp.float32)
    d_active = dot_right(grad_out, regathered[10])
    d_hidden_low = jax.vjp(gelu_exact, hidden)[1](d_active)[0].astype(jnp.bfloat16)
    d_second = dot_right(d_hidden_low, regathered[8])
    d_mixed_low = (
        dot_right(grad_out, regathered[6]).astype(jnp.bfloat16).reshape(row_count, HEADS, head_dim)
    )
    probs_again = jnp.exp(score_block(keys_back) - log_total)
    probs_again_low = probs_again.astype(jnp.bfloat16)
    grad_probs = jnp.einsum(
        "qhd,khd->hqk",
        d_mixed_low,
        values_back.reshape(seq_length, HEADS, head_dim),
        preferred_element_type=jnp.float32,
    )
    row_delta = jnp.sum(probs_again * grad_probs, axis=-1, keepdims=True)
    grad_scores = (probs_again * (grad_probs - row_delta) * score_scale).astype(jnp.bfloat16)
    d_query = jnp.einsum(
        "hqk,khd->qhd",
        grad_scores,
        keys_back.reshape(seq_length, HEADS, head_dim),
        preferred_element_type=jnp.float32,
    )
    d_key = jnp.einsum(
        "hqk,qhd->khd", grad_scores, query_low, preferred_element_type=jnp.float32
    ).reshape(row_count * lax.axis_size("ctx"), model_width)
    d_value = jnp.einsum(
        "hqk,qhd->khd", probs_again_low, d_mixed_low, preferred_element_type=jnp.float32
    ).reshape(row_count * lax.axis_size("ctx"), model_width)
    kv_grad = lax.psum_scatter(
        jnp.concatenate([d_key, d_value], axis=1).astype(jnp.bfloat16),
        "ctx",
        scatter_dimension=0,
        tiled=True,
    ).astype(jnp.float32)
    d_key_own = kv_grad[:, :model_width].reshape(row_count, HEADS, head_dim)
    d_packed = jnp.concatenate(
        [
            rotate(d_query, cosine, -sine_table).reshape(row_count, model_width),
            rotate(d_key_own, cosine, -sine_table).reshape(row_count, model_width),
            kv_grad[:, model_width:],
        ],
        axis=1,
    )
    d_packed_low = d_packed.astype(jnp.bfloat16)
    d_first = dot_right(d_packed_low, regathered[4])
    norm_back_one = jax.vjp(layer_norm, values, gain_one, shift_one)[1]
    d_values_one, d_gain_one, d_shift_one = norm_back_one(d_first)
    norm_back_two = jax.vjp(layer_norm, values, gain_two, shift_two)[1]
    d_values_two, d_gain_two, d_shift_two = norm_back_two(d_second)
    input_grad = (grad_wide + d_values_one + d_values_two).reshape(tokens.shape)
    grad_sum = jnp.sum(grad_wide, axis=0)
    mlp_grads = reduce_grads(
        dot_left(normed_two, d_hidden_low),
        jnp.sum(d_hidden_low.astype(jnp.float32), axis=0),
        dot_left(active_low, grad_out),
        grad_sum,
        d_gain_two,
        d_shift_two,
    )
    attn_grads = reduce_grads(
        dot_left(normed_one, d_packed_low),
        jnp.sum(d_packed_low.astype(jnp.float32), axis=0),
        dot_left(mixed_low, grad_out),
        grad_sum,
        d_gain_one,
        d_shift_one,
    )
    return (
        output,
        input_grad,
        attn_grads[4],
        attn_grads[5],
        mlp_grads[4],
        mlp_grads[5],
        attn_grads[0],
        attn_grads[1],
        attn_grads[2],
        attn_grads[3],
        mlp_grads[0],
        mlp_grads[1],
        mlp_grads[2],
        mlp_grads[3],
    )


LANES = 128
FAST = pltpu.CompilerParams(vmem_limit_bytes=56 * 1024 * 1024)
SMALL = pl.CostEstimate(flops=1, bytes_accessed=1, transcendentals=0)
ANY = pl.BlockSpec(memory_space=pl.ANY)
SCALARS = pl.BlockSpec(memory_space=pltpu.SMEM)
WHOLE = pl.BlockSpec(memory_space=pltpu.VMEM)
low = jnp.bfloat16
wide = jnp.float32


def dot(a, b, left=1, right=0):
    return lax.dot_general(a, b, (((left,), (right,)), ((), ())), preferred_element_type=wide)


def swap(values, axis, mask):
    return lax.ppermute(values, axis, [(i, i ^ mask) for i in range(lax.axis_size(axis))])


def at(values, index, axis=0):
    return lax.dynamic_index_in_dim(values, index, axis, keepdims=False)


def added(*values):
    total = values[0].astype(wide)
    for v in values[1:]:
        total = total + v.astype(wide)
    return total.astype(low)


def then(value, *events):
    return lax.optimization_barrier((value,) + events)[0]


def gather_plane(first, second):
    first_x, second_y = swap(first, "ctx", 1), swap(second, "ctx", 2)
    first_y, second_x = swap(first, "ctx", 2), swap(second, "ctx", 1)
    first_xy = swap(first_y, "ctx", 1)
    second_xy = swap(second_x, "ctx", 2)
    return [first, first_x, first_y, first_xy], [second, second_x, second_y, second_xy]


def place(pieces, places, count):
    sizes = [p.shape[0] for p in pieces]

    total = sum(sizes)

    def body(places_ref, *refs):
        out, buf, sems_in, sems_out = refs[-4:]
        copies = []
        for ref, size in zip(refs, sizes):
            for i in range(size):
                n = len(copies)
                copies.append(pltpu.make_async_copy(ref.at[i], buf.at[n], sems_in.at[n]))
                copies[n].start()
        leaving = []
        for n in range(total):
            copies[n].wait()
            copy = pltpu.make_async_copy(buf.at[n], out.at[places_ref[n]], sems_out.at[n])
            copy.start()
            leaving.append(copy)
        for copy in leaving:
            copy.wait()

    return pl.pallas_call(
        body,
        name="place",
        out_shape=jax.ShapeDtypeStruct((count,) + pieces[0].shape[1:], pieces[0].dtype),
        in_specs=[SCALARS] + [ANY] * len(pieces),
        out_specs=ANY,
        scratch_shapes=[
            pltpu.VMEM((total,) + pieces[0].shape[1:], pieces[0].dtype),
            pltpu.SemaphoreType.DMA((total,)),
            pltpu.SemaphoreType.DMA((total,)),
        ],
        compiler_params=FAST,
        cost_estimate=SMALL,
    )(places, *pieces)


def cut_weights(qkv_weight, fc_in_weight, extra, places, hd, units, part):
    span = qkv_weight.shape[1] // 3
    cols = 3 * hd + units

    def body(places_ref, qkv_ref, in_ref, extra_ref, *refs):
        outs, buf, sems_in, sems_out = refs[:4], refs[4], refs[5], refs[6]
        row = pl.ds(pl.multiple_of(places_ref[8] * part, part), part)
        copies = []
        for n in range(8):
            f = places_ref[n]
            for t in range(3):
                copies.append(
                    pltpu.make_async_copy(
                        qkv_ref.at[row, pl.ds(pl.multiple_of(t * span + f * hd, LANES), hd)],
                        buf.at[n, :, pl.ds(t * hd, hd)],
                        sems_in.at[len(copies)],
                    )
                )
                copies[-1].start()
            copies.append(
                pltpu.make_async_copy(
                    in_ref.at[row, pl.ds(pl.multiple_of(f * units, LANES), units)],
                    buf.at[n, :, pl.ds(3 * hd, units)],
                    sems_in.at[len(copies)],
                )
            )
            copies[-1].start()
            copies.append(
                pltpu.make_async_copy(
                    extra_ref, buf.at[n, :, pl.ds(cols, LANES)], sems_in.at[len(copies)]
                )
            )
            copies[-1].start()
        leaving = []
        for n in range(8):
            for copy in copies[5 * n : 5 * n + 5]:
                copy.wait()
            copy = pltpu.make_async_copy(buf.at[n], outs[n % 4].at[n // 4], sems_out.at[n])
            copy.start()
            leaving.append(copy)
        for copy in leaving:
            copy.wait()

    return pl.pallas_call(
        body,
        name="cut_weights",
        out_shape=[jax.ShapeDtypeStruct((2, part, cols + LANES), low)] * 4,
        in_specs=[SCALARS, ANY, ANY, ANY],
        out_specs=[ANY] * 4,
        scratch_shapes=[
            pltpu.VMEM((8, part, cols + LANES), low),
            pltpu.SemaphoreType.DMA((40,)),
            pltpu.SemaphoreType.DMA((8,)),
        ],
        compiler_params=FAST,
        cost_estimate=SMALL,
    )(places, qkv_weight, fc_in_weight, extra)


def finish(pieces, rows_at, cols_at, shape, thirds=1, chosen=None):
    begin, size = chosen or (0, pieces[0].shape[0])
    total = size * len(pieces)
    rows, cols = pieces[0].shape[1:]
    span = cols // thirds

    def body(rows_ref, cols_ref, *refs):
        out, narrow, full, sems_in, sems_out = refs[-5:]
        copies = []
        for ref in refs[: len(pieces)]:
            for i in range(begin, begin + size):
                n = len(copies)
                copies.append(pltpu.make_async_copy(ref.at[i], narrow.at[n], sems_in.at[n]))
                copies[n].start()
        leaving = []
        for n in range(total):
            copies[n].wait()
            full[n] = narrow[n].astype(wide)
            row = pl.ds(pl.multiple_of(rows_ref[n] * rows, rows), rows)
            for t in range(thirds):
                start = t * (shape[1] // thirds) + cols_ref[n] * span
                copy = pltpu.make_async_copy(
                    full.at[n, :, pl.ds(t * span, span)],
                    out.at[row, pl.ds(pl.multiple_of(start, LANES), span)],
                    sems_out.at[n * thirds + t],
                )
                copy.start()
                leaving.append(copy)
        for copy in leaving:
            copy.wait()

    return pl.pallas_call(
        body,
        name="finish",
        out_shape=jax.ShapeDtypeStruct(shape, wide),
        in_specs=[SCALARS, SCALARS] + [ANY] * len(pieces),
        out_specs=ANY,
        scratch_shapes=[
            pltpu.VMEM((total, rows, cols), low),
            pltpu.VMEM((total, rows, cols), wide),
            pltpu.SemaphoreType.DMA((total,)),
            pltpu.SemaphoreType.DMA((total * thirds,)),
        ],
        compiler_params=FAST,
        cost_estimate=SMALL,
    )(rows_at, cols_at, *pieces)


def normalised(values):
    centred = values - jnp.mean(values, axis=-1, keepdims=True)
    spread = jnp.mean(centred * centred, axis=-1, keepdims=True)
    rstd = lax.rsqrt(spread + eps_norm)
    return centred * rstd, rstd


def turn_tables(position, rotary):
    cosine, sine = rotary_tables(position, rotary)
    half = rotary // 2
    zero = jnp.zeros((position.shape[0], LANES - rotary), wide)
    none = jnp.zeros_like(sine[:, :half])
    return (
        jnp.concatenate([cosine, zero + 1.0], axis=1),
        jnp.concatenate([-sine[:, :half], none, zero], axis=1),
        jnp.concatenate([none, sine[:, half:], zero], axis=1),
    )


def turn(values, here, above, below, half):
    return (
        values * here
        + pltpu.roll(values, LANES - half, 1) * above
        + pltpu.roll(values, half, 1) * below
    )


def project(x_all, weight, bias, norms, tables, block, hd):
    group, width = x_all.shape
    cols = weight.shape[1]
    half = hd // 8

    def body(x_ref, w_ref, b_ref, n_ref, t0, t1, t2, first_ref, second_ref, out_ref):
        normal, _ = normalised(x_ref[...].astype(wide))
        first = (normal * n_ref[0:1] + n_ref[1:2]).astype(low)
        second_ref[...] = (normal * n_ref[2:3] + n_ref[3:4]).astype(low)
        first_ref[...] = first
        packed = dot(first, w_ref[...]) + b_ref[...]
        for i in range(3):
            lead = packed[:, i * hd : i * hd + LANES]
            if i < 2:
                lead = turn(lead, t0[...], t1[...], t2[...], half)
            out_ref[:, i * hd : i * hd + LANES] = lead.astype(low)
            out_ref[:, i * hd + LANES : (i + 1) * hd] = packed[
                :, i * hd + LANES : (i + 1) * hd
            ].astype(low)

    row = lambda n: pl.BlockSpec((block, n), lambda i: (i, 0))
    return pl.pallas_call(
        body,
        name="project",
        grid=(group // block,),
        in_specs=[row(width), WHOLE, WHOLE, WHOLE, row(LANES), row(LANES), row(LANES)],
        out_specs=[row(width), row(width), row(cols)],
        out_shape=[
            jax.ShapeDtypeStruct((group, width), low),
            jax.ShapeDtypeStruct((group, width), low),
            jax.ShapeDtypeStruct((group, cols), low),
        ],
        compiler_params=FAST,
        cost_estimate=SMALL,
    )(x_all, weight, bias, norms, *tables)


def expand(second, weight, bias, block):
    group, width = second.shape
    cols = weight.shape[1]

    def body(s_ref, w_ref, b_ref, active_ref, slope_ref):
        hidden = dot(s_ref[...], w_ref[...]) + b_ref[...]
        upper = 0.5 * (1.0 + lax.erf(hidden * (0.5**0.5)))
        active_ref[...] = (hidden * upper).astype(low)
        bell = jnp.exp(-0.5 * hidden * hidden) * ((2.0 * jnp.pi) ** -0.5)
        slope_ref[...] = (upper + hidden * bell).astype(low)

    row = lambda n: pl.BlockSpec((block, n), lambda i: (i, 0))
    return pl.pallas_call(
        body,
        name="expand",
        grid=(group // block,),
        in_specs=[row(width), WHOLE, WHOLE],
        out_specs=[row(cols), row(cols)],
        out_shape=[jax.ShapeDtypeStruct((group, cols), low)] * 2,
        compiler_params=FAST,
        cost_estimate=SMALL,
    )(second, weight, bias)


def contract(left, weight, block, more=None):
    group = left.shape[0]
    width = weight.shape[1]

    def body(left_ref, weight_ref, *refs):
        total = dot(left_ref[...], weight_ref[...])
        if more is not None:
            total = total + refs[0][...].astype(wide)
        refs[-1][...] = total.astype(low)

    row = lambda n: pl.BlockSpec((block, n), lambda i: (i, 0))
    return pl.pallas_call(
        body,
        name="contract",
        grid=(group // block,),
        in_specs=[row(left.shape[1]), WHOLE] + ([] if more is None else [row(width)]),
        out_specs=row(width),
        out_shape=jax.ShapeDtypeStruct((group, width), low),
        compiler_params=FAST,
        cost_estimate=SMALL,
    )(left, weight, *(() if more is None else (more,)))


def hidden_back(g_all, fc_out_weight, slope, block):
    group, width = g_all.shape
    units = fc_out_weight.shape[0]

    def body(g_ref, w_ref, s_ref, out_ref, sum_ref):
        @pl.when(pl.program_id(0) == 0)
        def _():
            sum_ref[...] = jnp.zeros_like(sum_ref)

        d_hidden = (dot(g_ref[...], w_ref[...], 1, 1) * s_ref[...].astype(wide)).astype(low)
        out_ref[...] = d_hidden
        sum_ref[...] += jnp.sum(d_hidden.astype(wide), axis=0, keepdims=True)

    row = lambda n: pl.BlockSpec((block, n), lambda i: (i, 0))
    return pl.pallas_call(
        body,
        name="hidden_back",
        grid=(group // block,),
        in_specs=[row(width), WHOLE, row(units)],
        out_specs=[row(units), pl.BlockSpec((1, units), lambda i: (0, 0))],
        out_shape=[
            jax.ShapeDtypeStruct((group, units), low),
            jax.ShapeDtypeStruct((1, units), wide),
        ],
        compiler_params=FAST,
        cost_estimate=SMALL,
    )(g_all, fc_out_weight, slope)


def grad_pair(left, right, keep, send, parts):
    tokens = left.shape[0]
    cols = right.shape[1]
    n = len(keep)
    size = LANES // parts

    def body(keep_ref, send_ref, a_ref, b_ref, right_ref, keep_out, send_out):
        both = jnp.concatenate([a_ref[...], b_ref[...]], axis=1)
        result = dot(both, right_ref[...], 0, 0).astype(low)
        keep_out[...] = result[:LANES].reshape(1, parts, size, cols)
        send_out[...] = result[LANES:].reshape(1, parts, size, cols)

    shape = jax.ShapeDtypeStruct((n, parts, size, cols), low)
    out = pl.BlockSpec((1, parts, size, cols), lambda i, k, s: (i, 0, 0, 0))
    return pl.pallas_call(
        body,
        name="grad_pair",
        grid_spec=pltpu.PrefetchScalarGridSpec(
            num_scalar_prefetch=2,
            grid=(n,),
            in_specs=[
                pl.BlockSpec((tokens, LANES), lambda i, k, s: (0, k[i])),
                pl.BlockSpec((tokens, LANES), lambda i, k, s: (0, s[i])),
                pl.BlockSpec((tokens, cols), lambda i, k, s: (0, 0)),
            ],
            out_specs=[out, out],
        ),
        out_shape=[shape, shape],
        compiler_params=FAST,
        cost_estimate=SMALL,
    )(jnp.stack(keep).astype(jnp.int32), jnp.stack(send).astype(jnp.int32), left, left, right)


def add_split(kept, got, bit):
    n, _, rows, cols = kept.shape

    def body(bit_ref, a_ref, b_ref, keep_out, send_out):
        for out, half in ((keep_out, bit_ref[0]), (send_out, 1 - bit_ref[0])):
            out[...] = (a_ref[:, half].astype(wide) + b_ref[:, half].astype(wide)).astype(low)

    shape = jax.ShapeDtypeStruct((n, rows, cols), low)
    both = pl.BlockSpec((n // 2 if n > 1 else 1, 2, rows, cols), lambda i: (i, 0, 0, 0))
    out = pl.BlockSpec((n // 2 if n > 1 else 1, rows, cols), lambda i: (i, 0, 0))
    return pl.pallas_call(
        body,
        name="add_split",
        grid=(2 if n > 1 else 1,),
        in_specs=[SCALARS, both, both],
        out_specs=[out, out],
        out_shape=[shape, shape],
        compiler_params=FAST,
        cost_estimate=SMALL,
    )(bit[None].astype(jnp.int32), kept, got)


def add_split_two(kept, got, other_kept, other_got, bit):
    n, _, rows, cols = kept.shape
    more = other_kept.shape[3] // cols

    def body(bit_ref, a_ref, b_ref, c_ref, d_ref, keep_out, send_out):
        for out, half in ((keep_out, bit_ref[0]), (send_out, 1 - bit_ref[0])):
            out[:n] = (a_ref[:, half].astype(wide) + b_ref[:, half].astype(wide)).astype(low)
            other = (c_ref[0, half].astype(wide) + d_ref[0, half].astype(wide)).astype(low)
            for i in range(more):
                out[n + i] = other[:, i * cols : (i + 1) * cols]

    shape = jax.ShapeDtypeStruct((n + more, rows, cols), low)
    return pl.pallas_call(
        body,
        name="add_split_two",
        in_specs=[SCALARS] + [WHOLE] * 4,
        out_specs=[WHOLE] * 2,
        out_shape=[shape, shape],
        compiler_params=FAST,
        cost_estimate=SMALL,
    )(bit[None].astype(jnp.int32), kept, got, other_kept, other_got)


def fetch(source, target, sems):
    count, sequences, block, _ = source.shape
    copies = []
    for m in range(count):
        for s in range(sequences):
            n = len(copies)
            copies.append(
                pltpu.make_async_copy(
                    source.at[m, s], target.at[s, pl.ds(m * block, block)], sems.at[n]
                )
            )
            copies[n].start()
    return copies


def block_scores(buf, row_ref, col_ref, s, i, block, hd, scale):
    count = (i + 1) * block
    query = buf[s, i * block : count, 0:hd]
    key = buf[s, 0:count, hd : 2 * hd]
    scores = dot(query, key, 1, 1) * scale
    q_index = lax.broadcasted_iota(jnp.int32, (block, count), 0) + i * block
    k_index = lax.broadcasted_iota(jnp.int32, (block, count), 1)
    allowed = (col_ref[s, i * block : count, :] == row_ref[s, :, 0:count]) & (k_index <= q_index)
    scores = jnp.where(allowed, scores, -1e30)
    probs = jnp.exp(scores - jnp.max(scores, axis=-1, keepdims=True))
    return query, key, probs / jnp.sum(probs, axis=-1, keepdims=True)


def attend(parts, seg_row, seg_col, hd):
    count, sequences, block, cols = parts.shape
    scale = hd ** (-0.5)

    def body(row_ref, col_ref, parts_ref, out, buf, mixed, sems_in, sem_out):
        for copy in fetch(parts_ref, buf, sems_in):
            copy.wait()
        for s in range(sequences):
            for i in range(count):
                _, _, probs = block_scores(buf, row_ref, col_ref, s, i, block, hd, scale)
                value = buf[s, 0 : (i + 1) * block, 2 * hd : 3 * hd]
                mixed[i, s] = dot(probs.astype(low), value).astype(low)
        copy = pltpu.make_async_copy(mixed, out, sem_out)
        copy.start()
        copy.wait()

    return pl.pallas_call(
        body,
        name="attend",
        out_shape=jax.ShapeDtypeStruct((count, sequences, block, hd), low),
        in_specs=[WHOLE, WHOLE, ANY],
        out_specs=ANY,
        scratch_shapes=[
            pltpu.VMEM((sequences, count * block, cols), low),
            pltpu.VMEM((count, sequences, block, hd), low),
            pltpu.SemaphoreType.DMA((count * sequences,)),
            pltpu.SemaphoreType.DMA,
        ],
        compiler_params=FAST,
        cost_estimate=SMALL,
    )(seg_row, seg_col, parts)


def attend_back(parts, d_parts, seg_row, seg_col, tables, hd):
    count, sequences, block, cols = parts.shape
    length = count * block
    scale = hd ** (-0.5)
    half = hd // 8

    def body(row_ref, col_ref, t0, t1, t2, parts_ref, d_ref, out, *scratch):
        buf, d_buf, key_sum, value_sum, done, sems_in, sems_d, sem_out = scratch
        for copy in fetch(parts_ref, buf, sems_in) + fetch(d_ref, d_buf, sems_d):
            copy.wait()

        def put(values, s, i, which):
            lead = values[:, 0:LANES]
            if which < 2:
                rows = slice(i * block, (i + 1) * block)
                lead = turn(lead, t0[s, rows], -t1[s, rows], -t2[s, rows], half)
            done[i, s, :, which * hd : which * hd + LANES] = lead.astype(low)
            done[i, s, :, which * hd + LANES : (which + 1) * hd] = values[:, LANES:].astype(low)

        for s in range(sequences):
            for i in reversed(range(count)):
                n = (i + 1) * block
                query, key, probs = block_scores(buf, row_ref, col_ref, s, i, block, hd, scale)
                value = buf[s, 0:n, 2 * hd : 3 * hd]
                d_out = d_buf[s, i * block : n]
                d_probs = dot(d_out, value, 1, 1)
                delta = jnp.sum(probs * d_probs, axis=-1, keepdims=True)
                d_scores = (probs * (d_probs - delta) * scale).astype(low)
                put(dot(d_scores, key), s, i, 0)
                key_part = dot(d_scores, query, 0, 0)
                value_part = dot(probs.astype(low), d_out, 0, 0)
                if i == count - 1:
                    key_sum[...] = key_part
                    value_sum[...] = value_part
                else:
                    key_sum[0:n] += key_part
                    value_sum[0:n] += value_part
                put(key_sum[i * block : n], s, i, 1)
                put(value_sum[i * block : n], s, i, 2)
        copy = pltpu.make_async_copy(done, out, sem_out)
        copy.start()
        copy.wait()

    return pl.pallas_call(
        body,
        name="attend_back",
        out_shape=jax.ShapeDtypeStruct((count, sequences, block, cols), low),
        in_specs=[WHOLE] * 5 + [ANY] * 2,
        out_specs=ANY,
        scratch_shapes=[
            pltpu.VMEM((sequences, length, cols), low),
            pltpu.VMEM((sequences, length, hd), low),
            pltpu.VMEM((length, hd), wide),
            pltpu.VMEM((length, hd), wide),
            pltpu.VMEM((count, sequences, block, cols), low),
            pltpu.SemaphoreType.DMA((count * sequences,)),
            pltpu.SemaphoreType.DMA((count * sequences,)),
            pltpu.SemaphoreType.DMA,
        ],
        compiler_params=FAST,
        cost_estimate=SMALL,
    )(seg_row, seg_col, *tables, parts, d_parts)


def norm_back(x_all, d_packed, d_hidden, w_qkv, w_in, gains, block, half, before=()):
    group, width = x_all.shape
    steps = group // block // 2

    def body(x_ref, p_ref, h_ref, w1_ref, w2_ref, g_ref, *refs):
        out_ref, sums_ref = refs[-2:]

        @pl.when(pl.program_id(0) == 0)
        def _():
            sums_ref[...] = refs[1][...] if before else jnp.zeros_like(sums_ref)

        normal, _ = normalised(x_ref[...].astype(wide))
        one = dot(p_ref[...], w1_ref[...], 1, 1)
        two = dot(h_ref[...], w2_ref[...], 1, 1)
        out_ref[...] = (one * g_ref[0:1] + two * g_ref[2:3]).astype(low)
        sums_ref[0:1] += jnp.sum(one * normal, axis=0, keepdims=True)
        sums_ref[1:2] += jnp.sum(one, axis=0, keepdims=True)
        sums_ref[2:3] += jnp.sum(two * normal, axis=0, keepdims=True)
        sums_ref[3:4] += jnp.sum(two, axis=0, keepdims=True)

    row = lambda n: pl.BlockSpec((block, n), lambda i: (i + half * steps, 0))
    return pl.pallas_call(
        body,
        name="norm_back",
        grid=(steps,),
        in_specs=[row(width), row(d_packed.shape[1]), row(d_hidden.shape[1])] + [WHOLE] * 3
        + ([ANY, WHOLE] if before else []),
        out_specs=[row(width), pl.BlockSpec((4, width), lambda i: (0, 0))],
        out_shape=[
            jax.ShapeDtypeStruct((group, width), low),
            jax.ShapeDtypeStruct((4, width), wide),
        ],
        input_output_aliases={6: 0} if before else {},
        compiler_params=FAST,
        cost_estimate=SMALL,
    )(x_all, d_packed, d_hidden, w_qkv, w_in, gains, *before)


def local_by_head(
    tokens,
    segments,
    positions,
    ln1_gain,
    ln1_bias,
    ln2_gain,
    ln2_bias,
    qkv_weight,
    qkv_bias,
    dense_weight,
    dense_bias,
    fc_in_weight,
    fc_in_bias,
    fc_out_weight,
    fc_out_bias,
    cotangent,
):
    width = tokens.shape[-1]
    block = tokens.shape[1]
    nf = lax.axis_size("fsdp")
    nc = lax.axis_size("ctx")
    me_c = lax.axis_index("ctx")
    me_f = lax.axis_index("fsdp")
    hd = width // HEADS
    units = fc_in_weight.shape[1] // nf
    group = nf * block
    length = nc * block
    rows = width // nf
    part = rows // nc
    x_own = tokens.reshape(block, width)
    g_own = cotangent.reshape(block, width)
    order = jnp.array([2 * j + kk for kk in range(2) for j in range(4)], jnp.int32)
    owners = jnp.bitwise_xor(order, me_f)
    plane = jnp.bitwise_xor(jnp.arange(nc, dtype=jnp.int32), me_c)

    ints = jnp.concatenate([segments, positions], axis=0)
    digits = jnp.concatenate([ints // 32, ints % 32]).astype(low)
    vectors = [ln1_gain, ln1_bias, ln2_gain, ln2_bias, qkv_bias, dense_bias, fc_out_bias]
    sizes = [v.shape[0] for v in vectors]
    extra = jnp.concatenate([digits.reshape(-1)] + vectors)
    extra = jnp.pad(extra, (0, part * LANES - extra.shape[0])).reshape(part, LANES)

    pieces = cut_weights(
        qkv_weight,
        fc_in_weight,
        extra,
        jnp.concatenate([owners, me_c[None]]).astype(jnp.int32),
        hd,
        units,
        part,
    )
    got = [pieces[0]] + [swap(pieces[j], "fsdp", 2 * j) for j in (1, 2, 3)]
    x_all = lax.all_gather(then(x_own, *got), "fsdp", axis=0, tiled=True)
    across = swap(jnp.stack([g[1] for g in got]), "fsdp", 1)
    g_all = lax.all_gather(then(g_own, across), "fsdp", axis=0, tiled=True)
    quarter = jnp.concatenate([jnp.stack([g[0] for g in got]), across])
    cols = 3 * hd + units
    qkv_parts, in_parts = gather_plane(quarter[..., : 3 * hd], quarter[..., 3 * hd : cols])

    back = (jnp.arange(nf, dtype=jnp.int32)[:, None] == owners[None, :]).astype(low)
    small = dot(back, quarter[..., cols:].reshape(nf, part * LANES))
    count = 4 * block
    digits = small[:, :count].astype(jnp.int32).reshape(nf, 2, 2, block)
    numbers = digits[:, 0] * 32 + digits[:, 1]
    position_group = numbers[:, 1].reshape(group)
    of_chip = numbers.reshape(4, 2, 2, block)
    seq_ints = [at(of_chip, me_c)] + [swap(at(of_chip, plane[m]), "ctx", m) for m in range(1, nc)]
    seq_ints = jnp.stack(seq_ints, axis=2)
    seq_ints = jnp.stack([at(seq_ints, plane[b], 2) for b in range(nc)], axis=2)
    seq_ints = seq_ints.reshape(2, 2, length)
    seg_row = seq_ints[:, 0][:, None, :]
    seg_col = seq_ints[:, 0][:, :, None]
    tables = turn_tables(position_group, hd // 4)
    seq_tables = [
        t.reshape(2, length, LANES) for t in turn_tables(seq_ints[:, 1].reshape(-1), hd // 4)
    ]
    whole, start = [], count
    for size in sizes:
        whole.append(small[:, start : start + size].reshape(-1))
        start += size
    norms = jnp.stack(whole[:4])
    head_bias = at(whole[4].reshape(3, nf, hd), me_f, 1).reshape(1, -1)

    row_places = (owners[None, :] * nc + plane[:, None]).reshape(-1)
    w_qkv = place(qkv_parts, row_places, nf * nc).reshape(width, 3 * hd)
    w_in = place(in_parts, row_places, nf * nc).reshape(width, units)

    first, second, packed = project(
        then(x_all, w_in), w_qkv, head_bias, norms, tables, block, hd
    )

    def to_sequences(values):
        return lax.all_to_all(
            values.reshape(4, 2, block, values.shape[1]), "ctx", 0, 0, tiled=True
        )

    def to_group(values):
        moved = lax.all_to_all(values, "ctx", 0, 0, tiled=True)
        return moved.reshape(group, values.shape[-1])

    parts = to_sequences(packed)
    active, slope = expand(
        then(second, packed), w_in, fc_in_bias.astype(wide).reshape(1, -1), block
    )
    mlp = contract(active, fc_out_weight, 2 * block)
    o = attend(then(parts, mlp), seg_row, seg_col, hd)
    o_back = to_group(o)
    x_bit, y_bit = me_c % 2, me_c // 2
    d_o = dot(then(g_all, o), dense_weight, 1, 1).astype(low)
    d_parts = to_sequences(d_o)
    partial = contract(then(o_back, d_o), dense_weight, 2 * block, mlp)
    dense_kept, dense_sent = grad_pair(o_back, then(g_all, partial), [y_bit], [1 - y_bit], 2)
    dense_got = swap(dense_sent, "ctx", 2)
    d_qkv = attend_back(
        parts, then(d_parts, dense_sent), seg_row, seg_col, seq_tables, hd
    )
    d_packed = to_group(d_qkv)
    summed = lax.psum_scatter(then(partial, d_qkv), "fsdp", scatter_dimension=0, tiled=True)

    rows_of = units // (nc * LANES)
    blocks = [((2 * y) * rows_of, s) for y in range(2) for s in range(rows_of)]
    d_hidden, hidden_sum = hidden_back(then(g_all, d_qkv), fc_out_weight, slope, 2 * block)
    out_kept, out_sent = grad_pair(
        active,
        then(g_all, d_hidden),
        [b + x_bit * rows_of + s for b, s in blocks],
        [b + (1 - x_bit) * rows_of + s for b, s in blocks],
        1,
    )
    out_shape = (1, 2, rows_of * LANES, width)
    out_got = swap(out_sent.reshape(out_shape), "ctx", 1)
    out_kept = out_kept.reshape(out_shape)
    by_y = [2 * f + y_bit for f in range(nf)], [2 * f + 1 - y_bit for f in range(nf)]
    in_kept, in_sent = grad_pair(second, then(d_hidden, out_sent), *by_y, 2)
    in_got = swap(in_sent, "ctx", 2)
    to_x = [2 * f + x_bit for f in range(nf)], [2 * f + 1 - x_bit for f in range(nf)]
    qkv_kept, qkv_sent = grad_pair(first, then(d_packed, in_sent, dense_got), *to_x, 2)
    qkv_got = swap(qkv_sent, "ctx", 1)
    d_half = norm_back(then(x_all, qkv_sent), d_packed, d_hidden, w_qkv, w_in, norms, block, 0)
    rows_kept, rows_sent = add_split(out_kept, then(out_got, d_half[0]), y_bit)
    rows_got = swap(rows_sent, "ctx", 2)
    d_partial, sums = norm_back(
        then(x_all, rows_sent), d_packed, d_hidden, w_qkv, w_in, norms, block, 1, d_half
    )
    def spread_out(values, parts):
        whole = jnp.zeros((parts, nf, values.shape[0] // parts), wide)
        return lax.dynamic_update_slice_in_dim(
            whole, values.reshape(parts, 1, -1), me_f, 1
        ).reshape(nf, -1)

    totals = jnp.concatenate(
        [sums[i].reshape(nf, -1) for i in range(4)]
        + [
            spread_out(jnp.sum(d_packed.astype(wide), axis=0), 3),
            spread_out(hidden_sum[0], 1),
            jnp.sum(g_own.astype(wide), axis=0).reshape(nf, -1),
        ],
        axis=1,
    )
    both_kept, both_sent = add_split_two(
        in_kept, then(in_got, d_partial), dense_kept, dense_got, x_bit
    )
    both_got = swap(both_sent, "ctx", 1)
    qkv_kept2, qkv_sent2 = add_split(qkv_kept, then(qkv_got, both_sent), y_bit)
    qkv_got2 = swap(qkv_sent2, "ctx", 2)
    d_normal = lax.psum_scatter(
        then(d_partial, summed, qkv_sent2, rows_got), "fsdp", scatter_dimension=0, tiled=True
    )

    def with_totals(values):
        rest = jnp.pad(totals.astype(low).reshape(nf, -1, values.shape[2]), ((0, 0), (0, 4), (0, 0)))
        return jnp.concatenate([values, rest], axis=1)

    both_got = then(both_got, rows_got, qkv_got2)
    in_mine = added(both_kept, both_got)
    rows_mine = added(rows_kept, then(rows_got, both_got))
    rows_x, rows_y = swap(rows_mine, "ctx", 1), swap(rows_mine, "ctx", 2)
    in_rows = lax.all_to_all(in_mine[:nf], "fsdp", 0, 0, tiled=True)
    qkv_mine = added(qkv_kept2, then(qkv_got2, both_got, rows_x, rows_y))
    qkv_rows = lax.all_to_all(with_totals(qkv_mine), "fsdp", 0, 0, tiled=True)
    rows_xy = swap(rows_y, "ctx", 1)
    in_rows = jnp.concatenate([then(in_rows, rows_x, rows_y, rows_xy), in_mine[nf:]])
    in_x, in_y = swap(in_rows, "ctx", 1), swap(in_rows, "ctx", 2)
    totals = jnp.sum(qkv_rows[:, part:].astype(wide), axis=0).astype(low)
    totals = jnp.pad(totals, ((0, part - totals.shape[0]), (0, 0)))[None]
    qkv_rows = then(jnp.concatenate([qkv_rows[:, :part], totals]), in_y)
    qkv_x, qkv_y = swap(qkv_rows, "ctx", 1), swap(qkv_rows, "ctx", 2)
    in_xy = swap(then(in_x, qkv_rows), "ctx", 2)
    qkv_xy = swap(qkv_y, "ctx", 1)
    rows_all = [rows_mine, rows_x, rows_y, rows_xy]
    in_all = [in_rows, in_x, in_y, in_xy]
    qkv_all = [qkv_rows, qkv_x, qkv_y, qkv_xy]
    by_x = 2 * (plane % 2) + plane // 2

    def whole_columns(pieces, places, shape, thirds, begin=0, count=nf):
        at_rows = (places[:, None] * jnp.ones((count,), jnp.int32)).reshape(-1)
        at_cols = jnp.tile(jnp.arange(count, dtype=jnp.int32), nc)
        return finish(pieces, at_rows, at_cols, shape, thirds, (begin, count))

    x_wide = x_own.astype(wide)
    d_normal = then(d_normal, qkv_x).astype(wide)
    output = (x_wide + summed.astype(wide) + whole[5] + whole[6]).astype(low).reshape(tokens.shape)
    own_normal, own_rstd = normalised(x_wide)
    d_x = own_rstd * (
        d_normal
        - jnp.mean(d_normal, axis=-1, keepdims=True)
        - own_normal * jnp.mean(d_normal * own_normal, axis=-1, keepdims=True)
    )
    input_grad = (g_own.astype(wide) + d_x).reshape(tokens.shape)

    totals = sum(r[-1, :4].astype(wide) for r in qkv_all).reshape(-1)
    grad_fc_out = whole_columns(rows_all, plane, fc_out_weight.shape, 1, 0, 1)
    grad_dense = whole_columns(in_all, plane, dense_weight.shape, 1, nf, width // units)
    in_all[3] = then(in_all[3], grad_fc_out, grad_dense, input_grad, output)
    grad_fc_in = whole_columns(in_all, plane, fc_in_weight.shape, 1)
    qkv_all[3] = then(qkv_all[3], grad_fc_in)
    grad_qkv = whole_columns(qkv_all, by_x, qkv_weight.shape, 3)

    cuts, start = [], 0
    for size in (rows, rows, rows, rows, 3 * width // nf, units, rows):
        cuts.append(totals[start : start + size])
        start += size
    return (
        output,
        input_grad,
        cuts[0],
        cuts[1],
        cuts[2],
        cuts[3],
        grad_qkv,
        cuts[4],
        grad_dense,
        cuts[6],
        grad_fc_in,
        cuts[5],
        grad_fc_out,
        cuts[6],
    )


def solution(mesh):
    placed = (
        P("fsdp", "ctx", None),
        P("fsdp", "ctx"),
        P("fsdp", "ctx"),
        P("fsdp"),
        P("fsdp"),
        P("fsdp"),
        P("fsdp"),
        P("fsdp", None),
        P("fsdp"),
        P("fsdp", None),
        P("fsdp"),
        P("fsdp", None),
        P("fsdp"),
        P("fsdp", None),
        P("fsdp"),
        P("fsdp", "ctx", None),
    )
    by_head = mesh.shape["fsdp"] == HEADS and mesh.shape["ctx"] == 4
    return jax.shard_map(
        local_by_head if by_head else local,
        mesh=mesh,
        in_specs=placed,
        out_specs=(
            P("fsdp", "ctx", None),
            P("fsdp", "ctx", None),
            P("fsdp"),
            P("fsdp"),
            P("fsdp"),
            P("fsdp"),
            P("fsdp", None),
            P("fsdp"),
            P("fsdp", None),
            P("fsdp"),
            P("fsdp", None),
            P("fsdp"),
            P("fsdp", None),
            P("fsdp"),
        ),
        check_vma=False,
    )
```
